32 devices in a mesh: seq: 16 (over z, y, x), tp: 2 (over core).
Axes of the slice: x: 2, y: 2, z: 4, core: 2. Of those that a mesh axis runs over, the one named last changes fastest.
Arguments:
- patches: bfloat16 [4096, 1152], P('seq'), may hold values from -6 to 6
- lengths: int32 [5], replicated, may hold values from 1 to 1792, as said below
- ln1_gain: float32 [1152], replicated, may hold values from 0.1 to 1.9
- ln1_bias: float32 [1152], replicated, may hold values from -4 to 4
- q_weight: bfloat16 [1152, 1152], P('seq', 'tp'), may hold values from -0.25 to 0.25
- q_bias: float32 [1152], P('tp'), may hold values from -4 to 4
- k_weight: bfloat16 [1152, 1152], P('seq', 'tp'), may hold values from -0.1875 to 0.1875
- v_weight: bfloat16 [1152, 1152], P('seq', 'tp'), may hold values from -0.1875 to 0.1875
- v_bias: float32 [1152], P('tp'), may hold values from -4 to 4
- o_weight: bfloat16 [1152, 1152], P('tp', 'seq'), may hold values from -3 to 3
- o_bias: float32 [1152], replicated, may hold values from -4 to 4
- ln2_gain: float32 [1152], replicated, may hold values from 0.1 to 1.9
- ln2_bias: float32 [1152], replicated, may hold values from -4 to 4
- up_weight: bfloat16 [1152, 4304], P('seq', 'tp'), may hold values from -0.1875 to 0.1875
- up_bias: float32 [4304], P('tp'), may hold values from -4 to 4
- down_weight: bfloat16 [4304, 1152], P('tp', 'seq'), may hold values from -0.09375 to 0.09375
- down_bias: float32 [1152], replicated, may hold values from -4 to 4
- gate_proj: bfloat16 [1152, 14336], P('seq', 'tp'), may hold values from -0.1875 to 0.1875
- up_proj: bfloat16 [1152, 14336], P('seq', 'tp'), may hold values from -0.1875 to 0.1875
- down_proj: bfloat16 [14336, 4096], P('tp', 'seq'), may hold values from -0.046875 to 0.046875
- ctx_gain: float32 [4096], replicated, may hold values from 0.1 to 1.9
- rk_weight: bfloat16 [4096, 384], P('seq', 'tp'), may hold values from -0.09375 to 0.09375
- rv_weight: bfloat16 [4096, 384], P('seq', 'tp'), may hold values from -0.09375 to 0.09375
- latents: float32 [64, 4096], replicated, may hold values from -6 to 6
- lat_gain: float32 [4096], replicated, may hold values from 0.1 to 1.9
- rq_weight: bfloat16 [4096, 1536], P(None, 'tp'), may hold values from -0.1875 to 0.1875
- ro_weight: bfloat16 [1536, 4096], P('tp'), may hold values from -6 to 6
- feat_grad: bfloat16 [4096, 1152], P('seq'), may hold values from -6 to 6
- lat_grad: bfloat16 [64, 4096], replicated, may hold values from -6 to 6
Outputs:
- features: bfloat16 [4096, 1152], P('seq')
- latents_out: float32 [64, 4096], replicated
- patches_grad: bfloat16 [4096, 1152], P('seq')
- latents_grad: float32 [64, 4096], replicated
- ln1_gain_grad: float32 [1152], replicated
- ln1_bias_grad: float32 [1152], replicated
- q_weight_grad: float32 [1152, 1152], P('seq', 'tp')
- q_bias_grad: float32 [1152], P('tp')
- k_weight_grad: float32 [1152, 1152], P('seq', 'tp')
- v_weight_grad: float32 [1152, 1152], P('seq', 'tp')
- v_bias_grad: float32 [1152], P('tp')
- o_weight_grad: float32 [1152, 1152], P('tp', 'seq')
- o_bias_grad: float32 [1152], replicated
- ln2_gain_grad: float32 [1152], replicated
- ln2_bias_grad: float32 [1152], replicated
- up_weight_grad: float32 [1152, 4304], P('seq', 'tp')
- up_bias_grad: float32 [4304], P('tp')
- down_weight_grad: float32 [4304, 1152], P('tp', 'seq')
- down_bias_grad: float32 [1152], replicated
- gate_proj_grad: float32 [1152, 14336], P('seq', 'tp')
- up_proj_grad: float32 [1152, 14336], P('seq', 'tp')
- down_proj_grad: float32 [14336, 4096], P('tp', 'seq')
- ctx_gain_grad: float32 [4096], replicated
- rk_weight_grad: float32 [4096, 384], P('seq', 'tp')
- rv_weight_grad: float32 [4096, 384], P('seq', 'tp')
- lat_gain_grad: float32 [4096], replicated
- rq_weight_grad: float32 [4096, 1536], P('seq', 'tp')
- ro_weight_grad: float32 [1536, 4096], P('tp', 'seq')
The draws below stay inside these ranges and needn't reach their ends.
Inputs may be any that keep to these rules, and one draw needn't show every extreme that they name: `lengths`: patches of each image; they sum to 4096; the first and the last image have exactly 1792 patches.
All inputs are finite; a program needn't handle non-finite values.
Results may differ from the reference program's by a relative error of at most 0.018.
Values may be sent and summed in bfloat16 or wider, within the bound.
A program may use at most 576 MiB of HBM per device.

```python
import jax
import jax.numpy as jnp
from jax import lax

D = 1152
HEADS = 16
HD = 72
FF = 4304
PF = 14336
RD = 4096
RH = 16
RHD = 96
RKV = 4
LAT = 64
TOKENS = 4096
MAXLEN = 1792
NIMG = 5


def draw_lengths(key, part):
    key = jax.random.fold_in(key, 11)
    middle_count = NIMG - 2
    ceiling = MAXLEN - 1
    remaining = TOKENS - 2 * MAXLEN - middle_count
    weights = jax.random.randint(key, (middle_count,), 0, ceiling + 1).astype(jnp.int32)
    weight_total = jnp.maximum(jnp.sum(weights), 1)
    extras = jnp.minimum(weights * remaining // weight_total, ceiling).astype(jnp.int32)
    leftover = remaining - jnp.sum(extras)
    room = (ceiling - extras).astype(jnp.int32)
    before = jnp.cumsum(room) - room
    added = jnp.clip(leftover - before, 0, room).astype(jnp.int32)
    middle = (1 + extras + added).astype(jnp.int32)
    edge = jnp.full((1,), MAXLEN, jnp.int32)
    return jnp.concatenate([edge, middle, edge], axis=0).astype(jnp.int32)


def block_levels(stream_key, extent, split, least, largest):
    def one(axis_at, blocks):
        heights = jax.random.uniform(jax.random.fold_in(jax.random.fold_in(stream_key, 6), axis_at), (blocks,), jnp.float32, least / len(split), largest / len(split))
        return jnp.repeat(jnp.exp(heights), extent[axis_at] // blocks).reshape((-1,) + (1,) * (len(extent) - axis_at - 1))

    level = one(*split[0])
    for cut in split[1:]:
        level = level * one(*cut)
    return level


def scatter_about(rng, extent, deviation, most, pieces=(), dtype=jnp.bfloat16):
    values = deviation * jax.random.normal(rng, extent, jnp.float32)
    if pieces:
        values = values * block_levels(rng, extent, pieces, -0.22, 0.18)
    return jnp.clip(values, -most, most).astype(dtype)


def setup_inputs(seed: int = 0) -> dict:
    keys = jax.random.split(jax.random.key(seed), 30)
    return {
        "patches": scatter_about(keys[0], (TOKENS, D), 1.0, 6.0, ((0, 16),)),
        "lengths": draw_lengths(jax.random.fold_in(keys[29], 71), 0),
        "ln1_gain": jnp.clip(1.0 + 0.18 * jax.random.normal(keys[2], (D,), jnp.float32), 0.1, 1.9),
        "ln1_bias": scatter_about(keys[3], (D,), 0.3, 4.0, (), jnp.float32),
        "q_weight": scatter_about(keys[4], (D, D), (D // 2) ** -0.5, 0.25, ((0, 16), (1, 2))),
        "q_bias": scatter_about(keys[5], (D,), 0.3, 4.0, ((0, 2),), jnp.float32),
        "k_weight": scatter_about(keys[6], (D, D), D ** -0.5, 0.1875, ((0, 16), (1, 2))),
        "v_weight": scatter_about(keys[7], (D, D), D ** -0.5, 0.1875, ((0, 16), (1, 2))),
        "v_bias": scatter_about(keys[8], (D,), 0.3, 4.0, ((0, 2),), jnp.float32),
        "o_weight": scatter_about(keys[9], (D, D), 4 ** -0.5, 3.0, ((0, 2), (1, 16))),
        "o_bias": scatter_about(keys[10], (D,), 0.3, 4.0, (), jnp.float32),
        "ln2_gain": jnp.clip(1.0 + 0.18 * jax.random.normal(keys[11], (D,), jnp.float32), 0.1, 1.9),
        "ln2_bias": scatter_about(keys[12], (D,), 0.3, 4.0, (), jnp.float32),
        "up_weight": scatter_about(keys[13], (D, FF), D ** -0.5, 0.1875, ((0, 16), (1, 2))),
        "up_bias": scatter_about(keys[14], (FF,), 0.3, 4.0, ((0, 2),), jnp.float32),
        "down_weight": scatter_about(keys[15], (FF, D), FF ** -0.5, 0.09375, ((0, 2), (1, 16))),
        "down_bias": scatter_about(keys[16], (D,), 0.3, 4.0, (), jnp.float32),
        "gate_proj": scatter_about(keys[17], (D, PF), D ** -0.5, 0.1875, ((0, 16), (1, 2))),
        "up_proj": scatter_about(keys[18], (D, PF), D ** -0.5, 0.1875, ((0, 16), (1, 2))),
        "down_proj": scatter_about(keys[19], (PF, RD), PF ** -0.5, 0.046875, ((0, 2), (1, 16))),
        "ctx_gain": jnp.clip(1.0 + 0.18 * jax.random.normal(keys[20], (RD,), jnp.float32), 0.1, 1.9),
        "rk_weight": scatter_about(keys[21], (RD, RKV * RHD), RD ** -0.5, 0.09375, ((0, 16), (1, 2))),
        "rv_weight": scatter_about(keys[22], (RD, RKV * RHD), RD ** -0.5, 0.09375, ((0, 16), (1, 2))),
        "latents": scatter_about(keys[23], (LAT, RD), 1.0, 6.0, (), jnp.float32),
        "lat_gain": jnp.clip(1.0 + 0.18 * jax.random.normal(keys[24], (RD,), jnp.float32), 0.1, 1.9),
        "rq_weight": scatter_about(keys[25], (RD, RH * RHD), (RD // 4) ** -0.5, 0.1875, ((1, 2),)),
        "ro_weight": scatter_about(keys[26], (RH * RHD, RD), 1 ** -0.5, 6.0, ((0, 2),)),
        "feat_grad": scatter_about(keys[27], (TOKENS, D), 1.0, 6.0, ((0, 16),)),
        "lat_grad": scatter_about(keys[28], (LAT, RD), 1.0, 6.0),
    }


EPS = 1e-06

@jax.custom_vjp
def low(v):
    return lax.optimization_barrier(v.astype(jnp.bfloat16)).astype(jnp.float32)

@jax.custom_vjp
def low_back(v):
    return v

def low_keep(v):
    return (low(v), None)

def low_pass(kept, grad):
    return (grad,)

def back_keep(v):
    return (v, None)

def back_low(kept, grad):
    return (low(grad),)
low.defvjp(low_keep, low_pass)
low_back.defvjp(back_keep, back_low)

def matmul(left, right):
    return jnp.dot(left, right, precision=lax.Precision.HIGHEST, preferred_element_type=jnp.float32)

def layer_norm(value, gain, bias):
    centred = value - lax.optimization_barrier(jnp.mean(value, axis=-1, keepdims=True))
    return centred * lax.rsqrt(lax.optimization_barrier(jnp.mean(centred * centred, axis=-1, keepdims=True)) + EPS) * gain + bias

def rms_norm(value, gain):
    return value * lax.rsqrt(lax.optimization_barrier(jnp.mean(value * value, axis=-1, keepdims=True)) + EPS) * gain

def image_ids(lengths, positions):
    image_ends = jnp.cumsum(lengths)
    return lax.optimization_barrier(jnp.sum((image_ends[None, :] <= positions[:, None]).astype(jnp.int32), axis=1))

def patch_attention(queries, key_rows, values, image_id):
    total_rows = queries.shape[0]
    block_rows = min(1024, total_rows)
    margin = MAXLEN - 1
    scaling = HD ** (-0.5)
    query_heads = queries.reshape(total_rows, HEADS, HD)
    padded_keys = jnp.pad(key_rows.reshape(total_rows, HEADS, HD), ((margin, margin), (0, 0), (0, 0)))
    padded_values = jnp.pad(values.reshape(total_rows, HEADS, HD), ((margin, margin), (0, 0), (0, 0)))
    padded_ids = jnp.pad(image_id, (margin, margin), constant_values=-1)

    def one_block(first_row):
        query_block = lax.dynamic_slice_in_dim(query_heads, first_row, block_rows, 0)
        key_block = lax.dynamic_slice_in_dim(padded_keys, first_row, block_rows + 2 * margin, 0)
        value_block = lax.dynamic_slice_in_dim(padded_values, first_row, block_rows + 2 * margin, 0)
        query_ids = lax.dynamic_slice_in_dim(image_id, first_row, block_rows, 0)
        key_ids = lax.dynamic_slice_in_dim(padded_ids, first_row, block_rows + 2 * margin, 0)
        scores = low_back(jnp.einsum('qhd,khd->hqk', query_block, key_block, precision=lax.Precision.HIGHEST) * scaling)
        same_image = query_ids[:, None] == key_ids[None, :]
        masked = jnp.where(same_image[None], scores, -1e+30)
        peak = lax.optimization_barrier(jnp.max(masked, axis=-1, keepdims=True))
        exponent = jnp.exp(masked - peak)
        probability = low(exponent / lax.optimization_barrier(jnp.sum(exponent, axis=-1, keepdims=True)))
        result = jnp.einsum('hqk,khd->qhd', probability, value_block, precision=lax.Precision.HIGHEST)
        return result.reshape(block_rows, D)
    starts = (jnp.arange(total_rows // block_rows) * block_rows).astype(jnp.int32)
    return lax.map(jax.checkpoint(one_block), starts).reshape(total_rows, D)

def latent_attention(lat_queries, all_keys, all_values):
    group = RH // RKV
    query_heads = lat_queries.reshape(LAT, RKV, group, RHD)
    key_heads = all_keys.reshape(-1, RKV, RHD)
    value_heads = all_values.reshape(-1, RKV, RHD)
    scores = low_back(jnp.einsum('lkgd,tkd->kglt', query_heads, key_heads, precision=lax.Precision.HIGHEST) * RHD ** (-0.5))
    peak = lax.optimization_barrier(jnp.max(scores, axis=-1, keepdims=True))
    exponent = jnp.exp(scores - peak)
    probability = exponent / lax.optimization_barrier(jnp.sum(exponent, axis=-1, keepdims=True))
    result = jnp.einsum('kglt,tkd->lkgd', probability, value_heads, precision=lax.Precision.HIGHEST)
    return result.reshape(LAT, RH * RHD)

def forward(patches, ln1_gain, ln1_bias, q_weight, q_bias, k_weight, v_weight, v_bias, o_weight, o_bias, ln2_gain, ln2_bias, up_weight, up_bias, down_weight, down_bias, gate_proj, up_proj, down_proj, ctx_gain, rk_weight, rv_weight, latents, lat_gain, rq_weight, ro_weight, image_id):
    normed_in = low(layer_norm(patches, ln1_gain, ln1_bias))
    queries = low_back(low(matmul(normed_in, q_weight) + q_bias))
    key_rows = low_back(low(matmul(normed_in, k_weight)))
    values = low_back(low(matmul(normed_in, v_weight) + v_bias))
    attended = low_back(low(patch_attention(queries, key_rows, values, image_id)))
    after_attn = patches + low_back(matmul(attended, o_weight) + o_bias)
    mlp_in = low(layer_norm(after_attn, ln2_gain, ln2_bias))
    hidden = low_back(matmul(mlp_in, up_weight) + up_bias)
    active = low(jax.nn.gelu(hidden, approximate=True))
    after_mlp = after_attn + low_back(matmul(active, down_weight) + down_bias)
    proj_input = low(after_mlp)
    proj_gate = low_back(matmul(proj_input, gate_proj))
    proj_up = low_back(matmul(proj_input, up_proj))
    proj_hidden = low(jax.nn.silu(proj_gate) * proj_up)
    proj_out = low_back(matmul(proj_hidden, down_proj))
    context = low(rms_norm(proj_out, ctx_gain))
    ctx_keys = low_back(low(matmul(context, rk_weight)))
    ctx_values = low_back(low(matmul(context, rv_weight)))
    lat_normed = low(rms_norm(latents, lat_gain))
    lat_queries = low_back(low(matmul(lat_normed, rq_weight)))
    lat_keys = low_back(low(matmul(lat_normed, rk_weight)))
    lat_values = low_back(low(matmul(lat_normed, rv_weight)))
    all_keys = jnp.concatenate([ctx_keys, lat_keys], axis=0)
    all_values = jnp.concatenate([ctx_values, lat_values], axis=0)
    pooled = low_back(low(latent_attention(lat_queries, all_keys, all_values)))
    latents_out = latents + low_back(matmul(pooled, ro_weight))
    return (after_mlp, latents_out)

def reference(patches, lengths, ln1_gain, ln1_bias, q_weight, q_bias, k_weight, v_weight, v_bias, o_weight, o_bias, ln2_gain, ln2_bias, up_weight, up_bias, down_weight, down_bias, gate_proj, up_proj, down_proj, ctx_gain, rk_weight, rv_weight, latents, lat_gain, rq_weight, ro_weight, feat_grad, lat_grad):
    positions = jnp.arange(TOKENS).astype(jnp.int32)
    image_id = image_ids(lengths, positions)
    inputs = (patches.astype(jnp.float32), ln1_gain, ln1_bias, q_weight.astype(jnp.float32), q_bias, k_weight.astype(jnp.float32), v_weight.astype(jnp.float32), v_bias, o_weight.astype(jnp.float32), o_bias, ln2_gain, ln2_bias, up_weight.astype(jnp.float32), up_bias, down_weight.astype(jnp.float32), down_bias, gate_proj.astype(jnp.float32), up_proj.astype(jnp.float32), down_proj.astype(jnp.float32), ctx_gain, rk_weight.astype(jnp.float32), rv_weight.astype(jnp.float32), latents, lat_gain, rq_weight.astype(jnp.float32), ro_weight.astype(jnp.float32))

    def applied(*operands):
        return forward(*operands, image_id)
    outputs, pullback = jax.vjp(applied, *inputs)
    gradient = pullback((feat_grad.astype(jnp.float32), lat_grad.astype(jnp.float32)))
    return (outputs[0].astype(jnp.bfloat16), outputs[1], gradient[0].astype(jnp.bfloat16), gradient[22], gradient[1], gradient[2], gradient[3], gradient[4], gradient[5], gradient[6], gradient[7], gradient[8], gradient[9], gradient[10], gradient[11], gradient[12], gradient[13], gradient[14], gradient[15], gradient[16], gradient[17], gradient[18], gradient[19], gradient[20], gradient[21], gradient[23], gradient[24], gradient[25])
```

```python
import functools

import jax
import jax.experimental.pallas as pl
import jax.experimental.pallas.tpu as pltpu
import jax.numpy as jnp
from jax import lax
from jax.sharding import PartitionSpec as P

HD = 72
RHD = 96
IMGMAX = 4900


EPS = 1e-06


def passed_along(value, axis, steps):
    count = lax.axis_size(axis)
    first, last = (max(0, -steps), min(count, count - steps))
    return lax.ppermute(value, axis, [(source, source + steps) for source in range(first, last)])


def joined(part, axis, combine):
    gathered = jax.tree.map(lambda a: lax.all_gather(a, axis), part)

    def take(source):
        return jax.tree.map(lambda a: lax.dynamic_index_in_dim(a, source, 0, False), gathered)

    return lax.fori_loop(
        1, lax.axis_size(axis), lambda source, state: combine(state, take(source)), take(0)
    )


def layer_norm(value, gain, bias):
    centred = value - jnp.mean(value, axis=-1, keepdims=True)
    return (
        centred * lax.rsqrt(jnp.mean(centred * centred, axis=-1, keepdims=True) + EPS) * gain + bias
    )


def rms_norm(value, gain):
    return value * lax.rsqrt(jnp.mean(value * value, axis=-1, keepdims=True) + EPS) * gain


def gelu_tanh(value):
    return jax.nn.gelu(value, approximate=True)


def product(left, right):
    return jnp.dot(left, right, preferred_element_type=jnp.float32)


def product_nt(left, right):
    return lax.dot_general(
        left, right, (((1,), (1,)), ((), ())), preferred_element_type=jnp.float32
    )


def product_tn(left, right):
    return lax.dot_general(
        left, right, (((0,), (0,)), ((), ())), preferred_element_type=jnp.float32
    )


def image_ids(lengths, positions, total_rows):
    image_ends = jnp.cumsum(lengths)
    counted = jnp.sum((image_ends[None, :] <= positions[:, None]).astype(jnp.int32), axis=1)
    inside = (positions >= 0) & (positions < total_rows)
    return jnp.where(inside, counted, -1)


def split_heads(matrix, count):
    return matrix.reshape(matrix.shape[0], count, -1).transpose(1, 0, 2)


def join_heads(stacked):
    return stacked.transpose(1, 0, 2).reshape(stacked.shape[1], -1)


def neighbour(first, second, offset):
    return passed_along((first, second), "seq", offset)


def returned(first, second, offset):
    return (
        passed_along(first.astype(jnp.bfloat16), "seq", offset).astype(first.dtype),
        passed_along(second.astype(jnp.bfloat16), "seq", offset).astype(second.dtype),
    )


def partial_stats(scores, value_heads):
    peak = jnp.max(scores, axis=-1)
    weights = jnp.exp(scores - peak[..., None])
    total = jnp.sum(weights, axis=-1)
    numer = jnp.einsum(
        "kglt,tkd->kgld", weights, value_heads.astype(jnp.float32), precision=lax.Precision.HIGHEST
    )
    return (peak, total, numer)


def joint_stats(left, right):
    peak = jnp.maximum(left[0], right[0])
    left_scale = jnp.exp(left[0] - peak)
    right_scale = jnp.exp(right[0] - peak)
    total = left[1] * left_scale + right[1] * right_scale
    numer = left[2] * left_scale[..., None] + right[2] * right_scale[..., None]
    return (peak, total, numer)


def weights_travel(
    patches,
    lengths,
    ln1_gain,
    ln1_bias,
    q_weight,
    q_bias,
    k_weight,
    v_weight,
    v_bias,
    o_weight,
    o_bias,
    ln2_gain,
    ln2_bias,
    up_weight,
    up_bias,
    down_weight,
    down_bias,
    gate_proj,
    up_proj,
    down_proj,
    ctx_gain,
    rk_weight,
    rv_weight,
    latents,
    lat_gain,
    rq_weight,
    ro_weight,
    feat_grad,
    lat_grad,
):
    tok_rows = patches.shape[0]
    seq_count = lax.axis_size("seq")
    seq_place = lax.axis_index("seq")
    total_rows = tok_rows * seq_count
    longest = min(IMGMAX, (seq_count // 2 - 1) * tok_rows)
    reach_blocks = (longest + tok_rows - 2) // tok_rows
    local_heads = q_bias.shape[0] // HD
    kv_heads = rk_weight.shape[1] // RHD
    q_heads = rq_weight.shape[1] // RHD
    group = q_heads // kv_heads
    lat_rows = latents.shape[0]
    scaling = HD ** (-0.5)
    lat_scaling = RHD ** (-0.5)
    first_block = (seq_place == 0).astype(jnp.float32)
    gathered = (
        lax.all_gather(q_weight, "seq", axis=0, tiled=True),
        lax.all_gather(k_weight, "seq", axis=0, tiled=True),
        lax.all_gather(v_weight, "seq", axis=0, tiled=True),
        lax.all_gather(o_weight, "seq", axis=1, tiled=True),
        lax.all_gather(up_weight, "seq", axis=0, tiled=True),
        lax.all_gather(down_weight, "seq", axis=1, tiled=True),
        lax.all_gather(gate_proj, "seq", axis=0, tiled=True),
        lax.all_gather(up_proj, "seq", axis=0, tiled=True),
        lax.all_gather(down_proj, "seq", axis=1, tiled=True),
        lax.all_gather(rk_weight, "seq", axis=0, tiled=True),
        lax.all_gather(rv_weight, "seq", axis=0, tiled=True),
    )
    (
        w_query,
        w_key,
        w_value,
        w_out,
        w_up,
        w_down,
        w_gate_proj,
        w_up_proj,
        w_down_proj,
        w_ctxkey,
        w_ctxval,
    ) = gathered
    input_f32 = patches.astype(jnp.float32)
    normed_in = layer_norm(input_f32, ln1_gain, ln1_bias).astype(jnp.bfloat16)
    queries_low = (product(normed_in, w_query) + q_bias).astype(jnp.bfloat16)
    keys_low = product(normed_in, w_key).astype(jnp.bfloat16)
    values_low = (product(normed_in, w_value) + v_bias).astype(jnp.bfloat16)
    upper_pairs = []
    lower_pairs = []
    upper_pair = (keys_low, values_low)
    lower_pair = (keys_low, values_low)
    for distance in range(1, reach_blocks + 1):
        upper_pair = neighbour(upper_pair[0], upper_pair[1], -1)
        lower_pair = neighbour(lower_pair[0], lower_pair[1], 1)
        upper_pairs.append(upper_pair)
        lower_pairs.append(lower_pair)
    ordered = lower_pairs[::-1] + [(keys_low, values_low)] + upper_pairs
    key_buffer = jnp.concatenate([pair[0] for pair in ordered], axis=0)
    value_buffer = jnp.concatenate([pair[1] for pair in ordered], axis=0)
    own_positions = seq_place * tok_rows + jnp.arange(tok_rows, dtype=jnp.int32)
    query_ids = image_ids(lengths, own_positions, total_rows)
    key_positions = (seq_place - reach_blocks) * tok_rows + jnp.arange(
        (2 * reach_blocks + 1) * tok_rows, dtype=jnp.int32
    )
    key_ids = image_ids(lengths, key_positions, total_rows)
    allowed = query_ids[:, None] == key_ids[None, :]
    query_heads = split_heads(queries_low, local_heads)
    key_heads = split_heads(key_buffer, local_heads)
    value_heads = split_heads(value_buffer, local_heads)

    def head_forward(operands):
        query_one, key_one, value_one = operands
        scores = jnp.where(allowed, product_nt(query_one, key_one) * scaling, -1e30)
        peak = jnp.max(scores, axis=1, keepdims=True)
        exponent = jnp.exp(scores - peak)
        total_exp = jnp.sum(exponent, axis=1, keepdims=True)
        probability = exponent / total_exp
        result = product(probability.astype(jnp.bfloat16), value_one)
        return (result, peak[:, 0] + jnp.log(total_exp[:, 0]))

    head_result, head_lse = lax.map(head_forward, (query_heads, key_heads, value_heads))
    attended_low = join_heads(head_result).astype(jnp.bfloat16)
    attn_sum = lax.psum(product(attended_low, w_out), "tp")
    after_attn = input_f32 + attn_sum + o_bias
    mlp_in = layer_norm(after_attn, ln2_gain, ln2_bias).astype(jnp.bfloat16)
    hidden = product(mlp_in, w_up) + up_bias
    active_low = gelu_tanh(hidden).astype(jnp.bfloat16)
    mlp_sum = lax.psum(product(active_low, w_down).astype(jnp.bfloat16), "tp").astype(jnp.float32)
    after_mlp = after_attn + mlp_sum + down_bias
    features = after_mlp.astype(jnp.bfloat16)
    proj_gate = product(features, w_gate_proj)
    proj_up = product(features, w_up_proj)
    silu_gate = jax.nn.silu(proj_gate)
    proj_hidden = (silu_gate * proj_up).astype(jnp.bfloat16)
    proj_out = lax.psum(product(proj_hidden, w_down_proj).astype(jnp.bfloat16), "tp").astype(
        jnp.float32
    )
    context_low = rms_norm(proj_out, ctx_gain).astype(jnp.bfloat16)
    ctx_keys = product(context_low, w_ctxkey).astype(jnp.bfloat16)
    ctx_values = product(context_low, w_ctxval).astype(jnp.bfloat16)
    lat_normed = rms_norm(latents, lat_gain).astype(jnp.bfloat16)
    lat_queries = product(lat_normed, rq_weight).astype(jnp.bfloat16)
    lat_keys = product(lat_normed, w_ctxkey).astype(jnp.bfloat16)
    lat_values = product(lat_normed, w_ctxval).astype(jnp.bfloat16)
    query_grouped = lat_queries.reshape(lat_rows, kv_heads, group, RHD)
    key_grouped = ctx_keys.reshape(tok_rows, kv_heads, RHD)
    value_grouped = ctx_values.reshape(tok_rows, kv_heads, RHD)
    self_keys = lat_keys.reshape(lat_rows, kv_heads, RHD)
    self_values = lat_values.reshape(lat_rows, kv_heads, RHD)
    lat_scores = (
        jnp.einsum("lkgd,tkd->kglt", query_grouped, key_grouped, preferred_element_type=jnp.float32)
        * lat_scaling
    )
    self_scores = (
        jnp.einsum("lkgd,tkd->kglt", query_grouped, self_keys, preferred_element_type=jnp.float32)
        * lat_scaling
    )
    merged = joined(partial_stats(lat_scores, value_grouped), "seq", joint_stats)
    lat_peak, lat_total, lat_numer = joint_stats(merged, partial_stats(self_scores, self_values))
    lat_lse = lat_peak + jnp.log(lat_total)
    pooled_exact = lat_numer / lat_total[..., None]
    pooled_low = pooled_exact.transpose(2, 0, 1, 3).reshape(lat_rows, -1).astype(jnp.bfloat16)
    lat_mix = product(pooled_low, ro_weight)
    ro_width = ro_weight.shape[1] // seq_count
    ro_columns = lax.dynamic_slice_in_dim(lat_grad, seq_place * ro_width, ro_width, 1)
    ro_weight_grad = product_tn(pooled_low, ro_columns)
    pooled_grad = product_nt(lat_grad, ro_weight).astype(jnp.bfloat16)
    pooled_grouped = pooled_grad.reshape(lat_rows, kv_heads, group, RHD)
    pooled_f32 = pooled_grouped.astype(jnp.float32)
    lat_delta = jnp.sum(pooled_f32.transpose(1, 2, 0, 3) * pooled_exact, axis=-1)

    def score_grads(scores, key_part, value_part):
        probability = jnp.exp(scores - lat_lse[..., None])
        dprob = jnp.einsum(
            "lkgd,tkd->kglt", pooled_grouped, value_part, preferred_element_type=jnp.float32
        )
        dscore = (probability * (dprob - lat_delta[..., None])).astype(jnp.bfloat16)
        query_term = (
            jnp.einsum("kglt,tkd->lkgd", dscore, key_part, preferred_element_type=jnp.float32)
            * lat_scaling
        )
        key_term = (
            jnp.einsum("kglt,lkgd->tkd", dscore, query_grouped, preferred_element_type=jnp.float32)
            * lat_scaling
        ).astype(jnp.bfloat16)
        value_term = jnp.einsum(
            "kglt,lkgd->tkd", probability, pooled_f32, precision=lax.Precision.HIGHEST
        ).astype(jnp.bfloat16)
        return (
            query_term,
            key_term.reshape(key_part.shape[0], -1),
            value_term.reshape(key_part.shape[0], -1),
        )

    ctx_query_term, ctx_keys_grad, ctx_values_grad = score_grads(
        lat_scores, key_grouped, value_grouped
    )
    self_query_term, self_keys_grad, self_values_grad = score_grads(
        self_scores, self_keys, self_values
    )
    query_part = ctx_query_term + first_block * self_query_term
    query_sum = lax.psum(query_part, "seq")
    lat_queries_grad = query_sum.reshape(lat_rows, -1).astype(jnp.bfloat16)
    rq_rows = rq_weight.shape[0] // seq_count
    rq_weight_grad = product_tn(
        lax.dynamic_slice_in_dim(lat_normed, seq_place * rq_rows, rq_rows, 1), lat_queries_grad
    )
    rk_part = product_tn(context_low, ctx_keys_grad) + first_block * product_tn(
        lat_normed, self_keys_grad
    )
    rv_part = product_tn(context_low, ctx_values_grad) + first_block * product_tn(
        lat_normed, self_values_grad
    )
    ctx_part = product_nt(ctx_keys_grad, w_ctxkey) + product_nt(ctx_values_grad, w_ctxval)
    lat_part = (
        product_nt(lat_queries_grad, rq_weight)
        + product_nt(self_keys_grad, w_ctxkey)
        + product_nt(self_values_grad, w_ctxval)
    )
    ctx_back, lat_back, lat_mix_sum = (
        lax.psum(ctx_part.astype(jnp.bfloat16), "tp").astype(jnp.float32),
        lax.psum(lat_part.astype(jnp.bfloat16), "tp").astype(jnp.float32),
        lax.psum(lat_mix.astype(jnp.bfloat16), "tp").astype(jnp.float32),
    )
    latents_out = latents + lat_mix_sum
    lat_pull = jax.vjp(rms_norm, latents, lat_gain)[1]
    lat_in_grad, lat_gain_grad = lat_pull(lat_back)
    latents_grad = lat_grad.astype(jnp.float32) + lat_in_grad
    ctx_pull = jax.vjp(rms_norm, proj_out, ctx_gain)[1]
    proj_out_grad, ctx_gain_part = ctx_pull(ctx_back)
    proj_out_low = proj_out_grad.astype(jnp.bfloat16)
    down_proj_part = product_tn(proj_hidden, proj_out_low)
    hidden_pgrad = product_nt(proj_out_low, w_down_proj)
    silu_pull = jax.vjp(jax.nn.silu, proj_gate)[1]
    gate_grad_low = silu_pull(hidden_pgrad * proj_up)[0].astype(jnp.bfloat16)
    up_grad_low = (hidden_pgrad * silu_gate).astype(jnp.bfloat16)
    gate_proj_part = product_tn(features, gate_grad_low)
    up_proj_part = product_tn(features, up_grad_low)
    proj_in_grad = lax.psum(
        (product_nt(gate_grad_low, w_gate_proj) + product_nt(up_grad_low, w_up_proj)).astype(
            jnp.bfloat16
        ),
        "tp",
    ).astype(jnp.float32)
    mlp_out_grad = feat_grad.astype(jnp.float32) + proj_in_grad
    mlp_out_low = mlp_out_grad.astype(jnp.bfloat16)
    down_part = product_tn(active_low, mlp_out_low)
    down_bias_part = jnp.sum(mlp_out_low.astype(jnp.float32), axis=0)
    active_grad = product_nt(mlp_out_low, w_down)
    gelu_pull = jax.vjp(gelu_tanh, hidden)[1]
    hidden_grad = gelu_pull(active_grad)[0].astype(jnp.bfloat16)
    up_part = product_tn(mlp_in, hidden_grad)
    up_bias_part = jnp.sum(hidden_grad.astype(jnp.float32), axis=0)
    mlp_back = lax.psum(product_nt(hidden_grad, w_up).astype(jnp.bfloat16), "tp").astype(
        jnp.float32
    )
    ln2_pull = jax.vjp(layer_norm, after_attn, ln2_gain, ln2_bias)[1]
    norm_grad, ln2_gain_part, ln2_bias_part = ln2_pull(mlp_back)
    attn_out_grad = mlp_out_grad + norm_grad
    attn_out_low = attn_out_grad.astype(jnp.bfloat16)
    o_part = product_tn(attended_low, attn_out_low)
    o_bias_part = jnp.sum(attn_out_low.astype(jnp.float32), axis=0)
    attended_grad = product_nt(attn_out_low, w_out).astype(jnp.bfloat16)
    grad_heads = split_heads(attended_grad, local_heads)

    def head_backward(operands):
        query_one, key_one, value_one, grad_one, lse_one = operands
        scores = jnp.where(allowed, product_nt(query_one, key_one) * scaling, -1e30)
        probability = jnp.exp(scores - lse_one[:, None])
        dprob = product_nt(grad_one, value_one)
        row_inner = jnp.sum(probability * dprob, axis=1, keepdims=True)
        score_low = (probability * (dprob - row_inner)).astype(jnp.bfloat16)
        query_one_grad = product(score_low, key_one) * scaling
        key_one_grad = product_tn(score_low, query_one) * scaling
        value_one_grad = product_tn(probability.astype(jnp.bfloat16), grad_one)
        return (query_one_grad, key_one_grad, value_one_grad)

    query_hgrad, key_hgrad, value_hgrad = lax.map(
        head_backward, (query_heads, key_heads, value_heads, grad_heads, head_lse)
    )
    key_blocks = join_heads(key_hgrad).reshape(2 * reach_blocks + 1, tok_rows, -1)
    value_blocks = join_heads(value_hgrad).reshape(2 * reach_blocks + 1, tok_rows, -1)
    key_total = key_blocks[reach_blocks]
    value_total = value_blocks[reach_blocks]
    carry_upper = (key_blocks[2 * reach_blocks], value_blocks[2 * reach_blocks])
    carry_lower = (key_blocks[0], value_blocks[0])
    for distance in range(reach_blocks - 1, 0, -1):
        moved_upper = returned(carry_upper[0], carry_upper[1], 1)
        carry_upper = (
            moved_upper[0] + key_blocks[reach_blocks + distance],
            moved_upper[1] + value_blocks[reach_blocks + distance],
        )
        moved_lower = returned(carry_lower[0], carry_lower[1], -1)
        carry_lower = (
            moved_lower[0] + key_blocks[reach_blocks - distance],
            moved_lower[1] + value_blocks[reach_blocks - distance],
        )
    moved_upper = returned(carry_upper[0], carry_upper[1], 1)
    moved_lower = returned(carry_lower[0], carry_lower[1], -1)
    key_total = key_total + moved_upper[0] + moved_lower[0]
    value_total = value_total + moved_upper[1] + moved_lower[1]
    queries_grad = join_heads(query_hgrad).astype(jnp.bfloat16)
    keys_grad = key_total.astype(jnp.bfloat16)
    values_grad = value_total.astype(jnp.bfloat16)
    q_part = product_tn(normed_in, queries_grad)
    k_part = product_tn(normed_in, keys_grad)
    v_part = product_tn(normed_in, values_grad)
    q_bias_part = jnp.sum(queries_grad.astype(jnp.float32), axis=0)
    v_bias_part = jnp.sum(values_grad.astype(jnp.float32), axis=0)
    attn_back = lax.psum(
        (
            product_nt(queries_grad, w_query)
            + product_nt(keys_grad, w_key)
            + product_nt(values_grad, w_value)
        ).astype(jnp.bfloat16),
        "tp",
    ).astype(jnp.float32)
    ln1_pull = jax.vjp(layer_norm, input_f32, ln1_gain, ln1_bias)[1]
    in_grad, ln1_gain_part, ln1_bias_part = ln1_pull(attn_back)
    patches_grad = (attn_out_grad + in_grad).astype(jnp.bfloat16)
    weight_sums = (
        lax.psum_scatter(q_part, "seq", scatter_dimension=0, tiled=True),
        lax.psum_scatter(k_part, "seq", scatter_dimension=0, tiled=True),
        lax.psum_scatter(v_part, "seq", scatter_dimension=0, tiled=True),
        lax.psum_scatter(o_part, "seq", scatter_dimension=1, tiled=True),
        lax.psum_scatter(up_part, "seq", scatter_dimension=0, tiled=True),
        lax.psum_scatter(down_part, "seq", scatter_dimension=1, tiled=True),
        lax.psum_scatter(gate_proj_part, "seq", scatter_dimension=0, tiled=True),
        lax.psum_scatter(up_proj_part, "seq", scatter_dimension=0, tiled=True),
        lax.psum_scatter(down_proj_part, "seq", scatter_dimension=1, tiled=True),
        lax.psum_scatter(rk_part, "seq", scatter_dimension=0, tiled=True),
        lax.psum_scatter(rv_part, "seq", scatter_dimension=0, tiled=True),
    )
    small_sums = lax.psum(
        (
            ln1_gain_part,
            ln1_bias_part,
            q_bias_part,
            v_bias_part,
            o_bias_part,
            ln2_gain_part,
            ln2_bias_part,
            up_bias_part,
            down_bias_part,
            ctx_gain_part,
        ),
        "seq",
    )
    return (
        features,
        latents_out,
        patches_grad,
        latents_grad,
        small_sums[0],
        small_sums[1],
        weight_sums[0],
        small_sums[2],
        weight_sums[1],
        weight_sums[2],
        small_sums[3],
        weight_sums[3],
        small_sums[4],
        small_sums[5],
        small_sums[6],
        weight_sums[4],
        small_sums[7],
        weight_sums[5],
        small_sums[8],
        weight_sums[6],
        weight_sums[7],
        weight_sums[8],
        small_sums[9],
        weight_sums[9],
        weight_sums[10],
        lat_gain_grad,
        rq_weight_grad,
        ro_weight_grad,
    )


MESH = pl.DeviceIdType.MESH


def greet(partners):
    barrier = pltpu.get_barrier_semaphore()
    for present, device in partners:

        @pl.when(present)
        def _():
            pl.semaphore_signal(
                barrier, inc=1, device_id={"seq": device}, device_id_type=MESH
            )

    pl.semaphore_wait(barrier, sum(jnp.where(present, 1, 0) for present, _ in partners))


def place():
    me = lax.axis_index("seq")
    x, y, z = lax.rem(me, 2), lax.rem(lax.div(me, 2), 2), lax.div(me, 4)
    first = lax.axis_index("tp") == 0
    a, b = jnp.where(first, x, y), jnp.where(first, y, x)
    step_a, step_b = jnp.where(first, 1, 2), jnp.where(first, 2, 1)
    return me, z, a, b, step_a, step_b


def neighbours(layers):
    me, z, a, b, step_a, step_b = place()
    up, down = z < layers - 1, z > 0
    return (
        (up, jnp.where(up, me + 4, me)),
        (down, jnp.where(down, me - 4, me)),
        (me >= 0, me + step_a * (1 - 2 * a)),
        (me >= 0, me + step_b * (1 - 2 * b)),
    )


def gather_kernel(n, x_ref, o_ref, sent, landed, local):
    layers = n // 4
    me, z, a, b, step_a, step_b = place()
    partners = neighbours(layers)
    (up, to_up), (down, to_down), (_, to_a), (_, to_b) = partners
    greet(partners)
    own = pltpu.make_async_copy(x_ref, o_ref.at[me], local)
    own.start()

    def send(slot, device, way, source=None):
        return pltpu.make_async_remote_copy(
            src_ref=o_ref.at[slot] if source is None else source,
            dst_ref=o_ref.at[slot],
            send_sem=sent.at[way, slot],
            recv_sem=landed.at[slot],
            device_id={"seq": device},
            device_id_type=MESH,
        )

    @pl.when(up)
    def _():
        send(me, to_up, 0, x_ref).start()

    @pl.when(down)
    def _():
        send(me, to_down, 1, x_ref).start()

    send(me, to_b, 3, x_ref).start()
    send(me, to_a, 2, x_ref).start()
    for distance in range(1, layers):

        @pl.when(z >= distance)
        def _():
            slot = me - 4 * distance
            send(slot, to_a, 2).wait_recv()

            @pl.when(up)
            def _():
                send(slot, to_up, 0).start()

            send(slot, to_b, 3).start()
            send(slot, to_a, 2).start()

        @pl.when(z + distance < layers)
        def _():
            slot = me + 4 * distance
            send(slot, to_a, 2).wait_recv()

            @pl.when(down)
            def _():
                send(slot, to_down, 1).start()

            send(slot, to_b, 3).start()
            send(slot, to_a, 2).start()

    for distance in range(layers):

        @pl.when(z >= distance)
        def _():
            slot = to_a - 4 * distance
            send(slot, to_b, 3).wait_recv()
            send(slot, to_b, 3).start()

        if distance:

            @pl.when(z + distance < layers)
            def _():
                slot = to_a + 4 * distance
                send(slot, to_b, 3).wait_recv()
                send(slot, to_b, 3).start()

    def at(layer, of_a, of_b):
        return layer * 4 + of_a * step_a + of_b * step_b

    def arrive(layer, _):
        send(at(layer, 0, 1 - b), to_b, 3).wait_recv()
        send(at(layer, 1, 1 - b), to_b, 3).wait_recv()
        return 0

    lax.fori_loop(0, layers, arrive, 0)
    own.wait()

    def drain(layer, _):
        slot = at(layer, a, b)
        send(slot, to_a, 2).wait_send()
        send(slot, to_b, 3).wait_send()
        send(at(layer, 1 - a, b), to_b, 3).wait_send()

        @pl.when((layer <= z) & up)
        def _():
            send(slot, to_up, 0).wait_send()

        @pl.when((layer >= z) & down)
        def _():
            send(slot, to_down, 1).wait_send()

        return 0

    lax.fori_loop(0, layers, drain, 0)


def gathered_blocks(x, collective_id):
    n = lax.axis_size("seq")
    return pl.pallas_call(
        functools.partial(gather_kernel, n),
        out_shape=jax.ShapeDtypeStruct((n,) + x.shape, x.dtype),
        in_specs=[pl.BlockSpec(memory_space=pl.ANY)],
        out_specs=pl.BlockSpec(memory_space=pl.ANY),
        scratch_shapes=[
            pltpu.SemaphoreType.DMA((4, n)),
            pltpu.SemaphoreType.DMA((n,)),
            pltpu.SemaphoreType.DMA(()),
        ],
        compiler_params=pltpu.CompilerParams(
            collective_id=collective_id, has_side_effects=True
        ),
    )(x)


def scatter_kernel(n, chunks, p_ref, o_ref, from_b, from_a, from_down, from_up, *semaphores):
    layers = n // 4
    me, z, a, b, step_a, step_b = place()
    partners = neighbours(layers)
    (up, to_up), (down, to_down), (_, to_a), (_, to_b) = partners
    b_sent, b_landed, a_sent, a_landed, u_sent, u_landed, d_sent, d_landed = semaphores
    greet(partners)

    def at(layer, of_a, of_b):
        return layer * 4 + of_a * step_a + of_b * step_b

    def copy(source, target, sent, landed, device):
        return pltpu.make_async_remote_copy(
            src_ref=source,
            dst_ref=target,
            send_sem=sent,
            recv_sem=landed,
            device_id={"seq": device},
            device_id_type=MESH,
        )

    def over_b(c, of_a, layer):
        return copy(
            p_ref.at[c, at(layer, of_a, 1 - b)],
            from_b.at[c, of_a, layer],
            b_sent.at[c, of_a, layer],
            b_landed.at[c, of_a, layer],
            to_b,
        )

    def over_a(c, layer):
        return copy(
            p_ref.at[c, at(layer, 1 - a, b)],
            from_a.at[c, layer],
            a_sent.at[c, layer],
            a_landed.at[c, layer],
            to_a,
        )

    def upward(c, layer):
        return copy(
            p_ref.at[c, at(layer, a, b)],
            from_down.at[c, layer],
            u_sent.at[c, layer],
            u_landed.at[c, layer],
            to_up,
        )

    def downward(c, layer):
        return copy(
            p_ref.at[c, at(layer, a, b)],
            from_up.at[c, layer],
            d_sent.at[c, layer],
            d_landed.at[c, layer],
            to_down,
        )

    def each_layer(body):
        lax.fori_loop(0, layers, lambda layer, _: (body(layer), 0)[1], 0)

    def send_b(c):
        each_layer(lambda layer: over_b(c, 1 - a, layer).start())
        each_layer(lambda layer: over_b(c, a, layer).start())

    def send_a(c):
        def body(layer):
            over_b(c, 1 - a, layer).wait_recv()
            slot = at(layer, 1 - a, b)
            p_ref[c, slot] = p_ref[c, slot] + from_b[c, 1 - a, layer]
            over_a(c, layer).start()

        each_layer(body)

    def join_line(c):
        def body(layer):
            over_b(c, a, layer).wait_recv()
            over_a(c, layer).wait_recv()
            slot = at(layer, a, b)
            p_ref[c, slot] = p_ref[c, slot] + from_b[c, a, layer] + from_a[c, layer]

            @pl.when((layer > z) & (z == 0))
            def _():
                upward(c, layer).start()

            @pl.when((layer < z) & (z == layers - 1))
            def _():
                downward(c, layer).start()

        each_layer(body)

    def pass_up(c):
        def body(layer):
            @pl.when(layer > z)
            def _():
                upward(c, layer).wait_recv()
                slot = at(layer, a, b)
                p_ref[c, slot] = p_ref[c, slot] + from_down[c, layer]
                upward(c, layer).start()

        each_layer(body)

    def pass_down(c):
        def body(layer):
            @pl.when(layer < z)
            def _():
                downward(c, layer).wait_recv()
                slot = at(layer, a, b)
                p_ref[c, slot] = p_ref[c, slot] + from_up[c, layer]
                downward(c, layer).start()

        each_layer(body)

    def finish(c):
        @pl.when(down)
        def _():
            upward(c, z).wait_recv()
            p_ref[c, me] = p_ref[c, me] + from_down[c, z]

        @pl.when(up)
        def _():
            downward(c, z).wait_recv()
            p_ref[c, me] = p_ref[c, me] + from_up[c, z]

        o_ref[c] = p_ref[c, me]

    def when_chunk(step, stage):
        @pl.when((step >= 0) & (step < chunks))
        def _():
            stage(jnp.clip(step, 0, chunks - 1))

    send_b(0)

    def step(t, _):
        when_chunk(t + 1, send_b)
        when_chunk(t, send_a)
        when_chunk(t - 1, join_line)
        inner = (z > 0) & (z < layers - 1)

        @pl.when(inner)
        def _():
            when_chunk(t - 1 - z, pass_up)
            when_chunk(t - layers + z, pass_down)

        when_chunk(t - layers, finish)
        return 0

    lax.fori_loop(0, chunks + layers, step, 0)

    def drain(c, _):
        def body(layer):
            over_b(c, 0, layer).wait_send()
            over_b(c, 1, layer).wait_send()
            over_a(c, layer).wait_send()

            @pl.when(layer > z)
            def _():
                upward(c, layer).wait_send()

            @pl.when(layer < z)
            def _():
                downward(c, layer).wait_send()

        each_layer(body)
        return 0

    lax.fori_loop(0, chunks, drain, 0)


def scattered_sum(terms, collective_id):
    chunks, n = terms.shape[:2]
    layers, block = n // 4, terms.shape[2:]

    def slots(*count):
        return pltpu.VMEM((chunks,) + count + block, terms.dtype)

    def semaphores(*count):
        return pltpu.SemaphoreType.DMA((chunks,) + count)

    return pl.pallas_call(
        functools.partial(scatter_kernel, n, chunks),
        out_shape=jax.ShapeDtypeStruct((chunks,) + block, terms.dtype),
        in_specs=[pl.BlockSpec(memory_space=pltpu.VMEM)],
        out_specs=pl.BlockSpec(memory_space=pltpu.VMEM),
        scratch_shapes=[slots(2, layers)]
        + [slots(layers)] * 3
        + [semaphores(2, layers)] * 2
        + [semaphores(layers)] * 6,
        compiler_params=pltpu.CompilerParams(
            collective_id=collective_id, has_side_effects=True, vmem_limit_bytes=60 * 2**20
        ),
    )(terms)


def exchange_kernel(group, spread, x_ref, o_ref, sent, landed, local):
    me = lax.axis_index("seq")
    base = lax.div(me, group) * group
    mine = me - base
    barrier = pltpu.get_barrier_semaphore()
    for step in range(1, group):
        pl.semaphore_signal(
            barrier,
            inc=1,
            device_id={"seq": base + lax.rem(mine + step, group)},
            device_id_type=MESH,
        )
    pl.semaphore_wait(barrier, group - 1)
    own = pltpu.make_async_copy(x_ref if spread else x_ref.at[mine], o_ref.at[mine], local)
    own.start()
    copies = []
    for step in range(1, group):
        other = lax.rem(mine + step, group)
        copies.append(
            pltpu.make_async_remote_copy(
                src_ref=x_ref if spread else x_ref.at[other],
                dst_ref=o_ref.at[mine],
                send_sem=sent.at[step],
                recv_sem=landed.at[step],
                device_id={"seq": base + other},
                device_id_type=MESH,
            )
        )
        copies[-1].start()
    own.wait()
    for copy in copies:
        copy.wait()


def exchanged(x, collective_id, group=None, spread=False):
    group = lax.axis_size("seq") if group is None else group
    shape = (group,) + x.shape if spread else x.shape
    return pl.pallas_call(
        functools.partial(exchange_kernel, group, spread),
        out_shape=jax.ShapeDtypeStruct(shape, x.dtype),
        in_specs=[pl.BlockSpec(memory_space=pl.ANY)],
        out_specs=pl.BlockSpec(memory_space=pl.ANY),
        scratch_shapes=[
            pltpu.SemaphoreType.DMA((group,)),
            pltpu.SemaphoreType.DMA((group,)),
            pltpu.SemaphoreType.DMA(()),
        ],
        compiler_params=pltpu.CompilerParams(
            collective_id=collective_id, has_side_effects=True
        ),
    )(x)


def summed(x, collective_id):
    n = lax.axis_size("seq")
    shares = exchanged(x.reshape(n, -1, x.shape[1]), collective_id)
    total = jnp.sum(shares, axis=0)
    return exchanged(total, collective_id + 1, spread=True).reshape(x.shape)


def swapped(value):
    return lax.ppermute(value, "tp", [(0, 1), (1, 0)])


def rounded(value):
    return lax.reduce_precision(value, 8, 7)


def paired(value):
    kept = rounded(value)
    return kept + swapped(kept.astype(jnp.bfloat16)).astype(jnp.float32)


def in_order(mine, other, axis):
    first = lax.axis_index("tp") == 0
    return jnp.concatenate(
        [jnp.where(first, mine, other), jnp.where(first, other, mine)], axis=axis
    )


def attend_kernel(scaling, q_ref, k_ref, v_ref, qid_ref, kid_ref, o_ref, lse_ref):
    scores = product_nt(q_ref[...], k_ref[...]) * scaling
    scores = jnp.where(qid_ref[...] == kid_ref[...], scores, -1e30)
    peak = jnp.max(scores, axis=1, keepdims=True)
    weights = jnp.exp(scores - peak)
    total = jnp.sum(weights, axis=1, keepdims=True)
    probability = (weights / total).astype(jnp.bfloat16)
    o_ref[...] = product(probability, v_ref[...]).astype(o_ref.dtype)
    lse_ref[...] = peak + jnp.log(total)


def attend_back_kernel(
    scaling, q_ref, k_ref, v_ref, g_ref, qid_ref, kid_ref, lse_ref, dq_ref, dk_ref, dv_ref
):
    @pl.when(pl.program_id(0) == 0)
    def _():
        dk_ref[...] = jnp.zeros_like(dk_ref)
        dv_ref[...] = jnp.zeros_like(dv_ref)

    scores = product_nt(q_ref[...], k_ref[...]) * scaling
    scores = jnp.where(qid_ref[...] == kid_ref[...], scores, -1e30)
    probability = jnp.exp(scores - lse_ref[...])
    dprob = product_nt(g_ref[...], v_ref[...])
    inner = jnp.sum(probability * dprob, axis=1, keepdims=True)
    low = (probability * (dprob - inner)).astype(jnp.bfloat16)
    dq_ref[...] = product(low, k_ref[...]) * scaling
    dk_ref[...] += product_tn(low, q_ref[...]) * scaling
    dv_ref[...] += product_tn(probability.astype(jnp.bfloat16), g_ref[...])


def attention_calls(queries, window, width, tile, scaling):
    tiled = lambda columns: pl.BlockSpec((tile, columns), lambda i: (i, 0))
    whole = lambda rows, columns: pl.BlockSpec((rows, columns), lambda i: (0, 0))
    params = pltpu.CompilerParams(vmem_limit_bytes=56 * 2**20)
    forward = pl.pallas_call(
        functools.partial(attend_kernel, scaling),
        grid=(queries // tile,),
        in_specs=[
            tiled(width),
            whole(window, width),
            whole(window, width),
            tiled(1),
            whole(1, window),
        ],
        out_specs=[tiled(width), tiled(1)],
        out_shape=[
            jax.ShapeDtypeStruct((queries, width), jnp.bfloat16),
            jax.ShapeDtypeStruct((queries, 1), jnp.float32),
        ],
        compiler_params=params,
        cost_estimate=pl.CostEstimate(
            flops=4 * queries * window * width,
            bytes_accessed=2 * (2 * window + 2 * queries) * 128,
            transcendentals=queries * window,
        ),
    )
    backward = pl.pallas_call(
        functools.partial(attend_back_kernel, scaling),
        grid=(queries // tile,),
        in_specs=[
            tiled(width),
            whole(window, width),
            whole(window, width),
            tiled(width),
            tiled(1),
            whole(1, window),
            tiled(1),
        ],
        out_specs=[tiled(width), whole(window, width), whole(window, width)],
        out_shape=[
            jax.ShapeDtypeStruct((queries, width), jnp.float32),
            jax.ShapeDtypeStruct((window, width), jnp.float32),
            jax.ShapeDtypeStruct((window, width), jnp.float32),
        ],
        compiler_params=params,
        cost_estimate=pl.CostEstimate(
            flops=10 * queries * window * width,
            bytes_accessed=2 * (6 * window + 4 * queries) * 128,
            transcendentals=queries * window,
        ),
    )
    return forward, backward


def padded_columns(matrix, width):
    return jnp.pad(matrix, ((0, 0), (0, width - matrix.shape[1])))


def tokens_travel(
    patches,
    lengths,
    ln1_gain,
    ln1_bias,
    q_weight,
    q_bias,
    k_weight,
    v_weight,
    v_bias,
    o_weight,
    o_bias,
    ln2_gain,
    ln2_bias,
    up_weight,
    up_bias,
    down_weight,
    down_bias,
    gate_proj,
    up_proj,
    down_proj,
    ctx_gain,
    rk_weight,
    rv_weight,
    latents,
    lat_gain,
    rq_weight,
    ro_weight,
    feat_grad,
    lat_grad,
):
    low = jnp.bfloat16
    rows, width = patches.shape
    half = rows // 2
    n = lax.axis_size("seq")
    me = lax.axis_index("seq")
    core = lax.axis_index("tp")
    total_rows = rows * n
    longest = min(IMGMAX, (n // 2 - 1) * rows)
    heads = q_bias.shape[0] // HD
    part = me // heads
    queries = total_rows // 2
    window = total_rows - longest
    window_start = part * longest
    query_start = part * (queries - longest)
    scaling = HD ** (-0.5)
    kv_heads = rk_weight.shape[1] // RHD
    q_heads = rq_weight.shape[1] // RHD
    group = q_heads // kv_heads
    lat_rows = latents.shape[0]
    lat_scaling = RHD ** (-0.5)
    first_block = (me == 0).astype(jnp.float32)
    shard = q_weight.shape[0]
    hidden_units = up_bias.shape[0]
    hidden_pad = -(-hidden_units // 128) * 128
    proj_units = gate_proj.shape[1] // n
    out_width = down_proj.shape[1] * n

    def my_half(value):
        return lax.dynamic_slice_in_dim(value, core * half, half, 0)

    vision_shard = jnp.concatenate(
        [
            padded_columns(up_weight, hidden_pad),
            padded_columns(down_weight.T, hidden_pad),
            o_weight.T,
            q_weight,
            k_weight,
            v_weight,
        ],
        axis=1,
    )
    vision = lax.all_gather(vision_shard, "seq", axis=0, tiled=True)
    w_up = vision[:, :hidden_units]
    w_down_t = vision[:, hidden_pad : hidden_pad + hidden_units]
    at = 2 * hidden_pad
    own_width = heads * HD
    w_out_t, w_query, w_key, w_value = (
        vision[:, at + i * own_width : at + (i + 1) * own_width] for i in range(4)
    )
    w_ctx = lax.all_gather(
        jnp.concatenate([rk_weight, rv_weight], axis=1), "seq", axis=0, tiled=True
    )
    ctx_width = rk_weight.shape[1]
    w_ctxkey, w_ctxval = w_ctx[:, :ctx_width], w_ctx[:, ctx_width:]

    input_f32 = patches.astype(jnp.float32)
    normed_in = layer_norm(input_f32, ln1_gain, ln1_bias).astype(low)
    head_shard = jnp.concatenate(
        [split_heads(w, heads) for w in (q_weight, k_weight, v_weight)], axis=2
    )
    head_weight = exchanged(jnp.concatenate([head_shard] * 2, axis=0), 1).reshape(width, 3 * HD)
    normed_half = gathered_blocks(my_half(normed_in), 2)
    normed_half = lax.dynamic_slice_in_dim(normed_half, window_start // rows, window // rows, 0)
    normed_window = in_order(
        normed_half[:, None], swapped(normed_half)[:, None], 1
    ).reshape(window, width)
    head = me - part * heads
    q_bias_one = lax.dynamic_slice_in_dim(q_bias, head * HD, HD, 0)
    v_bias_one = lax.dynamic_slice_in_dim(v_bias, head * HD, HD, 0)
    bias_one = jnp.concatenate([q_bias_one, jnp.zeros_like(q_bias_one), v_bias_one])
    qkv = (product(normed_window, head_weight) + bias_one).astype(low)
    query_one = lax.dynamic_slice_in_dim(qkv[:, :HD], query_start, queries, 0)
    key_one = qkv[:, HD : 2 * HD]
    value_one = qkv[:, 2 * HD :]
    key_ids = image_ids(
        lengths, window_start + jnp.arange(window, dtype=jnp.int32), total_rows
    )
    query_ids = lax.dynamic_slice_in_dim(key_ids, query_start, queries, 0)[:, None]
    key_ids = key_ids[None, :]
    attend, attend_back = attention_calls(queries, window, HD, rows, scaling)
    attended_one, lse_one = attend(query_one, key_one, value_one, query_ids, key_ids)
    attended_low = join_heads(exchanged(attended_one.reshape(heads, rows, HD), 3, group=heads))

    def to_units(matrix):
        blocks = matrix.reshape(shard, n, proj_units).transpose(1, 0, 2)
        return lax.all_to_all(blocks, "seq", 0, 0).reshape(width, proj_units)

    gate_mine, up_mine = to_units(gate_proj), to_units(up_proj)
    down_mine = (
        lax.all_to_all(down_proj.reshape(n, proj_units, -1), "seq", 0, 0)
        .transpose(1, 0, 2)
        .reshape(proj_units, out_width)
    )
    w_gate = jnp.concatenate([gate_mine, swapped(gate_mine)], axis=1)
    w_up_proj = jnp.concatenate([up_mine, swapped(up_mine)], axis=1)
    w_down_proj = jnp.concatenate([down_mine, swapped(down_mine)], axis=0)

    attn_part = product_nt(attended_low, w_out_t)
    attn_sum = attn_part + swapped(attn_part)
    after_attn = input_f32 + attn_sum + o_bias
    mlp_in = layer_norm(after_attn, ln2_gain, ln2_bias).astype(low)
    hidden = product(mlp_in, w_up) + up_bias
    active_low = gelu_tanh(hidden).astype(low)
    after_mlp = after_attn + paired(product_nt(active_low, w_down_t)) + down_bias
    features = after_mlp.astype(low)

    features_all = gathered_blocks(my_half(features), 4).reshape(n * half, width)
    proj_gate = product(features_all, w_gate)
    proj_up = product(features_all, w_up_proj)
    silu_gate = jax.nn.silu(proj_gate)
    proj_hidden = (silu_gate * proj_up).astype(low)

    def chunked(terms, chunks):
        return terms.reshape(n, half, chunks, -1).transpose(2, 0, 1, 3)

    def joined_chunks(sums):
        return sums.transpose(1, 0, 2).reshape(half, -1)

    out_chunks = out_width // 512
    out_terms = jnp.stack(
        [
            product(proj_hidden, w_down_proj[:, c * 512 : (c + 1) * 512]).astype(low)
            for c in range(out_chunks)
        ]
    ).reshape(out_chunks, n, half, 512)
    proj_out_low = joined_chunks(scattered_sum(out_terms, 5))
    proj_out_half = proj_out_low.astype(jnp.float32)
    proj_out = in_order(proj_out_low, swapped(proj_out_low), 0).astype(jnp.float32)

    context_low = rms_norm(proj_out, ctx_gain).astype(low)
    ctx_keys = product(context_low, w_ctxkey).astype(low)
    ctx_values = product(context_low, w_ctxval).astype(low)
    lat_normed = rms_norm(latents, lat_gain).astype(low)
    lat_queries = product(lat_normed, rq_weight).astype(low)
    lat_keys = product(lat_normed, w_ctxkey).astype(low)
    lat_values = product(lat_normed, w_ctxval).astype(low)
    query_grouped = lat_queries.reshape(lat_rows, kv_heads, group, RHD)
    key_grouped = ctx_keys.reshape(rows, kv_heads, RHD)
    value_grouped = ctx_values.reshape(rows, kv_heads, RHD)
    self_keys = lat_keys.reshape(lat_rows, kv_heads, RHD)
    self_values = lat_values.reshape(lat_rows, kv_heads, RHD)
    lat_scores = (
        jnp.einsum("lkgd,tkd->kglt", query_grouped, key_grouped, preferred_element_type=jnp.float32)
        * lat_scaling
    )
    self_scores = (
        jnp.einsum("lkgd,tkd->kglt", query_grouped, self_keys, preferred_element_type=jnp.float32)
        * lat_scaling
    )
    stats = partial_stats(lat_scores, value_grouped)
    packed = jnp.concatenate([stats[2], stats[0][..., None], stats[1][..., None]], axis=-1)
    packed = jnp.pad(packed.reshape(n, -1, RHD + 2), ((0, 0), (0, 0), (0, 126 - RHD)))
    shares = exchanged(packed, 6)
    share_peak = jnp.max(shares[..., RHD], axis=0)
    share_scale = jnp.exp(shares[..., RHD] - share_peak)
    share_sums = jnp.sum(shares * share_scale[..., None], axis=0)
    share_sums = jnp.where(
        jnp.arange(128) == RHD, share_peak[:, None], share_sums
    )
    merged = exchanged(share_sums, 7, spread=True).reshape(kv_heads, group, lat_rows, 128)
    lat_peak, lat_total, lat_numer = joint_stats(
        (merged[..., RHD], merged[..., RHD + 1], merged[..., :RHD]),
        partial_stats(self_scores, self_values),
    )
    lat_lse = lat_peak + jnp.log(lat_total)
    pooled_exact = lat_numer / lat_total[..., None]
    pooled_low = pooled_exact.transpose(2, 0, 1, 3).reshape(lat_rows, -1).astype(low)
    lat_mix = product(pooled_low, ro_weight)
    ro_width = ro_weight.shape[1] // n
    ro_columns = lax.dynamic_slice_in_dim(lat_grad, me * ro_width, ro_width, 1)
    ro_weight_grad = product_tn(pooled_low, ro_columns)
    pooled_grad = product_nt(lat_grad, ro_weight).astype(low)
    pooled_grouped = pooled_grad.reshape(lat_rows, kv_heads, group, RHD)
    pooled_f32 = pooled_grouped.astype(jnp.float32)
    lat_delta = jnp.sum(pooled_f32.transpose(1, 2, 0, 3) * pooled_exact, axis=-1)

    def score_grads(scores, key_part, value_part):
        probability = jnp.exp(scores - lat_lse[..., None])
        dprob = jnp.einsum(
            "lkgd,tkd->kglt", pooled_grouped, value_part, preferred_element_type=jnp.float32
        )
        dscore = (probability * (dprob - lat_delta[..., None])).astype(low)
        query_term = (
            jnp.einsum("kglt,tkd->lkgd", dscore, key_part, preferred_element_type=jnp.float32)
            * lat_scaling
        )
        key_term = (
            jnp.einsum("kglt,lkgd->tkd", dscore, query_grouped, preferred_element_type=jnp.float32)
            * lat_scaling
        ).astype(low)
        value_term = jnp.einsum(
            "kglt,lkgd->tkd", probability, pooled_f32, precision=lax.Precision.HIGHEST
        ).astype(low)
        return (
            query_term,
            key_term.reshape(key_part.shape[0], -1),
            value_term.reshape(key_part.shape[0], -1),
        )

    ctx_query_term, ctx_keys_grad, ctx_values_grad = score_grads(
        lat_scores, key_grouped, value_grouped
    )
    self_query_term, self_keys_grad, self_values_grad = score_grads(
        self_scores, self_keys, self_values
    )
    ctx_part = product_nt(ctx_keys_grad, w_ctxkey) + product_nt(ctx_values_grad, w_ctxval)
    ctx_kept = rounded(my_half(ctx_part))
    ctx_sent = lax.dynamic_slice_in_dim(ctx_part, (1 - core) * half, half, 0).astype(low)
    ctx_back = ctx_kept + swapped(ctx_sent).astype(jnp.float32)
    ctx_pull = jax.vjp(rms_norm, proj_out_half, ctx_gain)[1]
    proj_out_grad, ctx_gain_part = ctx_pull(ctx_back)
    proj_out_grads = gathered_blocks(proj_out_grad.astype(low), 8).reshape(n * half, out_width)

    query_part = ctx_query_term + first_block * self_query_term
    query_sum = summed(query_part.reshape(lat_rows, -1), 9)
    lat_queries_grad = query_sum.astype(low)
    rq_rows = rq_weight.shape[0] // n
    rq_weight_grad = product_tn(
        lax.dynamic_slice_in_dim(lat_normed, me * rq_rows, rq_rows, 1), lat_queries_grad
    )
    ctx_grads = jnp.concatenate([ctx_keys_grad, ctx_values_grad], axis=1)
    self_grads = jnp.concatenate([self_keys_grad, self_values_grad], axis=1)
    r_part = product_tn(context_low, ctx_grads) + first_block * product_tn(lat_normed, self_grads)
    r_grad = lax.psum_scatter(r_part.astype(low), "seq", scatter_dimension=0, tiled=True).astype(
        jnp.float32
    )
    lat_part = (
        product_nt(lat_queries_grad, rq_weight)
        + product_nt(self_keys_grad, w_ctxkey)
        + product_nt(self_values_grad, w_ctxval)
    )
    lat_back, lat_mix_sum = paired(lat_part), paired(lat_mix)
    latents_out = latents + lat_mix_sum
    lat_pull = jax.vjp(rms_norm, latents, lat_gain)[1]
    lat_in_grad, lat_gain_grad = lat_pull(lat_back)
    latents_grad = lat_grad.astype(jnp.float32) + lat_in_grad

    hidden_pgrad = product_nt(proj_out_grads, w_down_proj)
    silu_pull = jax.vjp(jax.nn.silu, proj_gate)[1]
    gate_grad_low = silu_pull(hidden_pgrad * proj_up)[0].astype(low)
    up_grad_low = (hidden_pgrad * silu_gate).astype(low)
    feat_terms = (product_nt(gate_grad_low, w_gate) + product_nt(up_grad_low, w_up_proj)).astype(low)
    feat_half = joined_chunks(scattered_sum(chunked(feat_terms, width // 384), 11))
    proj_in_grad = in_order(feat_half, swapped(feat_half), 0).astype(jnp.float32)

    def unit_grads(left, right, axis):
        mine = lax.slice_in_dim(left, 0, proj_units, axis=1) if axis == 0 else left
        other = lax.slice_in_dim(left, proj_units, 2 * proj_units, axis=1) if axis == 0 else left
        mine_r = right if axis == 0 else lax.slice_in_dim(right, 0, proj_units, axis=1)
        other_r = right if axis == 0 else lax.slice_in_dim(right, proj_units, 2 * proj_units, axis=1)
        sent = swapped(product_tn(other, other_r).astype(low))
        return (product_tn(mine, mine_r) + sent.astype(jnp.float32)).astype(low)

    def to_rows(grad):
        blocks = lax.all_to_all(grad.reshape(n, shard, proj_units), "seq", 0, 0)
        return blocks.transpose(1, 0, 2).reshape(shard, n * proj_units).astype(jnp.float32)

    gate_proj_grad = to_rows(unit_grads(features_all, gate_grad_low, 1))
    up_proj_grad = to_rows(unit_grads(features_all, up_grad_low, 1))
    down_blocks = unit_grads(proj_hidden, proj_out_grads, 0)
    down_blocks = down_blocks.reshape(proj_units, n, -1).transpose(1, 0, 2)
    down_proj_grad = (
        lax.all_to_all(down_blocks, "seq", 0, 0)
        .reshape(n * proj_units, -1)
        .astype(jnp.float32)
    )

    mlp_out_grad = feat_grad.astype(jnp.float32) + proj_in_grad
    mlp_out_low = mlp_out_grad.astype(low)
    down_part_t = product_tn(mlp_out_low, active_low)
    down_bias_part = jnp.sum(mlp_out_low.astype(jnp.float32), axis=0)
    active_grad = product(mlp_out_low, w_down_t)
    gelu_pull = jax.vjp(gelu_tanh, hidden)[1]
    hidden_grad = gelu_pull(active_grad)[0].astype(low)
    up_part = product_tn(mlp_in, hidden_grad)
    up_bias_part = jnp.sum(hidden_grad.astype(jnp.float32), axis=0)
    mlp_back = paired(product_nt(hidden_grad, w_up))
    ln2_pull = jax.vjp(layer_norm, after_attn, ln2_gain, ln2_bias)[1]
    norm_grad, ln2_gain_part, ln2_bias_part = ln2_pull(mlp_back)
    attn_out_grad = mlp_out_grad + norm_grad
    attn_out_low = attn_out_grad.astype(low)
    o_part_t = product_tn(attn_out_low, attended_low)
    o_bias_part = jnp.sum(attn_out_low.astype(jnp.float32), axis=0)
    vision_part = jnp.concatenate(
        [
            padded_columns(up_part.astype(low), hidden_pad),
            padded_columns(down_part_t.astype(low), hidden_pad),
            o_part_t.astype(low),
        ],
        axis=1,
    )
    vision_grad = lax.psum_scatter(vision_part, "seq", scatter_dimension=0, tiled=True).astype(
        jnp.float32
    )
    up_weight_grad = vision_grad[:, :hidden_units]
    down_weight_grad = vision_grad[:, hidden_pad : hidden_pad + hidden_units].T
    o_weight_grad = vision_grad[:, 2 * hidden_pad :].T

    attended_grad = product(attn_out_low, w_out_t).astype(low)
    grad_one = exchanged(split_heads(attended_grad, heads), 12, group=heads).reshape(queries, HD)
    dq, dk, dv = attend_back(
        query_one, key_one, value_one, grad_one, query_ids, key_ids, lse_one
    )
    dq_window = lax.dynamic_update_slice_in_dim(
        jnp.zeros((window, HD), jnp.float32), dq, query_start, 0
    )
    dqkv = jnp.concatenate([dq_window, dk, dv], axis=1)
    dqkv_low = dqkv.astype(low)
    head_grad = product_tn(normed_window, dqkv_low).astype(low).reshape(n, shard, 3 * HD)
    head_grads = exchanged(head_grad, 13).astype(jnp.float32)
    head_grads = head_grads[:heads] + head_grads[heads:]
    q_weight_grad, k_weight_grad, v_weight_grad = (
        join_heads(head_grads[:, :, i * HD : (i + 1) * HD]) for i in range(3)
    )
    bias_row = jnp.sum(dqkv_low.astype(jnp.float32), axis=0)
    bias_rows = jnp.zeros((heads, 3 * HD), jnp.float32)
    bias_rows = lax.dynamic_update_slice_in_dim(bias_rows, bias_row[None], head, 0)
    blocks = dqkv.reshape(window // rows, rows, 3 * HD)
    other_block = jnp.where(part == 0, blocks[-1], blocks[0]).astype(low)
    across = lax.ppermute(
        other_block, "seq", [(i, (i + heads) % n) for i in range(n)]
    ).astype(jnp.float32)
    own_blocks = lax.dynamic_slice_in_dim(blocks, part, heads, 0)
    edge = jnp.where(part == 0, heads - 1, 0)
    own_blocks = own_blocks + jnp.where(
        (jnp.arange(heads) == edge)[:, None, None], across[None], 0.0
    )
    token_grads = exchanged(own_blocks.astype(low), 14, group=heads)
    queries_grad, keys_grad, values_grad = (
        join_heads(token_grads[:, :, i * HD : (i + 1) * HD]) for i in range(3)
    )
    attn_back = paired(
        product_nt(queries_grad, w_query)
        + product_nt(keys_grad, w_key)
        + product_nt(values_grad, w_value)
    )
    ln1_pull = jax.vjp(layer_norm, input_f32, ln1_gain, ln1_bias)[1]
    in_grad, ln1_gain_part, ln1_bias_part = ln1_pull(attn_back)
    patches_grad = (attn_out_grad + in_grad).astype(low)

    smalls = (
        ln1_gain_part,
        ln1_bias_part,
        bias_rows[:, :HD].reshape(-1),
        bias_rows[:, 2 * HD :].reshape(-1),
        o_bias_part,
        ln2_gain_part,
        ln2_bias_part,
        up_bias_part,
        down_bias_part,
        ctx_gain_part,
    )
    joined_smalls = jnp.concatenate(smalls)
    length = joined_smalls.shape[0]
    per_device = -(-length // (n * 1024)) * 1024
    joined_smalls = jnp.pad(joined_smalls, (0, n * per_device - length))
    small_sum = summed(joined_smalls.reshape(n * per_device // 128, 128), 15).reshape(-1)
    small_sums, begin = [], 0
    for small in smalls:
        small_sums.append(small_sum[begin : begin + small.shape[0]])
        begin += small.shape[0]
    ctx_gain_grad = small_sums[9] + swapped(small_sums[9])
    return (
        features,
        latents_out,
        patches_grad,
        latents_grad,
        small_sums[0],
        small_sums[1],
        q_weight_grad,
        small_sums[2],
        k_weight_grad,
        v_weight_grad,
        small_sums[3],
        o_weight_grad,
        small_sums[4],
        small_sums[5],
        small_sums[6],
        up_weight_grad,
        small_sums[7],
        down_weight_grad,
        small_sums[8],
        gate_proj_grad,
        up_proj_grad,
        down_proj_grad,
        ctx_gain_grad,
        r_grad[:, :ctx_width],
        r_grad[:, ctx_width:],
        lat_gain_grad,
        rq_weight_grad,
        ro_weight_grad,
    )


def solution(mesh):
    placed = (
        P("seq", None),
        P(),
        P(),
        P(),
        P("seq", "tp"),
        P("tp"),
        P("seq", "tp"),
        P("seq", "tp"),
        P("tp"),
        P("tp", "seq"),
        P(),
        P(),
        P(),
        P("seq", "tp"),
        P("tp"),
        P("tp", "seq"),
        P(),
        P("seq", "tp"),
        P("seq", "tp"),
        P("tp", "seq"),
        P(),
        P("seq", "tp"),
        P("seq", "tp"),
        P(),
        P(),
        P(None, "tp"),
        P("tp", None),
        P("seq", None),
        P(),
    )
    few = mesh.shape["tp"] == 2 and mesh.shape["seq"] == 16
    return jax.shard_map(
        tokens_travel if few else weights_travel,
        mesh=mesh,
        in_specs=placed,
        out_specs=(
            P("seq", None),
            P(),
            P("seq", None),
            P(),
            P(),
            P(),
            P("seq", "tp"),
            P("tp"),
            P("seq", "tp"),
            P("seq", "tp"),
            P("tp"),
            P("tp", "seq"),
            P(),
            P(),
            P(),
            P("seq", "tp"),
            P("tp"),
            P("tp", "seq"),
            P(),
            P("seq", "tp"),
            P("seq", "tp"),
            P("tp", "seq"),
            P(),
            P("seq", "tp"),
            P("seq", "tp"),
            P(),
            P("seq", "tp"),
            P("tp", "seq"),
        ),
        check_vma=False,
    )
```

```python
import functools

import jax
import jax.experimental.pallas as pl
import jax.experimental.pallas.tpu as pltpu
import jax.numpy as jnp
from jax import lax
from jax.sharding import PartitionSpec as P

HD = 72
RHD = 96
IMGMAX = 4900


EPS = 1e-06


def passed_along(value, axis, steps):
    count = lax.axis_size(axis)
    first, last = (max(0, -steps), min(count, count - steps))
    return lax.ppermute(value, axis, [(source, source + steps) for source in range(first, last)])


def joined(part, axis, combine):
    gathered = jax.tree.map(lambda a: lax.all_gather(a, axis), part)

    def take(source):
        return jax.tree.map(lambda a: lax.dynamic_index_in_dim(a, source, 0, False), gathered)

    return lax.fori_loop(
        1, lax.axis_size(axis), lambda source, state: combine(state, take(source)), take(0)
    )


def layer_norm(value, gain, bias):
    centred = value - jnp.mean(value, axis=-1, keepdims=True)
    return (
        centred * lax.rsqrt(jnp.mean(centred * centred, axis=-1, keepdims=True) + EPS) * gain + bias
    )


def rms_norm(value, gain):
    return value * lax.rsqrt(jnp.mean(value * value, axis=-1, keepdims=True) + EPS) * gain


def gelu_tanh(value):
    return jax.nn.gelu(value, approximate=True)


def product(left, right):
    return jnp.dot(left, right, preferred_element_type=jnp.float32)


def product_nt(left, right):
    return lax.dot_general(
        left, right, (((1,), (1,)), ((), ())), preferred_element_type=jnp.float32
    )


def product_tn(left, right):
    return lax.dot_general(
        left, right, (((0,), (0,)), ((), ())), preferred_element_type=jnp.float32
    )


def image_ids(lengths, positions, total_rows):
    image_ends = jnp.cumsum(lengths)
    counted = jnp.sum((image_ends[None, :] <= positions[:, None]).astype(jnp.int32), axis=1)
    inside = (positions >= 0) & (positions < total_rows)
    return jnp.where(inside, counted, -1)


def split_heads(matrix, count):
    return matrix.reshape(matrix.shape[0], count, -1).transpose(1, 0, 2)


def join_heads(stacked):
    return stacked.transpose(1, 0, 2).reshape(stacked.shape[1], -1)


def neighbour(first, second, offset):
    return passed_along((first, second), "seq", offset)


def returned(first, second, offset):
    return (
        passed_along(first.astype(jnp.bfloat16), "seq", offset).astype(first.dtype),
        passed_along(second.astype(jnp.bfloat16), "seq", offset).astype(second.dtype),
    )


def partial_stats(scores, value_heads):
    peak = jnp.max(scores, axis=-1)
    weights = jnp.exp(scores - peak[..., None])
    total = jnp.sum(weights, axis=-1)
    numer = jnp.einsum(
        "kglt,tkd->kgld", weights, value_heads.astype(jnp.float32), precision=lax.Precision.HIGHEST
    )
    return (peak, total, numer)


def joint_stats(left, right):
    peak = jnp.maximum(left[0], right[0])
    left_scale = jnp.exp(left[0] - peak)
    right_scale = jnp.exp(right[0] - peak)
    total = left[1] * left_scale + right[1] * right_scale
    numer = left[2] * left_scale[..., None] + right[2] * right_scale[..., None]
    return (peak, total, numer)


def weights_travel(
    patches,
    lengths,
    ln1_gain,
    ln1_bias,
    q_weight,
    q_bias,
    k_weight,
    v_weight,
    v_bias,
    o_weight,
    o_bias,
    ln2_gain,
    ln2_bias,
    up_weight,
    up_bias,
    down_weight,
    down_bias,
    gate_proj,
    up_proj,
    down_proj,
    ctx_gain,
    rk_weight,
    rv_weight,
    latents,
    lat_gain,
    rq_weight,
    ro_weight,
    feat_grad,
    lat_grad,
):
    tok_rows = patches.shape[0]
    seq_count = lax.axis_size("seq")
    seq_place = lax.axis_index("seq")
    total_rows = tok_rows * seq_count
    longest = min(IMGMAX, (seq_count // 2 - 1) * tok_rows)
    reach_blocks = (longest + tok_rows - 2) // tok_rows
    local_heads = q_bias.shape[0] // HD
    kv_heads = rk_weight.shape[1] // RHD
    q_heads = rq_weight.shape[1] // RHD
    group = q_heads // kv_heads
    lat_rows = latents.shape[0]
    scaling = HD ** (-0.5)
    lat_scaling = RHD ** (-0.5)
    first_block = (seq_place == 0).astype(jnp.float32)
    gathered = (
        lax.all_gather(q_weight, "seq", axis=0, tiled=True),
        lax.all_gather(k_weight, "seq", axis=0, tiled=True),
        lax.all_gather(v_weight, "seq", axis=0, tiled=True),
        lax.all_gather(o_weight, "seq", axis=1, tiled=True),
        lax.all_gather(up_weight, "seq", axis=0, tiled=True),
        lax.all_gather(down_weight, "seq", axis=1, tiled=True),
        lax.all_gather(gate_proj, "seq", axis=0, tiled=True),
        lax.all_gather(up_proj, "seq", axis=0, tiled=True),
        lax.all_gather(down_proj, "seq", axis=1, tiled=True),
        lax.all_gather(rk_weight, "seq", axis=0, tiled=True),
        lax.all_gather(rv_weight, "seq", axis=0, tiled=True),
    )
    (
        w_query,
        w_key,
        w_value,
        w_out,
        w_up,
        w_down,
        w_gate_proj,
        w_up_proj,
        w_down_proj,
        w_ctxkey,
        w_ctxval,
    ) = gathered
    input_f32 = patches.astype(jnp.float32)
    normed_in = layer_norm(input_f32, ln1_gain, ln1_bias).astype(jnp.bfloat16)
    queries_low = (product(normed_in, w_query) + q_bias).astype(jnp.bfloat16)
    keys_low = product(normed_in, w_key).astype(jnp.bfloat16)
    values_low = (product(normed_in, w_value) + v_bias).astype(jnp.bfloat16)
    upper_pairs = []
    lower_pairs = []
    upper_pair = (keys_low, values_low)
    lower_pair = (keys_low, values_low)
    for distance in range(1, reach_blocks + 1):
        upper_pair = neighbour(upper_pair[0], upper_pair[1], -1)
        lower_pair = neighbour(lower_pair[0], lower_pair[1], 1)
        upper_pairs.append(upper_pair)
        lower_pairs.append(lower_pair)
    ordered = lower_pairs[::-1] + [(keys_low, values_low)] + upper_pairs
    key_buffer = jnp.concatenate([pair[0] for pair in ordered], axis=0)
    value_buffer = jnp.concatenate([pair[1] for pair in ordered], axis=0)
    own_positions = seq_place * tok_rows + jnp.arange(tok_rows, dtype=jnp.int32)
    query_ids = image_ids(lengths, own_positions, total_rows)
    key_positions = (seq_place - reach_blocks) * tok_rows + jnp.arange(
        (2 * reach_blocks + 1) * tok_rows, dtype=jnp.int32
    )
    key_ids = image_ids(lengths, key_positions, total_rows)
    allowed = query_ids[:, None] == key_ids[None, :]
    query_heads = split_heads(queries_low, local_heads)
    key_heads = split_heads(key_buffer, local_heads)
    value_heads = split_heads(value_buffer, local_heads)

    def head_forward(operands):
        query_one, key_one, value_one = operands
        scores = jnp.where(allowed, product_nt(query_one, key_one) * scaling, -1e30)
        peak = jnp.max(scores, axis=1, keepdims=True)
        exponent = jnp.exp(scores - peak)
        total_exp = jnp.sum(exponent, axis=1, keepdims=True)
        probability = exponent / total_exp
        result = product(probability.astype(jnp.bfloat16), value_one)
        return (result, peak[:, 0] + jnp.log(total_exp[:, 0]))

    head_result, head_lse = lax.map(head_forward, (query_heads, key_heads, value_heads))
    attended_low = join_heads(head_result).astype(jnp.bfloat16)
    attn_sum = lax.psum(product(attended_low, w_out), "tp")
    after_attn = input_f32 + attn_sum + o_bias
    mlp_in = layer_norm(after_attn, ln2_gain, ln2_bias).astype(jnp.bfloat16)
    hidden = product(mlp_in, w_up) + up_bias
    active_low = gelu_tanh(hidden).astype(jnp.bfloat16)
    mlp_sum = lax.psum(product(active_low, w_down).astype(jnp.bfloat16), "tp").astype(jnp.float32)
    after_mlp = after_attn + mlp_sum + down_bias
    features = after_mlp.astype(jnp.bfloat16)
    proj_gate = product(features, w_gate_proj)
    proj_up = product(features, w_up_proj)
    silu_gate = jax.nn.silu(proj_gate)
    proj_hidden = (silu_gate * proj_up).astype(jnp.bfloat16)
    proj_out = lax.psum(product(proj_hidden, w_down_proj).astype(jnp.bfloat16), "tp").astype(
        jnp.float32
    )
    context_low = rms_norm(proj_out, ctx_gain).astype(jnp.bfloat16)
    ctx_keys = product(context_low, w_ctxkey).astype(jnp.bfloat16)
    ctx_values = product(context_low, w_ctxval).astype(jnp.bfloat16)
    lat_normed = rms_norm(latents, lat_gain).astype(jnp.bfloat16)
    lat_queries = product(lat_normed, rq_weight).astype(jnp.bfloat16)
    lat_keys = product(lat_normed, w_ctxkey).astype(jnp.bfloat16)
    lat_values = product(lat_normed, w_ctxval).astype(jnp.bfloat16)
    query_grouped = lat_queries.reshape(lat_rows, kv_heads, group, RHD)
    key_grouped = ctx_keys.reshape(tok_rows, kv_heads, RHD)
    value_grouped = ctx_values.reshape(tok_rows, kv_heads, RHD)
    self_keys = lat_keys.reshape(lat_rows, kv_heads, RHD)
    self_values = lat_values.reshape(lat_rows, kv_heads, RHD)
    lat_scores = (
        jnp.einsum("lkgd,tkd->kglt", query_grouped, key_grouped, preferred_element_type=jnp.float32)
        * lat_scaling
    )
    self_scores = (
        jnp.einsum("lkgd,tkd->kglt", query_grouped, self_keys, preferred_element_type=jnp.float32)
        * lat_scaling
    )
    merged = joined(partial_stats(lat_scores, value_grouped), "seq", joint_stats)
    lat_peak, lat_total, lat_numer = joint_stats(merged, partial_stats(self_scores, self_values))
    lat_lse = lat_peak + jnp.log(lat_total)
    pooled_exact = lat_numer / lat_total[..., None]
    pooled_low = pooled_exact.transpose(2, 0, 1, 3).reshape(lat_rows, -1).astype(jnp.bfloat16)
    lat_mix = product(pooled_low, ro_weight)
    ro_width = ro_weight.shape[1] // seq_count
    ro_columns = lax.dynamic_slice_in_dim(lat_grad, seq_place * ro_width, ro_width, 1)
    ro_weight_grad = product_tn(pooled_low, ro_columns)
    pooled_grad = product_nt(lat_grad, ro_weight).astype(jnp.bfloat16)
    pooled_grouped = pooled_grad.reshape(lat_rows, kv_heads, group, RHD)
    pooled_f32 = pooled_grouped.astype(jnp.float32)
    lat_delta = jnp.sum(pooled_f32.transpose(1, 2, 0, 3) * pooled_exact, axis=-1)

    def score_grads(scores, key_part, value_part):
        probability = jnp.exp(scores - lat_lse[..., None])
        dprob = jnp.einsum(
            "lkgd,tkd->kglt", pooled_grouped, value_part, preferred_element_type=jnp.float32
        )
        dscore = (probability * (dprob - lat_delta[..., None])).astype(jnp.bfloat16)
        query_term = (
            jnp.einsum("kglt,tkd->lkgd", dscore, key_part, preferred_element_type=jnp.float32)
            * lat_scaling
        )
        key_term = (
            jnp.einsum("kglt,lkgd->tkd", dscore, query_grouped, preferred_element_type=jnp.float32)
            * lat_scaling
        ).astype(jnp.bfloat16)
        value_term = jnp.einsum(
            "kglt,lkgd->tkd", probability, pooled_f32, precision=lax.Precision.HIGHEST
        ).astype(jnp.bfloat16)
        return (
            query_term,
            key_term.reshape(key_part.shape[0], -1),
            value_term.reshape(key_part.shape[0], -1),
        )

    ctx_query_term, ctx_keys_grad, ctx_values_grad = score_grads(
        lat_scores, key_grouped, value_grouped
    )
    self_query_term, self_keys_grad, self_values_grad = score_grads(
        self_scores, self_keys, self_values
    )
    query_part = ctx_query_term + first_block * self_query_term
    query_sum = lax.psum(query_part, "seq")
    lat_queries_grad = query_sum.reshape(lat_rows, -1).astype(jnp.bfloat16)
    rq_rows = rq_weight.shape[0] // seq_count
    rq_weight_grad = product_tn(
        lax.dynamic_slice_in_dim(lat_normed, seq_place * rq_rows, rq_rows, 1), lat_queries_grad
    )
    rk_part = product_tn(context_low, ctx_keys_grad) + first_block * product_tn(
        lat_normed, self_keys_grad
    )
    rv_part = product_tn(context_low, ctx_values_grad) + first_block * product_tn(
        lat_normed, self_values_grad
    )
    ctx_part = product_nt(ctx_keys_grad, w_ctxkey) + product_nt(ctx_values_grad, w_ctxval)
    lat_part = (
        product_nt(lat_queries_grad, rq_weight)
        + product_nt(self_keys_grad, w_ctxkey)
        + product_nt(self_values_grad, w_ctxval)
    )
    ctx_back, lat_back, lat_mix_sum = (
        lax.psum(ctx_part.astype(jnp.bfloat16), "tp").astype(jnp.float32),
        lax.psum(lat_part.astype(jnp.bfloat16), "tp").astype(jnp.float32),
        lax.psum(lat_mix.astype(jnp.bfloat16), "tp").astype(jnp.float32),
    )
    latents_out = latents + lat_mix_sum
    lat_pull = jax.vjp(rms_norm, latents, lat_gain)[1]
    lat_in_grad, lat_gain_grad = lat_pull(lat_back)
    latents_grad = lat_grad.astype(jnp.float32) + lat_in_grad
    ctx_pull = jax.vjp(rms_norm, proj_out, ctx_gain)[1]
    proj_out_grad, ctx_gain_part = ctx_pull(ctx_back)
    proj_out_low = proj_out_grad.astype(jnp.bfloat16)
    down_proj_part = product_tn(proj_hidden, proj_out_low)
    hidden_pgrad = product_nt(proj_out_low, w_down_proj)
    silu_pull = jax.vjp(jax.nn.silu, proj_gate)[1]
    gate_grad_low = silu_pull(hidden_pgrad * proj_up)[0].astype(jnp.bfloat16)
    up_grad_low = (hidden_pgrad * silu_gate).astype(jnp.bfloat16)
    gate_proj_part = product_tn(features, gate_grad_low)
    up_proj_part = product_tn(features, up_grad_low)
    proj_in_grad = lax.psum(
        (product_nt(gate_grad_low, w_gate_proj) + product_nt(up_grad_low, w_up_proj)).astype(
            jnp.bfloat16
        ),
        "tp",
    ).astype(jnp.float32)
    mlp_out_grad = feat_grad.astype(jnp.float32) + proj_in_grad
    mlp_out_low = mlp_out_grad.astype(jnp.bfloat16)
    down_part = product_tn(active_low, mlp_out_low)
    down_bias_part = jnp.sum(mlp_out_low.astype(jnp.float32), axis=0)
    active_grad = product_nt(mlp_out_low, w_down)
    gelu_pull = jax.vjp(gelu_tanh, hidden)[1]
    hidden_grad = gelu_pull(active_grad)[0].astype(jnp.bfloat16)
    up_part = product_tn(mlp_in, hidden_grad)
    up_bias_part = jnp.sum(hidden_grad.astype(jnp.float32), axis=0)
    mlp_back = lax.psum(product_nt(hidden_grad, w_up).astype(jnp.bfloat16), "tp").astype(
        jnp.float32
    )
    ln2_pull = jax.vjp(layer_norm, after_attn, ln2_gain, ln2_bias)[1]
    norm_grad, ln2_gain_part, ln2_bias_part = ln2_pull(mlp_back)
    attn_out_grad = mlp_out_grad + norm_grad
    attn_out_low = attn_out_grad.astype(jnp.bfloat16)
    o_part = product_tn(attended_low, attn_out_low)
    o_bias_part = jnp.sum(attn_out_low.astype(jnp.float32), axis=0)
    attended_grad = product_nt(attn_out_low, w_out).astype(jnp.bfloat16)
    grad_heads = split_heads(attended_grad, local_heads)

    def head_backward(operands):
        query_one, key_one, value_one, grad_one, lse_one = operands
        scores = jnp.where(allowed, product_nt(query_one, key_one) * scaling, -1e30)
        probability = jnp.exp(scores - lse_one[:, None])
        dprob = product_nt(grad_one, value_one)
        row_inner = jnp.sum(probability * dprob, axis=1, keepdims=True)
        score_low = (probability * (dprob - row_inner)).astype(jnp.bfloat16)
        query_one_grad = product(score_low, key_one) * scaling
        key_one_grad = product_tn(score_low, query_one) * scaling
        value_one_grad = product_tn(probability.astype(jnp.bfloat16), grad_one)
        return (query_one_grad, key_one_grad, value_one_grad)

    query_hgrad, key_hgrad, value_hgrad = lax.map(
        head_backward, (query_heads, key_heads, value_heads, grad_heads, head_lse)
    )
    key_blocks = join_heads(key_hgrad).reshape(2 * reach_blocks + 1, tok_rows, -1)
    value_blocks = join_heads(value_hgrad).reshape(2 * reach_blocks + 1, tok_rows, -1)
    key_total = key_blocks[reach_blocks]
    value_total = value_blocks[reach_blocks]
    carry_upper = (key_blocks[2 * reach_blocks], value_blocks[2 * reach_blocks])
    carry_lower = (key_blocks[0], value_blocks[0])
    for distance in range(reach_blocks - 1, 0, -1):
        moved_upper = returned(carry_upper[0], carry_upper[1], 1)
        carry_upper = (
            moved_upper[0] + key_blocks[reach_blocks + distance],
            moved_upper[1] + value_blocks[reach_blocks + distance],
        )
        moved_lower = returned(carry_lower[0], carry_lower[1], -1)
        carry_lower = (
            moved_lower[0] + key_blocks[reach_blocks - distance],
            moved_lower[1] + value_blocks[reach_blocks - distance],
        )
    moved_upper = returned(carry_upper[0], carry_upper[1], 1)
    moved_lower = returned(carry_lower[0], carry_lower[1], -1)
    key_total = key_total + moved_upper[0] + moved_lower[0]
    value_total = value_total + moved_upper[1] + moved_lower[1]
    queries_grad = join_heads(query_hgrad).astype(jnp.bfloat16)
    keys_grad = key_total.astype(jnp.bfloat16)
    values_grad = value_total.astype(jnp.bfloat16)
    q_part = product_tn(normed_in, queries_grad)
    k_part = product_tn(normed_in, keys_grad)
    v_part = product_tn(normed_in, values_grad)
    q_bias_part = jnp.sum(queries_grad.astype(jnp.float32), axis=0)
    v_bias_part = jnp.sum(values_grad.astype(jnp.float32), axis=0)
    attn_back = lax.psum(
        (
            product_nt(queries_grad, w_query)
            + product_nt(keys_grad, w_key)
            + product_nt(values_grad, w_value)
        ).astype(jnp.bfloat16),
        "tp",
    ).astype(jnp.float32)
    ln1_pull = jax.vjp(layer_norm, input_f32, ln1_gain, ln1_bias)[1]
    in_grad, ln1_gain_part, ln1_bias_part = ln1_pull(attn_back)
    patches_grad = (attn_out_grad + in_grad).astype(jnp.bfloat16)
    weight_sums = (
        lax.psum_scatter(q_part, "seq", scatter_dimension=0, tiled=True),
        lax.psum_scatter(k_part, "seq", scatter_dimension=0, tiled=True),
        lax.psum_scatter(v_part, "seq", scatter_dimension=0, tiled=True),
        lax.psum_scatter(o_part, "seq", scatter_dimension=1, tiled=True),
        lax.psum_scatter(up_part, "seq", scatter_dimension=0, tiled=True),
        lax.psum_scatter(down_part, "seq", scatter_dimension=1, tiled=True),
        lax.psum_scatter(gate_proj_part, "seq", scatter_dimension=0, tiled=True),
        lax.psum_scatter(up_proj_part, "seq", scatter_dimension=0, tiled=True),
        lax.psum_scatter(down_proj_part, "seq", scatter_dimension=1, tiled=True),
        lax.psum_scatter(rk_part, "seq", scatter_dimension=0, tiled=True),
        lax.psum_scatter(rv_part, "seq", scatter_dimension=0, tiled=True),
    )
    small_sums = lax.psum(
        (
            ln1_gain_part,
            ln1_bias_part,
            q_bias_part,
            v_bias_part,
            o_bias_part,
            ln2_gain_part,
            ln2_bias_part,
            up_bias_part,
            down_bias_part,
            ctx_gain_part,
        ),
        "seq",
    )
    return (
        features,
        latents_out,
        patches_grad,
        latents_grad,
        small_sums[0],
        small_sums[1],
        weight_sums[0],
        small_sums[2],
        weight_sums[1],
        weight_sums[2],
        small_sums[3],
        weight_sums[3],
        small_sums[4],
        small_sums[5],
        small_sums[6],
        weight_sums[4],
        small_sums[7],
        weight_sums[5],
        small_sums[8],
        weight_sums[6],
        weight_sums[7],
        weight_sums[8],
        small_sums[9],
        weight_sums[9],
        weight_sums[10],
        lat_gain_grad,
        rq_weight_grad,
        ro_weight_grad,
    )


MESH = pl.DeviceIdType.MESH


def greet(partners):
    barrier = pltpu.get_barrier_semaphore()
    for present, device in partners:

        @pl.when(present)
        def _():
            pl.semaphore_signal(
                barrier, inc=1, device_id={"seq": device}, device_id_type=MESH
            )

    pl.semaphore_wait(barrier, sum(jnp.where(present, 1, 0) for present, _ in partners))


def place():
    me = lax.axis_index("seq")
    x, y, z = lax.rem(me, 2), lax.rem(lax.div(me, 2), 2), lax.div(me, 4)
    first = lax.axis_index("tp") == 0
    a, b = jnp.where(first, x, y), jnp.where(first, y, x)
    step_a, step_b = jnp.where(first, 1, 2), jnp.where(first, 2, 1)
    return me, z, a, b, step_a, step_b


def neighbours(layers):
    me, z, a, b, step_a, step_b = place()
    up, down = z < layers - 1, z > 0
    return (
        (up, jnp.where(up, me + 4, me)),
        (down, jnp.where(down, me - 4, me)),
        (me >= 0, me + step_a * (1 - 2 * a)),
        (me >= 0, me + step_b * (1 - 2 * b)),
    )


class Arrivals:
    def __init__(self, n, x_ref, slots, sent, landed, local):
        self.n, self.layers = n, n // 4
        self.x_ref, self.slots, self.sent, self.landed = x_ref, slots, sent, landed
        self.me, self.z, self.a, self.b, self.step_a, self.step_b = place()
        self.partners = neighbours(self.layers)
        (self.up, self.to_up), (self.down, self.to_down) = self.partners[:2]
        self.to_a, self.to_b = self.partners[2][1], self.partners[3][1]
        self.own = pltpu.make_async_copy(x_ref, slots.at[self.me], local)

    def at(self, layer, of_a, of_b):
        return layer * 4 + of_a * self.step_a + of_b * self.step_b

    def send(self, slot, device, way, source=None):
        return pltpu.make_async_remote_copy(
            src_ref=self.slots.at[slot] if source is None else source,
            dst_ref=self.slots.at[slot],
            send_sem=self.sent.at[way, slot],
            recv_sem=self.landed.at[slot],
            device_id={"seq": device},
            device_id_type=MESH,
        )

    def layer(self, k):
        z, last = self.z, self.layers - 1
        both = 2 * jnp.minimum(z, last - z)
        step = (k + 1) // 2
        near = jnp.where(k % 2 == 1, z - step, z + step)
        far = jnp.where(z < last - z, k, last - k)
        return jnp.where(k <= both, near, far)

    def block(self, i):
        last = 2 * self.layers - 1
        over_b = i // (2 * self.layers)
        j = i - over_b * 2 * self.layers
        over_a = jnp.where((j > 0) & ((j % 2 == 0) | (j == last)), 1, 0)
        nearness = jnp.where(over_a == 1, jnp.maximum(j - 1, 0) // 2, (j + 1) // 2)
        layer = self.layer(nearness)
        of_a = jnp.where(over_a == 1, 1 - self.a, self.a)
        of_b = jnp.where(over_b == 1, 1 - self.b, self.b)
        return layer, over_a, over_b, self.at(layer, of_a, of_b)

    def start(self, beside=None):
        if beside is None:
            greet(self.partners)
        else:
            beside.greet()
        self.own.start()
        me, x_ref = self.me, self.x_ref

        @pl.when(self.up)
        def _():
            self.send(me, self.to_up, 0, x_ref).start()

        @pl.when(self.down)
        def _():
            self.send(me, self.to_down, 1, x_ref).start()

        self.send(me, self.to_b, 3, x_ref).start()
        self.send(me, self.to_a, 2, x_ref).start()
        self.own.wait()

    def take(self, i):
        layer, over_a, over_b, slot = self.block(i)

        @pl.when(i > 0)
        def _():
            self.send(slot, self.to_b, 3).wait_recv()

        @pl.when((i > 0) & (over_b == 0))
        def _():
            @pl.when(over_a == 0)
            def _():
                @pl.when((layer < self.z) & self.up)
                def _():
                    self.send(slot, self.to_up, 0).start()

                @pl.when((layer > self.z) & self.down)
                def _():
                    self.send(slot, self.to_down, 1).start()

                self.send(slot, self.to_a, 2).start()

            self.send(slot, self.to_b, 3).start()

        return slot

    def drain(self):
        def body(layer, _):
            slot = self.at(layer, self.a, self.b)
            self.send(slot, self.to_a, 2).wait_send()
            self.send(slot, self.to_b, 3).wait_send()
            self.send(self.at(layer, 1 - self.a, self.b), self.to_b, 3).wait_send()

            @pl.when((layer <= self.z) & self.up)
            def _():
                self.send(slot, self.to_up, 0).wait_send()

            @pl.when((layer >= self.z) & self.down)
            def _():
                self.send(slot, self.to_down, 1).wait_send()

            return 0

        lax.fori_loop(0, self.layers, body, 0)


def gather_semaphores(n):
    return [
        pltpu.SemaphoreType.DMA((4, n)),
        pltpu.SemaphoreType.DMA((n,)),
        pltpu.SemaphoreType.DMA(()),
    ]


def gather_kernel(n, x_ref, o_ref, *semaphores):
    arrivals = Arrivals(n, x_ref, o_ref, *semaphores)
    arrivals.start()

    def body(i, _):
        arrivals.take(i)
        return 0

    lax.fori_loop(0, n, body, 0)
    arrivals.drain()


def gathered_blocks(x, collective_id):
    n = lax.axis_size("seq")
    return pl.pallas_call(
        functools.partial(gather_kernel, n),
        out_shape=jax.ShapeDtypeStruct((n,) + x.shape, x.dtype),
        in_specs=[pl.BlockSpec(memory_space=pl.ANY)],
        out_specs=pl.BlockSpec(memory_space=pl.ANY),
        scratch_shapes=gather_semaphores(n),
        compiler_params=pltpu.CompilerParams(
            collective_id=collective_id, has_side_effects=True
        ),
    )(x)


def gather_beside_kernel(n, x_ref, y_ref, o_ref, y_out, sent, landed, local, *semaphores):
    beside = Beside(n, 1, ((y_ref, y_out),), sent, landed, local)
    arrivals = Arrivals(n, x_ref, o_ref, *semaphores)
    arrivals.start(beside)

    def body(i, _):
        arrivals.take(i)
        beside.start(i)
        return 0

    lax.fori_loop(0, n, body, 0)
    beside.finish()
    arrivals.drain()


def gathered_beside(x, y, collective_id):
    n = lax.axis_size("seq")
    anywhere = pl.BlockSpec(memory_space=pl.ANY)
    return pl.pallas_call(
        functools.partial(gather_beside_kernel, n),
        out_shape=[
            jax.ShapeDtypeStruct((n,) + x.shape, x.dtype),
            jax.ShapeDtypeStruct(y.shape, y.dtype),
        ],
        in_specs=[anywhere] * 2,
        out_specs=[anywhere] * 2,
        scratch_shapes=[pltpu.SemaphoreType.DMA((1, n))] * 2
        + [pltpu.SemaphoreType.DMA((1,))]
        + gather_semaphores(n),
        compiler_params=pltpu.CompilerParams(
            collective_id=collective_id, has_side_effects=True
        ),
    )(x, y)


def pair_rows(pair):
    return pair.reshape(pair.shape[0] * pair.shape[1], pair.shape[2])


def units_kernel(
    n,
    x_ref,
    w_gate_ref,
    w_up_ref,
    slots,
    gate_ref,
    up_ref,
    hidden_ref,
    x_buf,
    gate_buf,
    up_buf,
    hidden_buf,
    load_sem,
    store_sem,
    *semaphores,
):
    arrivals = Arrivals(n, x_ref, slots, *semaphores)
    arrivals.start()
    kept = ((gate_ref, gate_buf), (up_ref, up_buf), (hidden_ref, hidden_buf))

    def stores(pair):
        buf = pair % 2
        return [
            pltpu.make_async_copy(
                held.at[buf, i], out.at[arrivals.block(2 * pair + i)[3]], store_sem.at[buf, i, j]
            )
            for i in range(2)
            for j, (out, held) in enumerate(kept)
        ]

    def body(pair, _):
        buf = pair % 2
        loads = [
            pltpu.make_async_copy(
                slots.at[arrivals.take(2 * pair + i)], x_buf.at[i], load_sem.at[i]
            )
            for i in range(2)
        ]
        for load in loads:
            load.start()
        for load in loads:
            load.wait()

        @pl.when(pair >= 2)
        def _():
            for store in stores(pair - 2):
                store.wait()

        x = pair_rows(x_buf[...])
        shape = gate_buf.shape[1:]
        gate = product(x, w_gate_ref[...])
        up = product(x, w_up_ref[...])
        gate_buf[buf] = gate.reshape(shape)
        up_buf[buf] = up.reshape(shape)
        hidden_buf[buf] = (gate * jax.nn.sigmoid(gate) * up).astype(jnp.bfloat16).reshape(shape)
        for store in stores(pair):
            store.start()
        return 0

    lax.fori_loop(0, n // 2, body, 0)
    for pair in (n // 2 - 2, n // 2 - 1):
        for store in stores(pair):
            store.wait()
    arrivals.drain()


def gathered_units(x, w_gate, w_up, collective_id):
    n = lax.axis_size("seq")
    rows, units = x.shape[0], w_gate.shape[1]
    exact = jax.ShapeDtypeStruct((n, rows, units), jnp.float32)
    low = jax.ShapeDtypeStruct((n, rows, units), jnp.bfloat16)
    anywhere = pl.BlockSpec(memory_space=pl.ANY)
    return pl.pallas_call(
        functools.partial(units_kernel, n),
        out_shape=[jax.ShapeDtypeStruct((n,) + x.shape, x.dtype), exact, exact, low],
        in_specs=[anywhere] + [pl.BlockSpec(memory_space=pltpu.VMEM)] * 2,
        out_specs=[anywhere] * 4,
        scratch_shapes=[
            pltpu.VMEM((2,) + x.shape, x.dtype),
            pltpu.VMEM((2, 2, rows, units), jnp.float32),
            pltpu.VMEM((2, 2, rows, units), jnp.float32),
            pltpu.VMEM((2, 2, rows, units), jnp.bfloat16),
            pltpu.SemaphoreType.DMA((2,)),
            pltpu.SemaphoreType.DMA((2, 2, 3)),
        ]
        + gather_semaphores(n),
        compiler_params=pltpu.CompilerParams(
            collective_id=collective_id, has_side_effects=True, vmem_limit_bytes=60 * 2**20
        ),
    )(x, w_gate, w_up)


def units_back_kernel(
    n,
    x_ref,
    w_gate_ref,
    w_up_ref,
    w_down_ref,
    features_ref,
    gate_ref,
    up_ref,
    slots,
    terms_ref,
    dunits_ref,
    ddown_ref,
    x_buf,
    features_buf,
    gate_buf,
    up_buf,
    terms_buf,
    hidden_grad,
    gate_sum,
    up_sum,
    down_sum,
    down_buf,
    units_buf,
    load_sem,
    store_sem,
    down_sem,
    units_sem,
    *semaphores,
):
    arrivals = Arrivals(n, x_ref, slots, *semaphores)
    arrivals.start()
    gate_sum[...] = jnp.zeros_like(gate_sum)
    up_sum[...] = jnp.zeros_like(up_sum)
    down_sum[...] = jnp.zeros_like(down_sum)
    out_width = w_down_ref.shape[1]
    tile = 1024
    chunks, chunk = terms_ref.shape[0], terms_ref.shape[3]

    def stores(pair):
        return [
            pltpu.make_async_copy(
                terms_buf.at[i, :, pl.ds(c * chunk, chunk)],
                terms_ref.at[c, arrivals.block(2 * pair + i)[3]],
                store_sem.at[i, c],
            )
            for i in range(2)
            for c in range(chunks)
        ]

    def loads(pair):
        return [
            pltpu.make_async_copy(
                source.at[arrivals.block(2 * pair + i)[3]],
                held.at[pair % 2, i] if j < 2 else held.at[i],
                load_sem.at[pair % 2, i, j],
            )
            for i in range(2)
            for j, (source, held) in enumerate(
                ((slots, x_buf), (features_ref, features_buf), (gate_ref, gate_buf), (up_ref, up_buf))
            )
        ]

    def take_pair(pair):
        arrivals.take(2 * pair)
        arrivals.take(2 * pair + 1)
        for load in loads(pair):
            load.start()

    take_pair(0)

    def body(pair, _):
        buf = pair % 2
        for load in loads(pair):
            load.wait()
        hidden_grad[...] = jnp.zeros_like(hidden_grad)

        def back_tile(t, _):
            columns = pl.ds(pl.multiple_of(t * tile, tile), tile)
            hidden_grad[...] += product_nt(
                pair_rows(x_buf[buf, :, :, columns]), w_down_ref[:, columns]
            )
            return 0

        lax.fori_loop(0, out_width // tile, back_tile, 0)
        gate, up, grad = pair_rows(gate_buf[...]), pair_rows(up_buf[...]), hidden_grad[...]
        share = jax.nn.sigmoid(gate)
        silu = gate * share
        gate_low = (grad * up * (share * (1.0 + gate * (1.0 - share)))).astype(jnp.bfloat16)
        up_low = (grad * silu).astype(jnp.bfloat16)
        hidden_t = (silu * up).astype(jnp.bfloat16).T
        terms = product_nt(gate_low, w_gate_ref[...]) + product_nt(up_low, w_up_ref[...])

        @pl.when(pair >= 1)
        def _():
            for store in stores(pair - 1):
                store.wait()

        terms_buf[...] = terms.astype(jnp.bfloat16).reshape(terms_buf.shape)
        for store in stores(pair):
            store.start()

        @pl.when(pair + 1 < n // 2)
        def _():
            take_pair(pair + 1)

        features_t = pair_rows(features_buf[buf]).T
        for begin in range(0, gate_low.shape[1], 256):
            columns = slice(begin, begin + 256)
            gate_sum[:, columns] += product(features_t, gate_low[:, columns])
            up_sum[:, columns] += product(features_t, up_low[:, columns])

        def down_tile(t, _):
            columns = pl.ds(pl.multiple_of(t * tile, tile), tile)
            down_sum[:, columns] += product(hidden_t, pair_rows(x_buf[buf, :, :, columns]))
            return 0

        lax.fori_loop(0, out_width // tile, down_tile, 0)
        return 0

    lax.fori_loop(0, n // 2, body, 0)
    share = out_width // n

    def down_store(j):
        return pltpu.make_async_copy(
            down_buf.at[j % 2], ddown_ref.at[j], down_sem.at[j % 2]
        )

    def down_out(j, _):
        @pl.when(j >= 2)
        def _():
            down_store(j - 2).wait()

        columns = pl.ds(pl.multiple_of(j * share, share), share)
        down_buf[j % 2] = down_sum[:, columns].astype(jnp.bfloat16)
        down_store(j).start()
        return 0

    lax.fori_loop(0, n, down_out, 0)

    def units_store(j):
        return pltpu.make_async_copy(units_buf.at[j % 2], dunits_ref.at[j], units_sem.at[j % 2])

    def units_out(j, _):
        @pl.when(j >= 2)
        def _():
            units_store(j - 2).wait()

        owned = units_buf.shape[2]
        owner = pl.ds(pl.multiple_of(j * owned, 8), owned)
        for i, total in enumerate((gate_sum, up_sum)):
            units_buf[j % 2, i] = total[owner].astype(jnp.bfloat16)
        units_store(j).start()
        return 0

    lax.fori_loop(0, n, units_out, 0)
    units_store(n - 2).wait()
    units_store(n - 1).wait()
    down_store(n - 2).wait()
    down_store(n - 1).wait()
    for store in stores(n // 2 - 1):
        store.wait()
    arrivals.drain()


def gathered_back(x, w_gate, w_up, w_down, features, gate, up, chunks, collective_id):
    n = lax.axis_size("seq")
    rows, out_width = x.shape
    width, units = w_gate.shape
    low, exact = jnp.bfloat16, jnp.float32
    anywhere = pl.BlockSpec(memory_space=pl.ANY)
    in_vmem = pl.BlockSpec(memory_space=pltpu.VMEM)
    return pl.pallas_call(
        functools.partial(units_back_kernel, n),
        out_shape=[
            jax.ShapeDtypeStruct((n,) + x.shape, low),
            jax.ShapeDtypeStruct((chunks, n, rows, width // chunks), low),
            jax.ShapeDtypeStruct((n, 2, width // n, units), low),
            jax.ShapeDtypeStruct((n, units, out_width // n), low),
        ],
        in_specs=[anywhere] + [in_vmem] * 3 + [anywhere] * 3,
        out_specs=[anywhere] * 4,
        scratch_shapes=[
            pltpu.VMEM((2, 2, rows, out_width), low),
            pltpu.VMEM((2, 2, rows, width), low),
            pltpu.VMEM((2, rows, units), exact),
            pltpu.VMEM((2, rows, units), exact),
            pltpu.VMEM((2, rows, width), low),
            pltpu.VMEM((2 * rows, units), exact),
            pltpu.VMEM((width, units), exact),
            pltpu.VMEM((width, units), exact),
            pltpu.VMEM((units, out_width), exact),
            pltpu.VMEM((2, units, out_width // n), low),
            pltpu.VMEM((2, 2, width // n, units), low),
            pltpu.SemaphoreType.DMA((2, 2, 4)),
            pltpu.SemaphoreType.DMA((2, chunks)),
            pltpu.SemaphoreType.DMA((2,)),
            pltpu.SemaphoreType.DMA((2,)),
        ]
        + gather_semaphores(n),
        compiler_params=pltpu.CompilerParams(
            collective_id=collective_id, has_side_effects=True, vmem_limit_bytes=60 * 2**20
        ),
    )(x, w_gate, w_up, w_down, features, gate, up)


def scatter_kernel(n, chunks, p_ref, o_ref, from_b, from_a, from_down, from_up, *semaphores, fill=None):
    layers = n // 4
    me, z, a, b, step_a, step_b = place()
    partners = neighbours(layers)
    (up, to_up), (down, to_down), (_, to_a), (_, to_b) = partners
    b_sent, b_landed, a_sent, a_landed, u_sent, u_landed, d_sent, d_landed = semaphores
    greet(partners)

    def at(layer, of_a, of_b):
        return layer * 4 + of_a * step_a + of_b * step_b

    def copy(source, target, sent, landed, device):
        return pltpu.make_async_remote_copy(
            src_ref=source,
            dst_ref=target,
            send_sem=sent,
            recv_sem=landed,
            device_id={"seq": device},
            device_id_type=MESH,
        )

    def over_b(c, of_a, layer):
        return copy(
            p_ref.at[c, at(layer, of_a, 1 - b)],
            from_b.at[c, of_a, layer],
            b_sent.at[c, of_a, layer],
            b_landed.at[c, of_a, layer],
            to_b,
        )

    def over_a(c, layer):
        return copy(
            p_ref.at[c, at(layer, 1 - a, b)],
            from_a.at[c, layer],
            a_sent.at[c, layer],
            a_landed.at[c, layer],
            to_a,
        )

    def upward(c, layer):
        return copy(
            p_ref.at[c, at(layer, a, b)],
            from_down.at[c, layer],
            u_sent.at[c, layer],
            u_landed.at[c, layer],
            to_up,
        )

    def downward(c, layer):
        return copy(
            p_ref.at[c, at(layer, a, b)],
            from_up.at[c, layer],
            d_sent.at[c, layer],
            d_landed.at[c, layer],
            to_down,
        )

    def each_layer(body):
        lax.fori_loop(0, layers, lambda layer, _: (body(layer), 0)[1], 0)

    def send_b(c):
        each_layer(lambda layer: over_b(c, 1 - a, layer).start())
        each_layer(lambda layer: over_b(c, a, layer).start())

    def send_a(c):
        def body(layer):
            over_b(c, 1 - a, layer).wait_recv()
            slot = at(layer, 1 - a, b)
            p_ref[c, slot] = p_ref[c, slot] + from_b[c, 1 - a, layer]
            over_a(c, layer).start()

        each_layer(body)

    def join_line(c):
        def body(layer):
            over_b(c, a, layer).wait_recv()
            over_a(c, layer).wait_recv()
            slot = at(layer, a, b)
            p_ref[c, slot] = p_ref[c, slot] + from_b[c, a, layer] + from_a[c, layer]

            @pl.when((layer > z) & (z == 0))
            def _():
                upward(c, layer).start()

            @pl.when((layer < z) & (z == layers - 1))
            def _():
                downward(c, layer).start()

        each_layer(body)

    def pass_up(c):
        def body(layer):
            @pl.when(layer > z)
            def _():
                upward(c, layer).wait_recv()
                slot = at(layer, a, b)
                p_ref[c, slot] = p_ref[c, slot] + from_down[c, layer]
                upward(c, layer).start()

        each_layer(body)

    def pass_down(c):
        def body(layer):
            @pl.when(layer < z)
            def _():
                downward(c, layer).wait_recv()
                slot = at(layer, a, b)
                p_ref[c, slot] = p_ref[c, slot] + from_up[c, layer]
                downward(c, layer).start()

        each_layer(body)

    def finish(c):
        @pl.when(down)
        def _():
            upward(c, z).wait_recv()
            p_ref[c, me] = p_ref[c, me] + from_down[c, z]

        @pl.when(up)
        def _():
            downward(c, z).wait_recv()
            p_ref[c, me] = p_ref[c, me] + from_up[c, z]

        o_ref[c] = p_ref[c, me]

    def when_chunk(step, stage):
        @pl.when((step >= 0) & (step < chunks))
        def _():
            stage(jnp.clip(step, 0, chunks - 1))

    def fill_and_send(c):
        if fill is not None:
            fill(c)
        send_b(c)

    fill_and_send(0)

    def step(t, _):
        when_chunk(t + 1, fill_and_send)
        when_chunk(t, send_a)
        when_chunk(t - 1, join_line)
        inner = (z > 0) & (z < layers - 1)

        @pl.when(inner)
        def _():
            when_chunk(t - 1 - z, pass_up)
            when_chunk(t - layers + z, pass_down)

        when_chunk(t - layers, finish)
        return 0

    lax.fori_loop(0, chunks + layers, step, 0)

    def drain(c, _):
        def body(layer):
            over_b(c, 0, layer).wait_send()
            over_b(c, 1, layer).wait_send()
            over_a(c, layer).wait_send()

            @pl.when(layer > z)
            def _():
                upward(c, layer).wait_send()

            @pl.when(layer < z)
            def _():
                downward(c, layer).wait_send()

        each_layer(body)
        return 0

    lax.fori_loop(0, chunks, drain, 0)


def scatter_scratch(chunks, n, block, dtype):
    layers = n // 4

    def slots(*count):
        return pltpu.VMEM((chunks,) + count + block, dtype)

    def semaphores(*count):
        return pltpu.SemaphoreType.DMA((chunks,) + count)

    return (
        [slots(2, layers)]
        + [slots(layers)] * 3
        + [semaphores(2, layers)] * 2
        + [semaphores(layers)] * 6
    )


def scattered_sum(terms, collective_id):
    chunks, n = terms.shape[:2]
    block = terms.shape[2:]
    return pl.pallas_call(
        functools.partial(scatter_kernel, n, chunks),
        out_shape=jax.ShapeDtypeStruct((chunks,) + block, terms.dtype),
        in_specs=[pl.BlockSpec(memory_space=pltpu.VMEM)],
        out_specs=pl.BlockSpec(memory_space=pltpu.VMEM),
        scratch_shapes=scatter_scratch(chunks, n, block, terms.dtype),
        compiler_params=pltpu.CompilerParams(
            collective_id=collective_id, has_side_effects=True, vmem_limit_bytes=60 * 2**20
        ),
    )(terms)


def down_kernel(n, chunks, hidden_ref, w_down_ref, o_ref, p_ref, *scratch):
    cols = w_down_ref.shape[1] // chunks

    def fill(c):
        columns = pl.ds(pl.multiple_of(c * cols, cols), cols)

        def body(pair, _):
            owners = pl.ds(2 * pair, 2)
            terms = product(pair_rows(hidden_ref[owners]), w_down_ref[:, columns])
            p_ref[c, owners] = terms.astype(p_ref.dtype).reshape(2, -1, cols)
            return 0

        lax.fori_loop(0, n // 2, body, 0)

    scatter_kernel(n, chunks, p_ref, o_ref, *scratch, fill=fill)


def scattered_down(hidden, w_down, chunks, collective_id):
    n, rows = hidden.shape[:2]
    block = (rows, w_down.shape[1] // chunks)
    return pl.pallas_call(
        functools.partial(down_kernel, n, chunks),
        out_shape=jax.ShapeDtypeStruct((chunks,) + block, hidden.dtype),
        in_specs=[pl.BlockSpec(memory_space=pltpu.VMEM)] * 2,
        out_specs=pl.BlockSpec(memory_space=pltpu.VMEM),
        scratch_shapes=[pltpu.VMEM((chunks, n) + block, hidden.dtype)]
        + scatter_scratch(chunks, n, block, hidden.dtype),
        compiler_params=pltpu.CompilerParams(
            collective_id=collective_id, has_side_effects=True, vmem_limit_bytes=60 * 2**20
        ),
    )(hidden, w_down)


class Beside:
    def __init__(self, n, per_step, pairs, sent, landed, local):
        self.n, self.per_step, self.pairs = n, per_step, pairs
        self.sent, self.landed = sent, landed
        self.me = lax.axis_index("seq")
        self.own = [
            pltpu.make_async_copy(source.at[self.me], target.at[self.me], local.at[j])
            for j, (source, target) in enumerate(pairs)
        ]

    def greet(self):
        barrier = pltpu.get_barrier_semaphore()
        for step in range(1, self.n):
            pl.semaphore_signal(
                barrier,
                inc=1,
                device_id={"seq": lax.rem(self.me + step, self.n)},
                device_id_type=MESH,
            )
        pl.semaphore_wait(barrier, self.n - 1)
        for own in self.own:
            own.start()

    def copies(self, step):
        other = lax.rem(self.me + step, self.n)
        return [
            pltpu.make_async_remote_copy(
                src_ref=source.at[other],
                dst_ref=target.at[self.me],
                send_sem=self.sent.at[j, step],
                recv_sem=self.landed.at[j, step],
                device_id={"seq": other},
                device_id_type=MESH,
            )
            for j, (source, target) in enumerate(self.pairs)
        ]

    def start(self, t):
        for i in range(self.per_step):
            step = t * self.per_step + i + 1

            @pl.when(step < self.n)
            def _():
                for copy in self.copies(jnp.minimum(step, self.n - 1)):
                    copy.start()

    def finish(self):
        def body(step, _):
            for copy in self.copies(step):
                copy.wait()
            return 0

        lax.fori_loop(1, self.n, body, 0)
        for own in self.own:
            own.wait()


def vision_kernel(n, chunks, spans, left_ref, right_ref, o_ref, p_ref, *scratch):
    cols = right_ref.shape[1] // chunks
    shard = left_ref.shape[1] // n

    def fill(c):
        def body(t, _):
            tile = c * (cols // 128) + t
            source = sum(jnp.where(tile >= span, 1, 0) for span in spans[1:])
            columns = pl.ds(pl.multiple_of(tile * 128, 128), 128)
            terms = product(left_ref[source], right_ref[:, columns])
            p_ref[c, :, :, pl.ds(pl.multiple_of(t * 128, 128), 128)] = terms.reshape(
                n, shard, 128
            ).astype(p_ref.dtype)
            return 0

        lax.fori_loop(0, cols // 128, body, 0)

    scatter_kernel(n, chunks, p_ref, o_ref, *scratch, fill=fill)


def scattered_vision(left, right, spans, chunks, collective_id):
    n = lax.axis_size("seq")
    block = (left.shape[1] // n, right.shape[1] // chunks)
    return pl.pallas_call(
        functools.partial(vision_kernel, n, chunks, spans),
        out_shape=jax.ShapeDtypeStruct((chunks,) + block, left.dtype),
        in_specs=[pl.BlockSpec(memory_space=pltpu.VMEM)] * 2,
        out_specs=pl.BlockSpec(memory_space=pltpu.VMEM),
        scratch_shapes=[pltpu.VMEM((chunks, n) + block, left.dtype)]
        + scatter_scratch(chunks, n, block, left.dtype),
        compiler_params=pltpu.CompilerParams(
            collective_id=collective_id, has_side_effects=True, vmem_limit_bytes=60 * 2**20
        ),
    )(left, right)


def exchange_kernel(n, groups, *refs):
    count = len(groups)
    sources, targets = refs[:count], refs[count : 2 * count]
    sent, landed, local = refs[2 * count :]
    me = lax.axis_index("seq")
    barrier = pltpu.get_barrier_semaphore()
    for step in range(1, n):
        pl.semaphore_signal(
            barrier, inc=1, device_id={"seq": lax.rem(me + step, n)}, device_id_type=MESH
        )
    pl.semaphore_wait(barrier, n - 1)
    copies = []
    for j, group in enumerate(groups):
        base = lax.div(me, group) * group
        mine = me - base
        copies.append(
            pltpu.make_async_copy(sources[j].at[mine], targets[j].at[mine], local.at[j])
        )
        copies[-1].start()
        for step in range(1, group):
            other = lax.rem(mine + step, group)
            copies.append(
                pltpu.make_async_remote_copy(
                    src_ref=sources[j].at[other],
                    dst_ref=targets[j].at[mine],
                    send_sem=sent.at[j, step],
                    recv_sem=landed.at[j, step],
                    device_id={"seq": base + other},
                    device_id_type=MESH,
                )
            )
            copies[-1].start()
    for copy in copies:
        copy.wait()


def exchanged(arrays, collective_id):
    n = lax.axis_size("seq")
    count = len(arrays)
    groups = tuple(x.shape[0] for x in arrays)
    return pl.pallas_call(
        functools.partial(exchange_kernel, n, groups),
        out_shape=[jax.ShapeDtypeStruct(x.shape, x.dtype) for x in arrays],
        in_specs=[pl.BlockSpec(memory_space=pl.ANY)] * count,
        out_specs=[pl.BlockSpec(memory_space=pl.ANY)] * count,
        scratch_shapes=[pltpu.SemaphoreType.DMA((count, n))] * 2
        + [pltpu.SemaphoreType.DMA((count,))],
        compiler_params=pltpu.CompilerParams(
            collective_id=collective_id, has_side_effects=True
        ),
    )(*arrays)


def reduce_kernel(n, combine, x_ref, o_ref, shares, total, sent, landed, sent_on, landed_on):
    me = lax.axis_index("seq")
    barrier = pltpu.get_barrier_semaphore()
    others = [lax.rem(me + step, n) for step in range(1, n)]
    for other in others:
        pl.semaphore_signal(barrier, inc=1, device_id={"seq": other}, device_id_type=MESH)
    pl.semaphore_wait(barrier, n - 1)

    def copy(step, source, target, sent, landed):
        return pltpu.make_async_remote_copy(
            src_ref=source,
            dst_ref=target,
            send_sem=sent.at[step],
            recv_sem=landed.at[step],
            device_id={"seq": others[step - 1]},
            device_id_type=MESH,
        )

    there = [copy(i, x_ref.at[others[i - 1]], shares.at[me], sent, landed) for i in range(1, n)]
    for move in there:
        move.start()
    shares[me] = x_ref[me]
    for move in there:
        move.wait()
    total[...] = combine(shares[...])
    back = [copy(i, total, o_ref.at[me], sent_on, landed_on) for i in range(1, n)]
    for move in back:
        move.start()
    o_ref[me] = total[...]
    for move in back:
        move.wait()


def reduced(x, combine, collective_id):
    n = x.shape[0]
    return pl.pallas_call(
        functools.partial(reduce_kernel, n, combine),
        out_shape=jax.ShapeDtypeStruct(x.shape, x.dtype),
        in_specs=[pl.BlockSpec(memory_space=pltpu.VMEM)],
        out_specs=pl.BlockSpec(memory_space=pltpu.VMEM),
        scratch_shapes=[pltpu.VMEM(x.shape, x.dtype), pltpu.VMEM(x.shape[1:], x.dtype)]
        + [pltpu.SemaphoreType.DMA((n,))] * 4,
        compiler_params=pltpu.CompilerParams(
            collective_id=collective_id, has_side_effects=True
        ),
    )(x)


def added(shares):
    return jnp.sum(shares, axis=0)


def softmax_shares(shares):
    column = lax.broadcasted_iota(jnp.int32, shares.shape, 2)
    at_peak = column == RHD
    peak = jnp.max(jnp.where(at_peak, shares, -jnp.inf), axis=2, keepdims=True)
    top = jnp.max(peak, axis=0, keepdims=True)
    sums = jnp.sum(shares * jnp.exp(peak - top), axis=0)
    return jnp.where(at_peak[0], top[0], sums)


def swapped(value):
    return lax.ppermute(value, "tp", [(0, 1), (1, 0)])


def rounded(value):
    return lax.reduce_precision(value, 8, 7)


def paired(value):
    kept = rounded(value)
    return kept + swapped(kept.astype(jnp.bfloat16)).astype(jnp.float32)


def in_order(mine, other, axis):
    first = lax.axis_index("tp") == 0
    return jnp.concatenate(
        [jnp.where(first, mine, other), jnp.where(first, other, mine)], axis=axis
    )


def attend_kernel(scaling, q_ref, k_ref, v_ref, qid_ref, kid_ref, o_ref, lse_ref):
    scores = product_nt(q_ref[...], k_ref[...]) * scaling
    scores = jnp.where(qid_ref[...] == kid_ref[...], scores, -1e30)
    peak = jnp.max(scores, axis=1, keepdims=True)
    weights = jnp.exp(scores - peak)
    total = jnp.sum(weights, axis=1, keepdims=True)
    probability = (weights / total).astype(jnp.bfloat16)
    o_ref[...] = product(probability, v_ref[...]).astype(o_ref.dtype)
    lse_ref[...] = peak + jnp.log(total)


def attend_back_kernel(
    scaling, q_ref, k_ref, v_ref, g_ref, qid_ref, kid_ref, lse_ref, dq_ref, dk_ref, dv_ref
):
    @pl.when(pl.program_id(0) == 0)
    def _():
        dk_ref[...] = jnp.zeros_like(dk_ref)
        dv_ref[...] = jnp.zeros_like(dv_ref)

    scores = product_nt(q_ref[...], k_ref[...]) * scaling
    scores = jnp.where(qid_ref[...] == kid_ref[...], scores, -1e30)
    probability = jnp.exp(scores - lse_ref[...])
    dprob = product_nt(g_ref[...], v_ref[...])
    inner = jnp.sum(probability * dprob, axis=1, keepdims=True)
    low = (probability * (dprob - inner)).astype(jnp.bfloat16)
    dq_ref[...] = product(low, k_ref[...]) * scaling
    dk_ref[...] += product_tn(low, q_ref[...]) * scaling
    dv_ref[...] += product_tn(probability.astype(jnp.bfloat16), g_ref[...])


def attention_calls(queries, window, width, tile, scaling):
    tiled = lambda columns: pl.BlockSpec((tile, columns), lambda i: (i, 0))
    whole = lambda rows, columns: pl.BlockSpec((rows, columns), lambda i: (0, 0))
    params = pltpu.CompilerParams(vmem_limit_bytes=56 * 2**20)
    forward = pl.pallas_call(
        functools.partial(attend_kernel, scaling),
        grid=(queries // tile,),
        in_specs=[
            tiled(width),
            whole(window, width),
            whole(window, width),
            tiled(1),
            whole(1, window),
        ],
        out_specs=[tiled(width), tiled(1)],
        out_shape=[
            jax.ShapeDtypeStruct((queries, width), jnp.bfloat16),
            jax.ShapeDtypeStruct((queries, 1), jnp.float32),
        ],
        compiler_params=params,
        cost_estimate=pl.CostEstimate(
            flops=4 * queries * window * width,
            bytes_accessed=2 * (2 * window + 2 * queries) * 128,
            transcendentals=queries * window,
        ),
    )
    backward = pl.pallas_call(
        functools.partial(attend_back_kernel, scaling),
        grid=(queries // tile,),
        in_specs=[
            tiled(width),
            whole(window, width),
            whole(window, width),
            tiled(width),
            tiled(1),
            whole(1, window),
            tiled(1),
        ],
        out_specs=[tiled(width), whole(window, width), whole(window, width)],
        out_shape=[
            jax.ShapeDtypeStruct((queries, width), jnp.float32),
            jax.ShapeDtypeStruct((window, width), jnp.float32),
            jax.ShapeDtypeStruct((window, width), jnp.float32),
        ],
        compiler_params=params,
        cost_estimate=pl.CostEstimate(
            flops=10 * queries * window * width,
            bytes_accessed=2 * (6 * window + 4 * queries) * 128,
            transcendentals=queries * window,
        ),
    )
    return forward, backward


def padded_columns(matrix, width):
    return jnp.pad(matrix, ((0, 0), (0, width - matrix.shape[1])))


def tokens_travel(
    patches,
    lengths,
    ln1_gain,
    ln1_bias,
    q_weight,
    q_bias,
    k_weight,
    v_weight,
    v_bias,
    o_weight,
    o_bias,
    ln2_gain,
    ln2_bias,
    up_weight,
    up_bias,
    down_weight,
    down_bias,
    gate_proj,
    up_proj,
    down_proj,
    ctx_gain,
    rk_weight,
    rv_weight,
    latents,
    lat_gain,
    rq_weight,
    ro_weight,
    feat_grad,
    lat_grad,
):
    low = jnp.bfloat16
    rows, width = patches.shape
    half = rows // 2
    n = lax.axis_size("seq")
    me = lax.axis_index("seq")
    core = lax.axis_index("tp")
    total_rows = rows * n
    longest = min(IMGMAX, (n // 2 - 1) * rows)
    heads = q_bias.shape[0] // HD
    part = me // heads
    queries = total_rows // 2
    window = total_rows - longest
    window_start = part * longest
    query_start = part * (queries - longest)
    scaling = HD ** (-0.5)
    kv_heads = rk_weight.shape[1] // RHD
    q_heads = rq_weight.shape[1] // RHD
    group = q_heads // kv_heads
    lat_rows = latents.shape[0]
    lat_scaling = RHD ** (-0.5)
    first_block = (me == 0).astype(jnp.float32)
    shard = q_weight.shape[0]
    hidden_units = up_bias.shape[0]
    hidden_pad = -(-hidden_units // 128) * 128
    proj_units = gate_proj.shape[1] // n
    own_width = heads * HD
    unit_lanes = -(-proj_units // 128) * 128
    out_width = down_proj.shape[1] * n

    def my_half(value):
        return lax.dynamic_slice_in_dim(value, core * half, half, 0)

    input_f32 = patches.astype(jnp.float32)
    normed_in = layer_norm(input_f32, ln1_gain, ln1_bias).astype(low)
    lanes = -(-HD // 128) * 128

    def wide(heads_of):
        return jnp.pad(heads_of, [(0, 0)] * (heads_of.ndim - 1) + [(0, lanes - HD)])

    def compact(parts):
        joined = jnp.concatenate([p[..., :HD] for p in parts], axis=-1)
        room = -(-joined.shape[-1] // 128) * 128 - joined.shape[-1]
        return jnp.pad(joined, [(0, 0)] * (joined.ndim - 1) + [(0, room)])

    head_shard = compact([split_heads(w, heads) for w in (q_weight, k_weight, v_weight)])
    normed_half, head_weight = gathered_beside(
        my_half(normed_in), jnp.concatenate([head_shard] * 2, axis=0), 2
    )

    unit_weights = jnp.stack([gate_proj, up_proj]).reshape(2, shard, n, proj_units)
    unit_weights = jnp.pad(unit_weights, ((0, 0),) * 3 + ((0, unit_lanes - proj_units),))
    ctx_width = rk_weight.shape[1]
    ctx_shard = jnp.concatenate([rk_weight, rv_weight], axis=1)
    unit_weights, normed_half, head_weight, ctx_shard = lax.optimization_barrier(
        (unit_weights.transpose(2, 0, 1, 3), normed_half, head_weight, ctx_shard)
    )
    w_ctx = lax.all_gather(ctx_shard, "seq", axis=0, tiled=True)
    w_ctxkey, w_ctxval = w_ctx[:, :ctx_width], w_ctx[:, ctx_width:]
    unit_weights = lax.all_to_all(unit_weights, "seq", 0, 0)
    normed_half = lax.dynamic_slice_in_dim(normed_half, window_start // rows, window // rows, 0)
    normed_window = in_order(
        normed_half[:, None], swapped(normed_half)[:, None], 1
    ).reshape(window, width)
    head_weight = head_weight.reshape(width, -1)
    head_weight = jnp.concatenate(
        [wide(head_weight[:, i * HD : (i + 1) * HD]) for i in range(3)], axis=1
    )
    head = me - part * heads
    q_bias_one = lax.dynamic_slice_in_dim(q_bias, head * HD, HD, 0)
    v_bias_one = lax.dynamic_slice_in_dim(v_bias, head * HD, HD, 0)
    bias_one = jnp.concatenate(
        [wide(q_bias_one), jnp.zeros((lanes,), jnp.float32), wide(v_bias_one)]
    )
    qkv = (product(normed_window, head_weight) + bias_one).astype(low)
    query_one = lax.dynamic_slice_in_dim(qkv[:, :lanes], query_start, queries, 0)
    key_one = qkv[:, lanes : 2 * lanes]
    value_one = qkv[:, 2 * lanes :]
    key_ids = image_ids(
        lengths, window_start + jnp.arange(window, dtype=jnp.int32), total_rows
    )
    query_ids = lax.dynamic_slice_in_dim(key_ids, query_start, queries, 0)[:, None]
    key_ids = key_ids[None, :]
    attend, attend_back = attention_calls(queries, window, lanes, rows, scaling)
    attended_one, lse_one = attend(query_one, key_one, value_one, query_ids, key_ids)
    attended_low = join_heads(
        exchanged([attended_one.reshape(heads, rows, lanes)], 3)[0][:, :, :HD]
    )

    vision_shard = jnp.concatenate(
        [
            padded_columns(up_weight, hidden_pad),
            padded_columns(down_weight.T, hidden_pad),
            o_weight.T,
        ],
        axis=1,
    )
    unit_weights, vision_shard, attended_low, down_proj = lax.optimization_barrier(
        (unit_weights, vision_shard, attended_low, down_proj)
    )
    vision, down_mine = gathered_beside(vision_shard, down_proj.reshape(n, proj_units, -1), 17)
    vision = vision.reshape(width, -1)
    down_mine = down_mine.transpose(1, 0, 2).reshape(proj_units, out_width)
    w_up = vision[:, :hidden_units]
    w_down_t = vision[:, hidden_pad : hidden_pad + hidden_units]
    w_out_t = vision[:, 2 * hidden_pad :]
    unit_weights = unit_weights.transpose(1, 0, 2, 3).reshape(2, width, unit_lanes)
    w_gate, w_up_proj = jnp.concatenate([unit_weights, swapped(unit_weights)], axis=2)
    down_mine = jnp.pad(down_mine, ((0, unit_lanes - proj_units), (0, 0)))
    w_down_proj = jnp.concatenate([down_mine, swapped(down_mine)], axis=0)

    attn_part = product_nt(attended_low, w_out_t)
    attn_sum = attn_part + swapped(attn_part)
    after_attn = input_f32 + attn_sum + o_bias
    mlp_in = layer_norm(after_attn, ln2_gain, ln2_bias).astype(low)
    hidden = product(mlp_in, w_up) + up_bias
    active_low = gelu_tanh(hidden).astype(low)
    after_mlp = after_attn + paired(product_nt(active_low, w_down_t)) + down_bias
    features = after_mlp.astype(low)

    features_all, proj_gate, proj_up, proj_hidden = gathered_units(
        my_half(features), w_gate, w_up_proj, 4
    )

    def joined_chunks(sums):
        return sums.transpose(1, 0, 2).reshape(half, -1)

    out_chunks = out_width // 256
    proj_out_low = joined_chunks(scattered_down(proj_hidden, w_down_proj, out_chunks, 5))
    proj_out_half = proj_out_low.astype(jnp.float32)
    proj_out = in_order(proj_out_low, swapped(proj_out_low), 0).astype(jnp.float32)
    qkv_shard, _ = lax.optimization_barrier(
        (jnp.concatenate([q_weight, k_weight, v_weight], axis=1), proj_out_low)
    )
    w_qkv = lax.all_gather(qkv_shard, "seq", axis=0, tiled=True)

    context_low = rms_norm(proj_out, ctx_gain).astype(low)
    ctx_keys = product(context_low, w_ctxkey).astype(low)
    ctx_values = product(context_low, w_ctxval).astype(low)
    lat_normed = rms_norm(latents, lat_gain).astype(low)
    lat_queries = product(lat_normed, rq_weight).astype(low)
    lat_keys = product(lat_normed, w_ctxkey).astype(low)
    lat_values = product(lat_normed, w_ctxval).astype(low)
    query_grouped = lat_queries.reshape(lat_rows, kv_heads, group, RHD)
    key_grouped = ctx_keys.reshape(rows, kv_heads, RHD)
    value_grouped = ctx_values.reshape(rows, kv_heads, RHD)
    self_keys = lat_keys.reshape(lat_rows, kv_heads, RHD)
    self_values = lat_values.reshape(lat_rows, kv_heads, RHD)
    lat_scores = (
        jnp.einsum("lkgd,tkd->kglt", query_grouped, key_grouped, preferred_element_type=jnp.float32)
        * lat_scaling
    )
    self_scores = (
        jnp.einsum("lkgd,tkd->kglt", query_grouped, self_keys, preferred_element_type=jnp.float32)
        * lat_scaling
    )
    stats = partial_stats(lat_scores, value_grouped)
    packed = jnp.concatenate([stats[2], stats[0][..., None], stats[1][..., None]], axis=-1)
    packed = jnp.pad(packed.reshape(n, -1, RHD + 2), ((0, 0), (0, 0), (0, 126 - RHD)))
    merged = reduced(packed, softmax_shares, 6).reshape(kv_heads, group, lat_rows, 128)
    lat_peak, lat_total, lat_numer = joint_stats(
        (merged[..., RHD], merged[..., RHD + 1], merged[..., :RHD]),
        partial_stats(self_scores, self_values),
    )
    lat_lse = lat_peak + jnp.log(lat_total)
    pooled_exact = lat_numer / lat_total[..., None]
    pooled_low = pooled_exact.transpose(2, 0, 1, 3).reshape(lat_rows, -1).astype(low)
    pooled_grad = product_nt(lat_grad, ro_weight).astype(low)
    pooled_grouped = pooled_grad.reshape(lat_rows, kv_heads, group, RHD)
    pooled_f32 = pooled_grouped.astype(jnp.float32)
    lat_delta = jnp.sum(pooled_f32.transpose(1, 2, 0, 3) * pooled_exact, axis=-1)

    def score_grads(scores, key_part, value_part):
        probability = jnp.exp(scores - lat_lse[..., None])
        dprob = jnp.einsum(
            "lkgd,tkd->kglt", pooled_grouped, value_part, preferred_element_type=jnp.float32
        )
        dscore = (probability * (dprob - lat_delta[..., None])).astype(low)
        query_term = (
            jnp.einsum("kglt,tkd->lkgd", dscore, key_part, preferred_element_type=jnp.float32)
            * lat_scaling
        )
        key_term = (
            jnp.einsum("kglt,lkgd->tkd", dscore, query_grouped, preferred_element_type=jnp.float32)
            * lat_scaling
        ).astype(low)
        value_term = jnp.einsum(
            "kglt,lkgd->tkd", probability, pooled_f32, precision=lax.Precision.HIGHEST
        ).astype(low)
        return (
            query_term,
            key_term.reshape(key_part.shape[0], -1),
            value_term.reshape(key_part.shape[0], -1),
        )

    ctx_query_term, ctx_keys_grad, ctx_values_grad = score_grads(
        lat_scores, key_grouped, value_grouped
    )
    self_query_term, self_keys_grad, self_values_grad = score_grads(
        self_scores, self_keys, self_values
    )
    ctx_part = product_nt(ctx_keys_grad, w_ctxkey) + product_nt(ctx_values_grad, w_ctxval)
    ctx_kept = rounded(my_half(ctx_part))
    ctx_sent = lax.dynamic_slice_in_dim(ctx_part, (1 - core) * half, half, 0).astype(low)
    ctx_back = ctx_kept + swapped(ctx_sent).astype(jnp.float32)
    ctx_pull = jax.vjp(rms_norm, proj_out_half, ctx_gain)[1]
    proj_out_grad, ctx_gain_part = ctx_pull(ctx_back)
    _, feat_terms, unit_grads, down_grads = gathered_back(
        proj_out_grad.astype(low),
        w_gate,
        w_up_proj,
        w_down_proj,
        features_all,
        proj_gate,
        proj_up,
        width // 128,
        8,
    )

    query_part = ctx_query_term + first_block * self_query_term
    ctx_grads = jnp.concatenate([ctx_keys_grad, ctx_values_grad], axis=1)
    self_grads = jnp.concatenate([self_keys_grad, self_values_grad], axis=1)
    r_part = product_tn(context_low, ctx_grads) + first_block * product_tn(lat_normed, self_grads)
    r_grad = lax.psum_scatter(r_part.astype(low), "seq", scatter_dimension=0, tiled=True).astype(
        jnp.float32
    )

    feat_half = joined_chunks(scattered_sum(feat_terms, 11))

    proj_in_grad = in_order(feat_half, swapped(feat_half), 0).astype(jnp.float32)
    def core_sum(mine, other):
        return (mine.astype(jnp.float32) + swapped(other).astype(jnp.float32)).astype(low)

    down_blocks = core_sum(
        down_grads[:, :proj_units], down_grads[:, unit_lanes : unit_lanes + proj_units]
    )
    unit_blocks = core_sum(unit_grads[..., :unit_lanes], unit_grads[..., unit_lanes:])
    unit_blocks = unit_blocks.reshape(n, 2 * shard, unit_lanes)

    mlp_out_grad = feat_grad.astype(jnp.float32) + proj_in_grad
    mlp_out_low = mlp_out_grad.astype(low)
    down_bias_part = jnp.sum(mlp_out_low.astype(jnp.float32), axis=0)
    active_grad = product(mlp_out_low, w_down_t)
    gelu_pull = jax.vjp(gelu_tanh, hidden)[1]
    hidden_grad = gelu_pull(active_grad)[0].astype(low)
    up_bias_part = jnp.sum(hidden_grad.astype(jnp.float32), axis=0)
    mlp_back = paired(product_nt(hidden_grad, w_up))
    ln2_pull = jax.vjp(layer_norm, after_attn, ln2_gain, ln2_bias)[1]
    norm_grad, ln2_gain_part, ln2_bias_part = ln2_pull(mlp_back)
    attn_out_grad = mlp_out_grad + norm_grad
    attn_out_low = attn_out_grad.astype(low)
    o_bias_part = jnp.sum(attn_out_low.astype(jnp.float32), axis=0)
    vision_chunks = 13
    vision_width = 2 * hidden_pad + own_width
    vision_cols = -(-vision_width // (vision_chunks * 128)) * 128
    vision_left = jnp.stack([mlp_in.T, mlp_out_low.T, attn_out_low.T])
    vision_right = jnp.concatenate(
        [
            padded_columns(hidden_grad, hidden_pad),
            padded_columns(active_low, hidden_pad),
            padded_columns(attended_low, vision_chunks * vision_cols - 2 * hidden_pad),
        ],
        axis=1,
    )
    spans = (0, hidden_pad // 128, 2 * hidden_pad // 128)
    vision_grad = scattered_vision(vision_left, vision_right, spans, vision_chunks, 18)

    attended_grad = product(attn_out_low, w_out_t).astype(low)
    grad_one = exchanged([wide(split_heads(attended_grad, heads))], 12)[0].reshape(queries, lanes)
    dq, dk, dv = attend_back(
        query_one, key_one, value_one, grad_one, query_ids, key_ids, lse_one
    )
    dq_window = lax.dynamic_update_slice_in_dim(
        jnp.zeros((window, lanes), jnp.float32), dq, query_start, 0
    )
    dqkv = compact([dq_window, dk, dv])
    dqkv_low = dqkv.astype(low)
    head_grad = product_tn(normed_window, dqkv_low).astype(low).reshape(n, shard, -1)
    bias_row = jnp.sum(dqkv_low.astype(jnp.float32), axis=0)
    bias_rows = jnp.zeros((heads, dqkv.shape[1]), jnp.float32)
    bias_rows = lax.dynamic_update_slice_in_dim(bias_rows, bias_row[None], head, 0)
    blocks = dqkv.reshape(window // rows, rows, -1)
    other_block = jnp.where(part == 0, blocks[-1], blocks[0]).astype(low)
    across = lax.ppermute(
        other_block, "seq", [(i, (i + heads) % n) for i in range(n)]
    ).astype(jnp.float32)
    own_blocks = lax.dynamic_slice_in_dim(blocks, part, heads, 0)
    edge = jnp.where(part == 0, heads - 1, 0)
    own_blocks = own_blocks + jnp.where(
        (jnp.arange(heads) == edge)[:, None, None], across[None], 0.0
    )
    head_grads, token_grads = exchanged([head_grad, own_blocks.astype(low)], 13)
    head_grads, token_grads, unit_blocks = lax.optimization_barrier(
        (head_grads, token_grads, unit_blocks)
    )
    unit_rows = lax.all_to_all(unit_blocks, "seq", 0, 0)
    queries_grad, keys_grad, values_grad = (
        join_heads(token_grads[:, :, i * HD : (i + 1) * HD]) for i in range(3)
    )
    attn_back = paired(
        product_nt(jnp.concatenate([queries_grad, keys_grad, values_grad], axis=1), w_qkv)
    )
    ln1_pull = jax.vjp(layer_norm, input_f32, ln1_gain, ln1_bias)[1]
    in_grad, ln1_gain_part, ln1_bias_part = ln1_pull(attn_back)
    patches_grad = (attn_out_grad + in_grad).astype(low)

    smalls = (
        ln1_gain_part,
        ln1_bias_part,
        bias_rows[:, :HD].reshape(-1),
        bias_rows[:, 2 * HD : 3 * HD].reshape(-1),
        o_bias_part,
        ln2_gain_part,
        ln2_bias_part,
        up_bias_part,
        down_bias_part,
        ctx_gain_part,
    )
    joined_smalls = jnp.concatenate(smalls)
    joined_smalls = jnp.concatenate([joined_smalls, query_part.reshape(-1)])
    length = joined_smalls.shape[0]
    per_device = -(-length // (n * 1024)) * 1024
    joined_smalls = jnp.pad(joined_smalls, (0, n * per_device - length))
    small_sum = reduced(joined_smalls.reshape(n, per_device // 128, 128), added, 15).reshape(-1)
    (
        small_sum,
        down_blocks,
        unit_rows,
        vision_grad,
        head_grads,
        pooled_late,
        self_grads,
    ) = lax.optimization_barrier(
        (small_sum, down_blocks, unit_rows, vision_grad, head_grads, pooled_low, self_grads)
    )
    down_rows = lax.all_to_all(down_blocks, "seq", 0, 0)
    vision_grad = vision_grad.transpose(1, 0, 2).reshape(shard, -1).astype(jnp.float32)
    up_weight_grad = vision_grad[:, :hidden_units]
    down_weight_grad = vision_grad[:, hidden_pad : hidden_pad + hidden_units].T
    o_weight_grad = vision_grad[:, 2 * hidden_pad : vision_width].T
    head_grads = head_grads.astype(jnp.float32)
    head_grads = head_grads[:heads] + head_grads[heads:]
    q_weight_grad, k_weight_grad, v_weight_grad = (
        join_heads(head_grads[:, :, i * HD : (i + 1) * HD]) for i in range(3)
    )
    lat_mix = product(pooled_late, ro_weight)
    ro_width = ro_weight.shape[1] // n
    ro_columns = lax.dynamic_slice_in_dim(lat_grad, me * ro_width, ro_width, 1)
    ro_weight_grad = product_tn(pooled_late, ro_columns)
    small_sums, begin = [], 0
    for small in smalls:
        small_sums.append(small_sum[begin : begin + small.shape[0]])
        begin += small.shape[0]
    ctx_gain_grad = small_sums[9] + swapped(small_sums[9])

    query_sum = small_sum[begin : begin + query_part.size].reshape(lat_rows, -1)
    lat_queries_grad = query_sum.astype(low)
    rq_rows = rq_weight.shape[0] // n
    rq_weight_grad = product_tn(
        lax.dynamic_slice_in_dim(lat_normed, me * rq_rows, rq_rows, 1), lat_queries_grad
    )
    lat_part = product_nt(lat_queries_grad, rq_weight) + product_nt(self_grads, w_ctx)
    down_proj_grad = down_rows.reshape(n * proj_units, -1).astype(jnp.float32)
    unit_rows = unit_rows.reshape(n, 2, shard, unit_lanes)[..., :proj_units]
    gate_proj_grad, up_proj_grad = (
        unit_rows.transpose(1, 2, 0, 3).reshape(2, shard, n * proj_units).astype(jnp.float32)
    )
    lat_back, lat_mix_sum = paired(lat_part), paired(lat_mix)
    latents_out = latents + lat_mix_sum
    lat_pull = jax.vjp(rms_norm, latents, lat_gain)[1]
    lat_in_grad, lat_gain_grad = lat_pull(lat_back)
    latents_grad = lat_grad.astype(jnp.float32) + lat_in_grad
    return (
        features,
        latents_out,
        patches_grad,
        latents_grad,
        small_sums[0],
        small_sums[1],
        q_weight_grad,
        small_sums[2],
        k_weight_grad,
        v_weight_grad,
        small_sums[3],
        o_weight_grad,
        small_sums[4],
        small_sums[5],
        small_sums[6],
        up_weight_grad,
        small_sums[7],
        down_weight_grad,
        small_sums[8],
        gate_proj_grad,
        up_proj_grad,
        down_proj_grad,
        ctx_gain_grad,
        r_grad[:, :ctx_width],
        r_grad[:, ctx_width:],
        lat_gain_grad,
        rq_weight_grad,
        ro_weight_grad,
    )


def solution(mesh):
    placed = (
        P("seq", None),
        P(),
        P(),
        P(),
        P("seq", "tp"),
        P("tp"),
        P("seq", "tp"),
        P("seq", "tp"),
        P("tp"),
        P("tp", "seq"),
        P(),
        P(),
        P(),
        P("seq", "tp"),
        P("tp"),
        P("tp", "seq"),
        P(),
        P("seq", "tp"),
        P("seq", "tp"),
        P("tp", "seq"),
        P(),
        P("seq", "tp"),
        P("seq", "tp"),
        P(),
        P(),
        P(None, "tp"),
        P("tp", None),
        P("seq", None),
        P(),
    )
    few = mesh.shape["tp"] == 2 and mesh.shape["seq"] == 16
    return jax.shard_map(
        tokens_travel if few else weights_travel,
        mesh=mesh,
        in_specs=placed,
        out_specs=(
            P("seq", None),
            P(),
            P("seq", None),
            P(),
            P(),
            P(),
            P("seq", "tp"),
            P("tp"),
            P("seq", "tp"),
            P("seq", "tp"),
            P("tp"),
            P("tp", "seq"),
            P(),
            P(),
            P(),
            P("seq", "tp"),
            P("tp"),
            P("tp", "seq"),
            P(),
            P("seq", "tp"),
            P("seq", "tp"),
            P("tp", "seq"),
            P(),
            P("seq", "tp"),
            P("seq", "tp"),
            P(),
            P("seq", "tp"),
            P("tp", "seq"),
        ),
        check_vma=False,
    )
```

```python
import functools

import jax
import jax.experimental.pallas as pl
import jax.experimental.pallas.tpu as pltpu
import jax.numpy as jnp
from jax import lax
from jax.sharding import PartitionSpec as P

HD = 72
RHD = 96
IMGMAX = 4900


EPS = 1e-06


def passed_along(value, axis, steps):
    count = lax.axis_size(axis)
    first, last = (max(0, -steps), min(count, count - steps))
    return lax.ppermute(value, axis, [(source, source + steps) for source in range(first, last)])


def joined(part, axis, combine):
    gathered = jax.tree.map(lambda a: lax.all_gather(a, axis), part)

    def take(source):
        return jax.tree.map(lambda a: lax.dynamic_index_in_dim(a, source, 0, False), gathered)

    return lax.fori_loop(
        1, lax.axis_size(axis), lambda source, state: combine(state, take(source)), take(0)
    )


def layer_norm(value, gain, bias):
    centred = value - jnp.mean(value, axis=-1, keepdims=True)
    return (
        centred * lax.rsqrt(jnp.mean(centred * centred, axis=-1, keepdims=True) + EPS) * gain + bias
    )


def rms_norm(value, gain):
    return value * lax.rsqrt(jnp.mean(value * value, axis=-1, keepdims=True) + EPS) * gain


def gelu_tanh(value):
    return jax.nn.gelu(value, approximate=True)


def product(left, right):
    return jnp.dot(left, right, preferred_element_type=jnp.float32)


def product_nt(left, right):
    return lax.dot_general(
        left, right, (((1,), (1,)), ((), ())), preferred_element_type=jnp.float32
    )


def product_tn(left, right):
    return lax.dot_general(
        left, right, (((0,), (0,)), ((), ())), preferred_element_type=jnp.float32
    )


def image_ids(lengths, positions, total_rows):
    image_ends = jnp.cumsum(lengths)
    counted = jnp.sum((image_ends[None, :] <= positions[:, None]).astype(jnp.int32), axis=1)
    inside = (positions >= 0) & (positions < total_rows)
    return jnp.where(inside, counted, -1)


def split_heads(matrix, count):
    return matrix.reshape(matrix.shape[0], count, -1).transpose(1, 0, 2)


def join_heads(stacked):
    return stacked.transpose(1, 0, 2).reshape(stacked.shape[1], -1)


def neighbour(first, second, offset):
    return passed_along((first, second), "seq", offset)


def returned(first, second, offset):
    return (
        passed_along(first.astype(jnp.bfloat16), "seq", offset).astype(first.dtype),
        passed_along(second.astype(jnp.bfloat16), "seq", offset).astype(second.dtype),
    )


def partial_stats(scores, value_heads):
    peak = jnp.max(scores, axis=-1)
    weights = jnp.exp(scores - peak[..., None])
    total = jnp.sum(weights, axis=-1)
    numer = jnp.einsum(
        "kglt,tkd->kgld", weights, value_heads.astype(jnp.float32), precision=lax.Precision.HIGHEST
    )
    return (peak, total, numer)


def joint_stats(left, right):
    peak = jnp.maximum(left[0], right[0])
    left_scale = jnp.exp(left[0] - peak)
    right_scale = jnp.exp(right[0] - peak)
    total = left[1] * left_scale + right[1] * right_scale
    numer = left[2] * left_scale[..., None] + right[2] * right_scale[..., None]
    return (peak, total, numer)


def weights_travel(
    patches,
    lengths,
    ln1_gain,
    ln1_bias,
    q_weight,
    q_bias,
    k_weight,
    v_weight,
    v_bias,
    o_weight,
    o_bias,
    ln2_gain,
    ln2_bias,
    up_weight,
    up_bias,
    down_weight,
    down_bias,
    gate_proj,
    up_proj,
    down_proj,
    ctx_gain,
    rk_weight,
    rv_weight,
    latents,
    lat_gain,
    rq_weight,
    ro_weight,
    feat_grad,
    lat_grad,
):
    tok_rows = patches.shape[0]
    seq_count = lax.axis_size("seq")
    seq_place = lax.axis_index("seq")
    total_rows = tok_rows * seq_count
    longest = min(IMGMAX, (seq_count // 2 - 1) * tok_rows)
    reach_blocks = (longest + tok_rows - 2) // tok_rows
    local_heads = q_bias.shape[0] // HD
    kv_heads = rk_weight.shape[1] // RHD
    q_heads = rq_weight.shape[1] // RHD
    group = q_heads // kv_heads
    lat_rows = latents.shape[0]
    scaling = HD ** (-0.5)
    lat_scaling = RHD ** (-0.5)
    first_block = (seq_place == 0).astype(jnp.float32)
    gathered = (
        lax.all_gather(q_weight, "seq", axis=0, tiled=True),
        lax.all_gather(k_weight, "seq", axis=0, tiled=True),
        lax.all_gather(v_weight, "seq", axis=0, tiled=True),
        lax.all_gather(o_weight, "seq", axis=1, tiled=True),
        lax.all_gather(up_weight, "seq", axis=0, tiled=True),
        lax.all_gather(down_weight, "seq", axis=1, tiled=True),
        lax.all_gather(gate_proj, "seq", axis=0, tiled=True),
        lax.all_gather(up_proj, "seq", axis=0, tiled=True),
        lax.all_gather(down_proj, "seq", axis=1, tiled=True),
        lax.all_gather(rk_weight, "seq", axis=0, tiled=True),
        lax.all_gather(rv_weight, "seq", axis=0, tiled=True),
    )
    (
        w_query,
        w_key,
        w_value,
        w_out,
        w_up,
        w_down,
        w_gate_proj,
        w_up_proj,
        w_down_proj,
        w_ctxkey,
        w_ctxval,
    ) = gathered
    input_f32 = patches.astype(jnp.float32)
    normed_in = layer_norm(input_f32, ln1_gain, ln1_bias).astype(jnp.bfloat16)
    queries_low = (product(normed_in, w_query) + q_bias).astype(jnp.bfloat16)
    keys_low = product(normed_in, w_key).astype(jnp.bfloat16)
    values_low = (product(normed_in, w_value) + v_bias).astype(jnp.bfloat16)
    upper_pairs = []
    lower_pairs = []
    upper_pair = (keys_low, values_low)
    lower_pair = (keys_low, values_low)
    for distance in range(1, reach_blocks + 1):
        upper_pair = neighbour(upper_pair[0], upper_pair[1], -1)
        lower_pair = neighbour(lower_pair[0], lower_pair[1], 1)
        upper_pairs.append(upper_pair)
        lower_pairs.append(lower_pair)
    ordered = lower_pairs[::-1] + [(keys_low, values_low)] + upper_pairs
    key_buffer = jnp.concatenate([pair[0] for pair in ordered], axis=0)
    value_buffer = jnp.concatenate([pair[1] for pair in ordered], axis=0)
    own_positions = seq_place * tok_rows + jnp.arange(tok_rows, dtype=jnp.int32)
    query_ids = image_ids(lengths, own_positions, total_rows)
    key_positions = (seq_place - reach_blocks) * tok_rows + jnp.arange(
        (2 * reach_blocks + 1) * tok_rows, dtype=jnp.int32
    )
    key_ids = image_ids(lengths, key_positions, total_rows)
    allowed = query_ids[:, None] == key_ids[None, :]
    query_heads = split_heads(queries_low, local_heads)
    key_heads = split_heads(key_buffer, local_heads)
    value_heads = split_heads(value_buffer, local_heads)

    def head_forward(operands):
        query_one, key_one, value_one = operands
        scores = jnp.where(allowed, product_nt(query_one, key_one) * scaling, -1e30)
        peak = jnp.max(scores, axis=1, keepdims=True)
        exponent = jnp.exp(scores - peak)
        total_exp = jnp.sum(exponent, axis=1, keepdims=True)
        probability = exponent / total_exp
        result = product(probability.astype(jnp.bfloat16), value_one)
        return (result, peak[:, 0] + jnp.log(total_exp[:, 0]))

    head_result, head_lse = lax.map(head_forward, (query_heads, key_heads, value_heads))
    attended_low = join_heads(head_result).astype(jnp.bfloat16)
    attn_sum = lax.psum(product(attended_low, w_out), "tp")
    after_attn = input_f32 + attn_sum + o_bias
    mlp_in = layer_norm(after_attn, ln2_gain, ln2_bias).astype(jnp.bfloat16)
    hidden = product(mlp_in, w_up) + up_bias
    active_low = gelu_tanh(hidden).astype(jnp.bfloat16)
    mlp_sum = lax.psum(product(active_low, w_down).astype(jnp.bfloat16), "tp").astype(jnp.float32)
    after_mlp = after_attn + mlp_sum + down_bias
    features = after_mlp.astype(jnp.bfloat16)
    proj_gate = product(features, w_gate_proj)
    proj_up = product(features, w_up_proj)
    silu_gate = jax.nn.silu(proj_gate)
    proj_hidden = (silu_gate * proj_up).astype(jnp.bfloat16)
    proj_out = lax.psum(product(proj_hidden, w_down_proj).astype(jnp.bfloat16), "tp").astype(
        jnp.float32
    )
    context_low = rms_norm(proj_out, ctx_gain).astype(jnp.bfloat16)
    ctx_keys = product(context_low, w_ctxkey).astype(jnp.bfloat16)
    ctx_values = product(context_low, w_ctxval).astype(jnp.bfloat16)
    lat_normed = rms_norm(latents, lat_gain).astype(jnp.bfloat16)
    lat_queries = product(lat_normed, rq_weight).astype(jnp.bfloat16)
    lat_keys = product(lat_normed, w_ctxkey).astype(jnp.bfloat16)
    lat_values = product(lat_normed, w_ctxval).astype(jnp.bfloat16)
    query_grouped = lat_queries.reshape(lat_rows, kv_heads, group, RHD)
    key_grouped = ctx_keys.reshape(tok_rows, kv_heads, RHD)
    value_grouped = ctx_values.reshape(tok_rows, kv_heads, RHD)
    self_keys = lat_keys.reshape(lat_rows, kv_heads, RHD)
    self_values = lat_values.reshape(lat_rows, kv_heads, RHD)
    lat_scores = (
        jnp.einsum("lkgd,tkd->kglt", query_grouped, key_grouped, preferred_element_type=jnp.float32)
        * lat_scaling
    )
    self_scores = (
        jnp.einsum("lkgd,tkd->kglt", query_grouped, self_keys, preferred_element_type=jnp.float32)
        * lat_scaling
    )
    merged = joined(partial_stats(lat_scores, value_grouped), "seq", joint_stats)
    lat_peak, lat_total, lat_numer = joint_stats(merged, partial_stats(self_scores, self_values))
    lat_lse = lat_peak + jnp.log(lat_total)
    pooled_exact = lat_numer / lat_total[..., None]
    pooled_low = pooled_exact.transpose(2, 0, 1, 3).reshape(lat_rows, -1).astype(jnp.bfloat16)
    lat_mix = product(pooled_low, ro_weight)
    ro_width = ro_weight.shape[1] // seq_count
    ro_columns = lax.dynamic_slice_in_dim(lat_grad, seq_place * ro_width, ro_width, 1)
    ro_weight_grad = product_tn(pooled_low, ro_columns)
    pooled_grad = product_nt(lat_grad, ro_weight).astype(jnp.bfloat16)
    pooled_grouped = pooled_grad.reshape(lat_rows, kv_heads, group, RHD)
    pooled_f32 = pooled_grouped.astype(jnp.float32)
    lat_delta = jnp.sum(pooled_f32.transpose(1, 2, 0, 3) * pooled_exact, axis=-1)

    def score_grads(scores, key_part, value_part):
        probability = jnp.exp(scores - lat_lse[..., None])
        dprob = jnp.einsum(
            "lkgd,tkd->kglt", pooled_grouped, value_part, preferred_element_type=jnp.float32
        )
        dscore = (probability * (dprob - lat_delta[..., None])).astype(jnp.bfloat16)
        query_term = (
            jnp.einsum("kglt,tkd->lkgd", dscore, key_part, preferred_element_type=jnp.float32)
            * lat_scaling
        )
        key_term = (
            jnp.einsum("kglt,lkgd->tkd", dscore, query_grouped, preferred_element_type=jnp.float32)
            * lat_scaling
        ).astype(jnp.bfloat16)
        value_term = jnp.einsum(
            "kglt,lkgd->tkd", probability, pooled_f32, precision=lax.Precision.HIGHEST
        ).astype(jnp.bfloat16)
        return (
            query_term,
            key_term.reshape(key_part.shape[0], -1),
            value_term.reshape(key_part.shape[0], -1),
        )

    ctx_query_term, ctx_keys_grad, ctx_values_grad = score_grads(
        lat_scores, key_grouped, value_grouped
    )
    self_query_term, self_keys_grad, self_values_grad = score_grads(
        self_scores, self_keys, self_values
    )
    query_part = ctx_query_term + first_block * self_query_term
    query_sum = lax.psum(query_part, "seq")
    lat_queries_grad = query_sum.reshape(lat_rows, -1).astype(jnp.bfloat16)
    rq_rows = rq_weight.shape[0] // seq_count
    rq_weight_grad = product_tn(
        lax.dynamic_slice_in_dim(lat_normed, seq_place * rq_rows, rq_rows, 1), lat_queries_grad
    )
    rk_part = product_tn(context_low, ctx_keys_grad) + first_block * product_tn(
        lat_normed, self_keys_grad
    )
    rv_part = product_tn(context_low, ctx_values_grad) + first_block * product_tn(
        lat_normed, self_values_grad
    )
    ctx_part = product_nt(ctx_keys_grad, w_ctxkey) + product_nt(ctx_values_grad, w_ctxval)
    lat_part = (
        product_nt(lat_queries_grad, rq_weight)
        + product_nt(self_keys_grad, w_ctxkey)
        + product_nt(self_values_grad, w_ctxval)
    )
    ctx_back, lat_back, lat_mix_sum = (
        lax.psum(ctx_part.astype(jnp.bfloat16), "tp").astype(jnp.float32),
        lax.psum(lat_part.astype(jnp.bfloat16), "tp").astype(jnp.float32),
        lax.psum(lat_mix.astype(jnp.bfloat16), "tp").astype(jnp.float32),
    )
    latents_out = latents + lat_mix_sum
    lat_pull = jax.vjp(rms_norm, latents, lat_gain)[1]
    lat_in_grad, lat_gain_grad = lat_pull(lat_back)
    latents_grad = lat_grad.astype(jnp.float32) + lat_in_grad
    ctx_pull = jax.vjp(rms_norm, proj_out, ctx_gain)[1]
    proj_out_grad, ctx_gain_part = ctx_pull(ctx_back)
    proj_out_low = proj_out_grad.astype(jnp.bfloat16)
    down_proj_part = product_tn(proj_hidden, proj_out_low)
    hidden_pgrad = product_nt(proj_out_low, w_down_proj)
    silu_pull = jax.vjp(jax.nn.silu, proj_gate)[1]
    gate_grad_low = silu_pull(hidden_pgrad * proj_up)[0].astype(jnp.bfloat16)
    up_grad_low = (hidden_pgrad * silu_gate).astype(jnp.bfloat16)
    gate_proj_part = product_tn(features, gate_grad_low)
    up_proj_part = product_tn(features, up_grad_low)
    proj_in_grad = lax.psum(
        (product_nt(gate_grad_low, w_gate_proj) + product_nt(up_grad_low, w_up_proj)).astype(
            jnp.bfloat16
        ),
        "tp",
    ).astype(jnp.float32)
    mlp_out_grad = feat_grad.astype(jnp.float32) + proj_in_grad
    mlp_out_low = mlp_out_grad.astype(jnp.bfloat16)
    down_part = product_tn(active_low, mlp_out_low)
    down_bias_part = jnp.sum(mlp_out_low.astype(jnp.float32), axis=0)
    active_grad = product_nt(mlp_out_low, w_down)
    gelu_pull = jax.vjp(gelu_tanh, hidden)[1]
    hidden_grad = gelu_pull(active_grad)[0].astype(jnp.bfloat16)
    up_part = product_tn(mlp_in, hidden_grad)
    up_bias_part = jnp.sum(hidden_grad.astype(jnp.float32), axis=0)
    mlp_back = lax.psum(product_nt(hidden_grad, w_up).astype(jnp.bfloat16), "tp").astype(
        jnp.float32
    )
    ln2_pull = jax.vjp(layer_norm, after_attn, ln2_gain, ln2_bias)[1]
    norm_grad, ln2_gain_part, ln2_bias_part = ln2_pull(mlp_back)
    attn_out_grad = mlp_out_grad + norm_grad
    attn_out_low = attn_out_grad.astype(jnp.bfloat16)
    o_part = product_tn(attended_low, attn_out_low)
    o_bias_part = jnp.sum(attn_out_low.astype(jnp.float32), axis=0)
    attended_grad = product_nt(attn_out_low, w_out).astype(jnp.bfloat16)
    grad_heads = split_heads(attended_grad, local_heads)

    def head_backward(operands):
        query_one, key_one, value_one, grad_one, lse_one = operands
        scores = jnp.where(allowed, product_nt(query_one, key_one) * scaling, -1e30)
        probability = jnp.exp(scores - lse_one[:, None])
        dprob = product_nt(grad_one, value_one)
        row_inner = jnp.sum(probability * dprob, axis=1, keepdims=True)
        score_low = (probability * (dprob - row_inner)).astype(jnp.bfloat16)
        query_one_grad = product(score_low, key_one) * scaling
        key_one_grad = product_tn(score_low, query_one) * scaling
        value_one_grad = product_tn(probability.astype(jnp.bfloat16), grad_one)
        return (query_one_grad, key_one_grad, value_one_grad)

    query_hgrad, key_hgrad, value_hgrad = lax.map(
        head_backward, (query_heads, key_heads, value_heads, grad_heads, head_lse)
    )
    key_blocks = join_heads(key_hgrad).reshape(2 * reach_blocks + 1, tok_rows, -1)
    value_blocks = join_heads(value_hgrad).reshape(2 * reach_blocks + 1, tok_rows, -1)
    key_total = key_blocks[reach_blocks]
    value_total = value_blocks[reach_blocks]
    carry_upper = (key_blocks[2 * reach_blocks], value_blocks[2 * reach_blocks])
    carry_lower = (key_blocks[0], value_blocks[0])
    for distance in range(reach_blocks - 1, 0, -1):
        moved_upper = returned(carry_upper[0], carry_upper[1], 1)
        carry_upper = (
            moved_upper[0] + key_blocks[reach_blocks + distance],
            moved_upper[1] + value_blocks[reach_blocks + distance],
        )
        moved_lower = returned(carry_lower[0], carry_lower[1], -1)
        carry_lower = (
            moved_lower[0] + key_blocks[reach_blocks - distance],
            moved_lower[1] + value_blocks[reach_blocks - distance],
        )
    moved_upper = returned(carry_upper[0], carry_upper[1], 1)
    moved_lower = returned(carry_lower[0], carry_lower[1], -1)
    key_total = key_total + moved_upper[0] + moved_lower[0]
    value_total = value_total + moved_upper[1] + moved_lower[1]
    queries_grad = join_heads(query_hgrad).astype(jnp.bfloat16)
    keys_grad = key_total.astype(jnp.bfloat16)
    values_grad = value_total.astype(jnp.bfloat16)
    q_part = product_tn(normed_in, queries_grad)
    k_part = product_tn(normed_in, keys_grad)
    v_part = product_tn(normed_in, values_grad)
    q_bias_part = jnp.sum(queries_grad.astype(jnp.float32), axis=0)
    v_bias_part = jnp.sum(values_grad.astype(jnp.float32), axis=0)
    attn_back = lax.psum(
        (
            product_nt(queries_grad, w_query)
            + product_nt(keys_grad, w_key)
            + product_nt(values_grad, w_value)
        ).astype(jnp.bfloat16),
        "tp",
    ).astype(jnp.float32)
    ln1_pull = jax.vjp(layer_norm, input_f32, ln1_gain, ln1_bias)[1]
    in_grad, ln1_gain_part, ln1_bias_part = ln1_pull(attn_back)
    patches_grad = (attn_out_grad + in_grad).astype(jnp.bfloat16)
    weight_sums = (
        lax.psum_scatter(q_part, "seq", scatter_dimension=0, tiled=True),
        lax.psum_scatter(k_part, "seq", scatter_dimension=0, tiled=True),
        lax.psum_scatter(v_part, "seq", scatter_dimension=0, tiled=True),
        lax.psum_scatter(o_part, "seq", scatter_dimension=1, tiled=True),
        lax.psum_scatter(up_part, "seq", scatter_dimension=0, tiled=True),
        lax.psum_scatter(down_part, "seq", scatter_dimension=1, tiled=True),
        lax.psum_scatter(gate_proj_part, "seq", scatter_dimension=0, tiled=True),
        lax.psum_scatter(up_proj_part, "seq", scatter_dimension=0, tiled=True),
        lax.psum_scatter(down_proj_part, "seq", scatter_dimension=1, tiled=True),
        lax.psum_scatter(rk_part, "seq", scatter_dimension=0, tiled=True),
        lax.psum_scatter(rv_part, "seq", scatter_dimension=0, tiled=True),
    )
    small_sums = lax.psum(
        (
            ln1_gain_part,
            ln1_bias_part,
            q_bias_part,
            v_bias_part,
            o_bias_part,
            ln2_gain_part,
            ln2_bias_part,
            up_bias_part,
            down_bias_part,
            ctx_gain_part,
        ),
        "seq",
    )
    return (
        features,
        latents_out,
        patches_grad,
        latents_grad,
        small_sums[0],
        small_sums[1],
        weight_sums[0],
        small_sums[2],
        weight_sums[1],
        weight_sums[2],
        small_sums[3],
        weight_sums[3],
        small_sums[4],
        small_sums[5],
        small_sums[6],
        weight_sums[4],
        small_sums[7],
        weight_sums[5],
        small_sums[8],
        weight_sums[6],
        weight_sums[7],
        weight_sums[8],
        small_sums[9],
        weight_sums[9],
        weight_sums[10],
        lat_gain_grad,
        rq_weight_grad,
        ro_weight_grad,
    )


MESH = pl.DeviceIdType.MESH


def greet(partners):
    barrier = pltpu.get_barrier_semaphore()
    for present, device in partners:

        @pl.when(present)
        def _():
            pl.semaphore_signal(
                barrier, inc=1, device_id={"seq": device}, device_id_type=MESH
            )

    pl.semaphore_wait(barrier, sum(jnp.where(present, 1, 0) for present, _ in partners))


def place():
    me = lax.axis_index("seq")
    x, y, z = lax.rem(me, 2), lax.rem(lax.div(me, 2), 2), lax.div(me, 4)
    first = lax.axis_index("tp") == 0
    a, b = jnp.where(first, x, y), jnp.where(first, y, x)
    step_a, step_b = jnp.where(first, 1, 2), jnp.where(first, 2, 1)
    return me, z, a, b, step_a, step_b


def neighbours(layers):
    me, z, a, b, step_a, step_b = place()
    up, down = z < layers - 1, z > 0
    return (
        (up, jnp.where(up, me + 4, me)),
        (down, jnp.where(down, me - 4, me)),
        (me >= 0, me + step_a * (1 - 2 * a)),
        (me >= 0, me + step_b * (1 - 2 * b)),
    )


class Arrivals:
    def __init__(self, n, x_ref, slots, sent, landed, local, reach=None):
        self.n, self.layers, self.reach = n, n // 4, reach
        self.x_ref, self.slots, self.sent, self.landed = x_ref, slots, sent, landed
        self.me, self.z, self.a, self.b, self.step_a, self.step_b = place()
        self.partners = neighbours(self.layers)
        (self.up, self.to_up), (self.down, self.to_down) = self.partners[:2]
        self.to_a, self.to_b = self.partners[2][1], self.partners[3][1]
        self.own = pltpu.make_async_copy(x_ref, slots.at[self.me], local)

    def at(self, layer, of_a, of_b):
        return layer * 4 + of_a * self.step_a + of_b * self.step_b

    def wanted(self, slot, layer):
        if self.reach is None:
            return slot >= 0
        return jnp.where(
            layer < self.layers // 2, slot < self.reach, slot >= self.n - self.reach
        )

    def send(self, slot, device, way, source=None):
        return pltpu.make_async_remote_copy(
            src_ref=self.slots.at[slot] if source is None else source,
            dst_ref=self.slots.at[slot],
            send_sem=self.sent.at[way, slot],
            recv_sem=self.landed.at[slot],
            device_id={"seq": device},
            device_id_type=MESH,
        )

    def layer(self, k):
        z, last = self.z, self.layers - 1
        both = 2 * jnp.minimum(z, last - z)
        step = (k + 1) // 2
        near = jnp.where(k % 2 == 1, z - step, z + step)
        far = jnp.where(z < last - z, k, last - k)
        return jnp.where(k <= both, near, far)

    def block(self, i):
        last = 2 * self.layers - 1
        over_b = i // (2 * self.layers)
        j = i - over_b * 2 * self.layers
        over_a = jnp.where((j > 0) & ((j % 2 == 0) | (j == last)), 1, 0)
        nearness = jnp.where(over_a == 1, jnp.maximum(j - 1, 0) // 2, (j + 1) // 2)
        layer = self.layer(nearness)
        of_a = jnp.where(over_a == 1, 1 - self.a, self.a)
        of_b = jnp.where(over_b == 1, 1 - self.b, self.b)
        return layer, over_a, over_b, self.at(layer, of_a, of_b)

    def start(self, beside=None):
        if beside is None:
            greet(self.partners)
        else:
            beside.greet()
        self.own.start()
        me, x_ref = self.me, self.x_ref

        @pl.when(self.up & self.wanted(me, self.z + 1))
        def _():
            self.send(me, self.to_up, 0, x_ref).start()

        @pl.when(self.down & self.wanted(me, self.z - 1))
        def _():
            self.send(me, self.to_down, 1, x_ref).start()

        self.send(me, self.to_b, 3, x_ref).start()
        self.send(me, self.to_a, 2, x_ref).start()
        self.own.wait()

    def take(self, i):
        layer, over_a, over_b, slot = self.block(i)
        here = (i > 0) & self.wanted(slot, self.z)

        @pl.when(here)
        def _():
            self.send(slot, self.to_b, 3).wait_recv()

        @pl.when(here & (over_b == 0))
        def _():
            @pl.when(over_a == 0)
            def _():
                @pl.when((layer < self.z) & self.up & self.wanted(slot, self.z + 1))
                def _():
                    self.send(slot, self.to_up, 0).start()

                @pl.when((layer > self.z) & self.down & self.wanted(slot, self.z - 1))
                def _():
                    self.send(slot, self.to_down, 1).start()

                self.send(slot, self.to_a, 2).start()

            self.send(slot, self.to_b, 3).start()

        return slot

    def drain(self):
        def body(layer, _):
            slot = self.at(layer, self.a, self.b)
            beyond = self.at(layer, 1 - self.a, self.b)

            @pl.when(self.wanted(slot, self.z))
            def _():
                self.send(slot, self.to_a, 2).wait_send()
                self.send(slot, self.to_b, 3).wait_send()

            @pl.when(self.wanted(beyond, self.z))
            def _():
                self.send(beyond, self.to_b, 3).wait_send()

            @pl.when((layer <= self.z) & self.up & self.wanted(slot, self.z + 1))
            def _():
                self.send(slot, self.to_up, 0).wait_send()

            @pl.when((layer >= self.z) & self.down & self.wanted(slot, self.z - 1))
            def _():
                self.send(slot, self.to_down, 1).wait_send()

            return 0

        lax.fori_loop(0, self.layers, body, 0)


def gather_semaphores(n):
    return [
        pltpu.SemaphoreType.DMA((4, n)),
        pltpu.SemaphoreType.DMA((n,)),
        pltpu.SemaphoreType.DMA(()),
    ]


def gather_kernel(n, x_ref, o_ref, *semaphores):
    arrivals = Arrivals(n, x_ref, o_ref, *semaphores)
    arrivals.start()

    def body(i, _):
        arrivals.take(i)
        return 0

    lax.fori_loop(0, n, body, 0)
    arrivals.drain()


def gathered_blocks(x, collective_id):
    n = lax.axis_size("seq")
    return pl.pallas_call(
        functools.partial(gather_kernel, n),
        out_shape=jax.ShapeDtypeStruct((n,) + x.shape, x.dtype),
        in_specs=[pl.BlockSpec(memory_space=pl.ANY)],
        out_specs=pl.BlockSpec(memory_space=pl.ANY),
        scratch_shapes=gather_semaphores(n),
        compiler_params=pltpu.CompilerParams(
            collective_id=collective_id, has_side_effects=True
        ),
    )(x)


def gather_beside_kernel(n, reach, x_ref, y_ref, o_ref, y_out, sent, landed, local, *semaphores):
    beside = Beside(n, 1, ((y_ref, y_out),), sent, landed, local)
    arrivals = Arrivals(n, x_ref, o_ref, *semaphores, reach=reach)
    arrivals.start(beside)

    def body(i, _):
        arrivals.take(i)
        beside.start(i)
        return 0

    lax.fori_loop(0, n, body, 0)
    beside.finish()
    arrivals.drain()


def gathered_beside(x, y, collective_id, reach=None):
    n = lax.axis_size("seq")
    anywhere = pl.BlockSpec(memory_space=pl.ANY)
    return pl.pallas_call(
        functools.partial(gather_beside_kernel, n, reach),
        out_shape=[
            jax.ShapeDtypeStruct((n,) + x.shape, x.dtype),
            jax.ShapeDtypeStruct(y.shape, y.dtype),
        ],
        in_specs=[anywhere] * 2,
        out_specs=[anywhere] * 2,
        scratch_shapes=[pltpu.SemaphoreType.DMA((1, n))] * 2
        + [pltpu.SemaphoreType.DMA((1,))]
        + gather_semaphores(n),
        compiler_params=pltpu.CompilerParams(
            collective_id=collective_id, has_side_effects=True
        ),
    )(x, y)


def pair_rows(pair):
    return pair.reshape(pair.shape[0] * pair.shape[1], pair.shape[2])


def units_kernel(
    n,
    x_ref,
    w_gate_ref,
    w_up_ref,
    slots,
    gate_ref,
    up_ref,
    hidden_ref,
    x_buf,
    gate_buf,
    up_buf,
    hidden_buf,
    load_sem,
    store_sem,
    *semaphores,
):
    arrivals = Arrivals(n, x_ref, slots, *semaphores)
    arrivals.start()
    kept = ((gate_ref, gate_buf), (up_ref, up_buf), (hidden_ref, hidden_buf))

    def stores(pair):
        buf = pair % 2
        return [
            pltpu.make_async_copy(
                held.at[buf, i], out.at[arrivals.block(2 * pair + i)[3]], store_sem.at[buf, i, j]
            )
            for i in range(2)
            for j, (out, held) in enumerate(kept)
        ]

    def body(pair, _):
        buf = pair % 2
        loads = [
            pltpu.make_async_copy(
                slots.at[arrivals.take(2 * pair + i)], x_buf.at[i], load_sem.at[i]
            )
            for i in range(2)
        ]
        for load in loads:
            load.start()
        for load in loads:
            load.wait()

        @pl.when(pair >= 2)
        def _():
            for store in stores(pair - 2):
                store.wait()

        x = pair_rows(x_buf[...])
        shape = gate_buf.shape[1:]
        gate = product(x, w_gate_ref[...])
        up = product(x, w_up_ref[...])
        gate_buf[buf] = gate.reshape(shape)
        up_buf[buf] = up.reshape(shape)
        hidden_buf[buf] = (gate * jax.nn.sigmoid(gate) * up).astype(jnp.bfloat16).reshape(shape)
        for store in stores(pair):
            store.start()
        return 0

    lax.fori_loop(0, n // 2, body, 0)
    for pair in (n // 2 - 2, n // 2 - 1):
        for store in stores(pair):
            store.wait()
    arrivals.drain()


def gathered_units(x, w_gate, w_up, collective_id):
    n = lax.axis_size("seq")
    rows, units = x.shape[0], w_gate.shape[1]
    exact = jax.ShapeDtypeStruct((n, rows, units), jnp.float32)
    low = jax.ShapeDtypeStruct((n, rows, units), jnp.bfloat16)
    anywhere = pl.BlockSpec(memory_space=pl.ANY)
    return pl.pallas_call(
        functools.partial(units_kernel, n),
        out_shape=[jax.ShapeDtypeStruct((n,) + x.shape, x.dtype), exact, exact, low],
        in_specs=[anywhere] + [pl.BlockSpec(memory_space=pltpu.VMEM)] * 2,
        out_specs=[anywhere] * 4,
        scratch_shapes=[
            pltpu.VMEM((2,) + x.shape, x.dtype),
            pltpu.VMEM((2, 2, rows, units), jnp.float32),
            pltpu.VMEM((2, 2, rows, units), jnp.float32),
            pltpu.VMEM((2, 2, rows, units), jnp.bfloat16),
            pltpu.SemaphoreType.DMA((2,)),
            pltpu.SemaphoreType.DMA((2, 2, 3)),
        ]
        + gather_semaphores(n),
        compiler_params=pltpu.CompilerParams(
            collective_id=collective_id, has_side_effects=True, vmem_limit_bytes=60 * 2**20
        ),
    )(x, w_gate, w_up)


def units_back_kernel(
    n,
    x_ref,
    w_gate_ref,
    w_up_ref,
    down_mine_ref,
    down_other_ref,
    features_ref,
    gate_ref,
    up_ref,
    slots,
    terms_ref,
    dunits_mine,
    dunits_other,
    ddown_mine,
    ddown_other,
    x_buf,
    features_buf,
    gate_buf,
    up_buf,
    terms_buf,
    hidden_grad,
    gate_sum,
    up_sum,
    down_sum,
    down_buf,
    units_buf,
    load_sem,
    store_sem,
    out_sem,
    *semaphores,
):
    arrivals = Arrivals(n, x_ref, slots, *semaphores)
    arrivals.start()
    gate_sum[...] = jnp.zeros_like(gate_sum)
    up_sum[...] = jnp.zeros_like(up_sum)
    down_sum[...] = jnp.zeros_like(down_sum)
    units, cols = down_mine_ref.shape[1:]
    room = hidden_grad.shape[1] // 2
    out_width = n * cols
    several = 4
    tile = several * cols
    chunks, chunk = terms_ref.shape[0], terms_ref.shape[3]

    def stores(pair):
        return [
            pltpu.make_async_copy(
                terms_buf.at[i, :, pl.ds(c * chunk, chunk)],
                terms_ref.at[c, arrivals.block(2 * pair + i)[3]],
                store_sem.at[i, c],
            )
            for i in range(2)
            for c in range(chunks)
        ]

    def loads(pair):
        return [
            pltpu.make_async_copy(
                source.at[arrivals.block(2 * pair + i)[3]],
                held.at[pair % 2, i] if j < 2 else held.at[i],
                load_sem.at[pair % 2, i, j],
            )
            for i in range(2)
            for j, (source, held) in enumerate(
                ((slots, x_buf), (features_ref, features_buf), (gate_ref, gate_buf), (up_ref, up_buf))
            )
        ]

    def take_pair(pair):
        arrivals.take(2 * pair)
        arrivals.take(2 * pair + 1)
        for load in loads(pair):
            load.start()

    take_pair(0)

    def body(pair, _):
        buf = pair % 2
        for load in loads(pair):
            load.wait()
        hidden_grad[...] = jnp.zeros_like(hidden_grad)

        def back_tile(t, _):
            for i, held in enumerate((down_mine_ref, down_other_ref)):
                hidden_grad[:, i * room : i * room + units] += sum(
                    product_nt(
                        pair_rows(
                            x_buf[buf, :, :, pl.ds(pl.multiple_of(t * tile + j * cols, cols), cols)]
                        ),
                        held[t * several + j],
                    )
                    for j in range(several)
                )
            return 0

        lax.fori_loop(0, out_width // tile, back_tile, 0)
        gate, up, grad = pair_rows(gate_buf[...]), pair_rows(up_buf[...]), hidden_grad[...]
        share = jax.nn.sigmoid(gate)
        silu = gate * share
        gate_low = (grad * up * (share * (1.0 + gate * (1.0 - share)))).astype(jnp.bfloat16)
        up_low = (grad * silu).astype(jnp.bfloat16)
        hidden_t = (silu * up).astype(jnp.bfloat16).T
        terms = product_nt(gate_low, w_gate_ref[...]) + product_nt(up_low, w_up_ref[...])

        @pl.when(pair >= 1)
        def _():
            for store in stores(pair - 1):
                store.wait()

        terms_buf[...] = terms.astype(jnp.bfloat16).reshape(terms_buf.shape)
        for store in stores(pair):
            store.start()

        @pl.when(pair + 1 < n // 2)
        def _():
            take_pair(pair + 1)

        features_t = pair_rows(features_buf[buf]).T
        for begin in range(0, gate_low.shape[1], 256):
            columns = slice(begin, begin + 256)
            gate_sum[:, columns] += product(features_t, gate_low[:, columns])
            up_sum[:, columns] += product(features_t, up_low[:, columns])

        def down_tile(t, _):
            columns = pl.ds(pl.multiple_of(t * tile, tile), tile)
            x = pair_rows(x_buf[buf, :, :, columns])
            for i in range(2):
                down_sum[i, :, columns] += product(hidden_t[i * room : i * room + units], x)
            return 0

        lax.fori_loop(0, out_width // tile, down_tile, 0)
        return 0

    lax.fori_loop(0, n // 2, body, 0)
    def grad_stores(j):
        return [
            pltpu.make_async_copy(source, target.at[j], out_sem.at[j % 2, i])
            for i, (source, target) in enumerate(
                (
                    (down_buf.at[j % 2, 0], ddown_mine),
                    (down_buf.at[j % 2, 1], ddown_other),
                    (units_buf.at[j % 2, 0], dunits_mine),
                    (units_buf.at[j % 2, 1], dunits_other),
                )
            )
        ]

    def grads_out(j, _):
        @pl.when(j >= 2)
        def _():
            for store in grad_stores(j - 2):
                store.wait()

        columns = pl.ds(pl.multiple_of(j * cols, cols), cols)
        down_buf[j % 2] = down_sum[:, :, columns].astype(jnp.bfloat16)
        owned = units_buf.shape[3]
        owner = pl.ds(pl.multiple_of(j * owned, 8), owned)
        for i in range(2):
            for k, total in enumerate((gate_sum, up_sum)):
                units_buf[j % 2, i, k] = total[owner, i * room : (i + 1) * room].astype(
                    jnp.bfloat16
                )
        for store in grad_stores(j):
            store.start()
        return 0

    lax.fori_loop(0, n, grads_out, 0)
    for j in (n - 2, n - 1):
        for store in grad_stores(j):
            store.wait()
    for store in stores(n // 2 - 1):
        store.wait()
    arrivals.drain()


def gathered_back(x, w_gate, w_up, mine, other, features, gate, up, chunks, collective_id):
    n = lax.axis_size("seq")
    rows, out_width = x.shape
    width, units = w_gate.shape
    low, exact = jnp.bfloat16, jnp.float32
    anywhere = pl.BlockSpec(memory_space=pl.ANY)
    in_vmem = pl.BlockSpec(memory_space=pltpu.VMEM)
    return pl.pallas_call(
        functools.partial(units_back_kernel, n),
        out_shape=[
            jax.ShapeDtypeStruct((n,) + x.shape, low),
            jax.ShapeDtypeStruct((chunks, n, rows, width // chunks), low),
            jax.ShapeDtypeStruct((n, 2, width // n, units // 2), low),
            jax.ShapeDtypeStruct((n, 2, width // n, units // 2), low),
            jax.ShapeDtypeStruct(mine.shape, low),
            jax.ShapeDtypeStruct(mine.shape, low),
        ],
        in_specs=[anywhere] + [in_vmem] * 4 + [anywhere] * 3,
        out_specs=[anywhere] * 6,
        scratch_shapes=[
            pltpu.VMEM((2, 2, rows, out_width), low),
            pltpu.VMEM((2, 2, rows, width), low),
            pltpu.VMEM((2, rows, units), exact),
            pltpu.VMEM((2, rows, units), exact),
            pltpu.VMEM((2, rows, width), low),
            pltpu.VMEM((2 * rows, units), exact),
            pltpu.VMEM((width, units), exact),
            pltpu.VMEM((width, units), exact),
            pltpu.VMEM((2, mine.shape[1], out_width), exact),
            pltpu.VMEM((2, 2) + mine.shape[1:], low),
            pltpu.VMEM((2, 2, 2, width // n, units // 2), low),
            pltpu.SemaphoreType.DMA((2, 2, 4)),
            pltpu.SemaphoreType.DMA((2, chunks)),
            pltpu.SemaphoreType.DMA((2, 4)),
        ]
        + gather_semaphores(n),
        compiler_params=pltpu.CompilerParams(
            collective_id=collective_id, has_side_effects=True, vmem_limit_bytes=60 * 2**20
        ),
    )(x, w_gate, w_up, mine, other, features, gate, up)


def scatter_kernel(n, chunks, p_ref, o_ref, from_b, from_a, from_down, from_up, *semaphores, fill=None, work=None):
    layers = n // 4
    me, z, a, b, step_a, step_b = place()
    partners = neighbours(layers)
    (up, to_up), (down, to_down), (_, to_a), (_, to_b) = partners
    b_sent, b_landed, a_sent, a_landed, u_sent, u_landed, d_sent, d_landed = semaphores
    greet(partners)

    def at(layer, of_a, of_b):
        return layer * 4 + of_a * step_a + of_b * step_b

    def copy(source, target, sent, landed, device):
        return pltpu.make_async_remote_copy(
            src_ref=source,
            dst_ref=target,
            send_sem=sent,
            recv_sem=landed,
            device_id={"seq": device},
            device_id_type=MESH,
        )

    def over_b(c, of_a, layer):
        return copy(
            p_ref.at[c, at(layer, of_a, 1 - b)],
            from_b.at[c, of_a, layer],
            b_sent.at[c, of_a, layer],
            b_landed.at[c, of_a, layer],
            to_b,
        )

    def over_a(c, layer):
        return copy(
            p_ref.at[c, at(layer, 1 - a, b)],
            from_a.at[c, layer],
            a_sent.at[c, layer],
            a_landed.at[c, layer],
            to_a,
        )

    def upward(c, layer):
        return copy(
            p_ref.at[c, at(layer, a, b)],
            from_down.at[c, layer],
            u_sent.at[c, layer],
            u_landed.at[c, layer],
            to_up,
        )

    def downward(c, layer):
        return copy(
            p_ref.at[c, at(layer, a, b)],
            from_up.at[c, layer],
            d_sent.at[c, layer],
            d_landed.at[c, layer],
            to_down,
        )

    def each_layer(body):
        lax.fori_loop(0, layers, lambda layer, _: (body(layer), 0)[1], 0)

    def send_b(c):
        each_layer(lambda layer: over_b(c, 1 - a, layer).start())
        each_layer(lambda layer: over_b(c, a, layer).start())

    def send_a(c):
        def body(layer):
            over_b(c, 1 - a, layer).wait_recv()
            slot = at(layer, 1 - a, b)
            p_ref[c, slot] = p_ref[c, slot] + from_b[c, 1 - a, layer]
            over_a(c, layer).start()

        each_layer(body)

    def join_line(c):
        def body(layer):
            over_b(c, a, layer).wait_recv()
            over_a(c, layer).wait_recv()
            slot = at(layer, a, b)
            p_ref[c, slot] = p_ref[c, slot] + from_b[c, a, layer] + from_a[c, layer]

            @pl.when((layer > z) & (z == 0))
            def _():
                upward(c, layer).start()

            @pl.when((layer < z) & (z == layers - 1))
            def _():
                downward(c, layer).start()

        each_layer(body)

    def pass_up(c):
        def body(layer):
            @pl.when(layer > z)
            def _():
                upward(c, layer).wait_recv()
                slot = at(layer, a, b)
                p_ref[c, slot] = p_ref[c, slot] + from_down[c, layer]
                upward(c, layer).start()

        each_layer(body)

    def pass_down(c):
        def body(layer):
            @pl.when(layer < z)
            def _():
                downward(c, layer).wait_recv()
                slot = at(layer, a, b)
                p_ref[c, slot] = p_ref[c, slot] + from_up[c, layer]
                downward(c, layer).start()

        each_layer(body)

    def finish(c):
        @pl.when(down)
        def _():
            upward(c, z).wait_recv()
            p_ref[c, me] = p_ref[c, me] + from_down[c, z]

        @pl.when(up)
        def _():
            downward(c, z).wait_recv()
            p_ref[c, me] = p_ref[c, me] + from_up[c, z]

        o_ref[c] = p_ref[c, me]

    def when_chunk(step, stage):
        @pl.when((step >= 0) & (step < chunks))
        def _():
            stage(jnp.clip(step, 0, chunks - 1))

    def fill_and_send(c):
        if fill is not None:
            fill(c)
        send_b(c)

    fill_and_send(0)

    def step(t, _):
        when_chunk(t + 1, fill_and_send)
        if work is not None:
            work(t)
        when_chunk(t, send_a)
        when_chunk(t - 1, join_line)
        inner = (z > 0) & (z < layers - 1)

        @pl.when(inner)
        def _():
            when_chunk(t - 1 - z, pass_up)
            when_chunk(t - layers + z, pass_down)

        when_chunk(t - layers, finish)
        return 0

    lax.fori_loop(0, chunks + layers, step, 0)

    def drain(c, _):
        def body(layer):
            over_b(c, 0, layer).wait_send()
            over_b(c, 1, layer).wait_send()
            over_a(c, layer).wait_send()

            @pl.when(layer > z)
            def _():
                upward(c, layer).wait_send()

            @pl.when(layer < z)
            def _():
                downward(c, layer).wait_send()

        each_layer(body)
        return 0

    lax.fori_loop(0, chunks, drain, 0)


def scatter_scratch(chunks, n, block, dtype):
    layers = n // 4

    def slots(*count):
        return pltpu.VMEM((chunks,) + count + block, dtype)

    def semaphores(*count):
        return pltpu.SemaphoreType.DMA((chunks,) + count)

    return (
        [slots(2, layers)]
        + [slots(layers)] * 3
        + [semaphores(2, layers)] * 2
        + [semaphores(layers)] * 6
    )


def scattered_sum(terms, collective_id):
    chunks, n = terms.shape[:2]
    block = terms.shape[2:]
    return pl.pallas_call(
        functools.partial(scatter_kernel, n, chunks),
        out_shape=jax.ShapeDtypeStruct((chunks,) + block, terms.dtype),
        in_specs=[pl.BlockSpec(memory_space=pltpu.VMEM)],
        out_specs=pl.BlockSpec(memory_space=pltpu.VMEM),
        scratch_shapes=scatter_scratch(chunks, n, block, terms.dtype),
        compiler_params=pltpu.CompilerParams(
            collective_id=collective_id, has_side_effects=True, vmem_limit_bytes=60 * 2**20
        ),
    )(terms)


def down_kernel(n, hidden_ref, mine_ref, other_ref, o_ref, p_ref, *scratch):
    units = mine_ref.shape[1]
    room = hidden_ref.shape[2] // 2

    def fill(c):
        def body(pair, _):
            owners = pl.ds(2 * pair, 2)
            terms = sum(
                product(pair_rows(hidden_ref[owners, :, pl.ds(i * room, units)]), held[c])
                for i, held in enumerate((mine_ref, other_ref))
            )
            p_ref[c, owners] = terms.astype(p_ref.dtype).reshape((2,) + p_ref.shape[2:])
            return 0

        lax.fori_loop(0, n // 2, body, 0)

    scatter_kernel(n, n, p_ref, o_ref, *scratch, fill=fill)


def scattered_down(hidden, mine, other, collective_id):
    n, rows = hidden.shape[:2]
    block = (rows, mine.shape[2])
    return pl.pallas_call(
        functools.partial(down_kernel, n),
        out_shape=jax.ShapeDtypeStruct((n,) + block, hidden.dtype),
        in_specs=[pl.BlockSpec(memory_space=pltpu.VMEM)] * 3,
        out_specs=pl.BlockSpec(memory_space=pltpu.VMEM),
        scratch_shapes=[pltpu.VMEM((n, n) + block, hidden.dtype)]
        + scatter_scratch(n, n, block, hidden.dtype),
        compiler_params=pltpu.CompilerParams(
            collective_id=collective_id, has_side_effects=True, vmem_limit_bytes=60 * 2**20
        ),
    )(hidden, mine, other)


class Beside:
    def __init__(self, n, per_step, pairs, sent, landed, local):
        self.n, self.per_step, self.pairs = n, per_step, pairs
        self.sent, self.landed = sent, landed
        self.me = lax.axis_index("seq")
        self.own = [
            pltpu.make_async_copy(source.at[self.me], target.at[self.me], local.at[j])
            for j, (source, target) in enumerate(pairs)
        ]

    def greet(self):
        barrier = pltpu.get_barrier_semaphore()
        for step in range(1, self.n):
            pl.semaphore_signal(
                barrier,
                inc=1,
                device_id={"seq": lax.rem(self.me + step, self.n)},
                device_id_type=MESH,
            )
        pl.semaphore_wait(barrier, self.n - 1)
        for own in self.own:
            own.start()

    def copies(self, step):
        other = lax.rem(self.me + step, self.n)
        return [
            pltpu.make_async_remote_copy(
                src_ref=source.at[other],
                dst_ref=target.at[self.me],
                send_sem=self.sent.at[j, step],
                recv_sem=self.landed.at[j, step],
                device_id={"seq": other},
                device_id_type=MESH,
            )
            for j, (source, target) in enumerate(self.pairs)
        ]

    def start(self, t):
        for i in range(self.per_step):
            step = t * self.per_step + i + 1

            @pl.when(step < self.n)
            def _():
                for copy in self.copies(jnp.minimum(step, self.n - 1)):
                    copy.start()

    def finish(self):
        def body(step, _):
            for copy in self.copies(step):
                copy.wait()
            return 0

        lax.fori_loop(1, self.n, body, 0)
        for own in self.own:
            own.wait()


def vision_kernel(n, chunks, spans, scaling, *refs):
    left_ref, right_ref, *attention = refs[:9]
    o_ref, *grads = refs[9:13]
    p_ref, *scratch = refs[13:]
    cols = right_ref.shape[1] // chunks
    shard = left_ref.shape[1] // n
    tile = 128
    for total in grads[1:]:
        total[...] = jnp.zeros_like(total)

    def fill(c):
        def body(t, _):
            tile = c * (cols // 128) + t
            source = sum(jnp.where(tile >= span, 1, 0) for span in spans[1:])
            columns = pl.ds(pl.multiple_of(tile * 128, 128), 128)
            terms = product(left_ref[source], right_ref[:, columns])
            p_ref[c, :, :, pl.ds(pl.multiple_of(t * 128, 128), 128)] = terms.reshape(
                n, shard, 128
            ).astype(p_ref.dtype)
            return 0

        lax.fori_loop(0, cols // 128, body, 0)

    tiles = attention[0].shape[0] // tile
    assert tiles <= chunks + n // 4

    def work(t):
        @pl.when(t < tiles)
        def _():
            attend_back_tile(scaling, tile, jnp.minimum(t, tiles - 1), *attention, *grads)

    scatter_kernel(n, chunks, p_ref, o_ref, *scratch, fill=fill, work=work)


def scattered_vision(left, right, attention, scaling, spans, chunks, collective_id):
    n = lax.axis_size("seq")
    block = (left.shape[1] // n, right.shape[1] // chunks)
    in_vmem = pl.BlockSpec(memory_space=pltpu.VMEM)
    return pl.pallas_call(
        functools.partial(vision_kernel, n, chunks, spans, scaling),
        out_shape=[jax.ShapeDtypeStruct((chunks,) + block, left.dtype)]
        + [jax.ShapeDtypeStruct(x.shape, jnp.float32) for x in attention[:3]],
        in_specs=[in_vmem] * 9,
        out_specs=[in_vmem] * 4,
        scratch_shapes=[pltpu.VMEM((chunks, n) + block, left.dtype)]
        + scatter_scratch(chunks, n, block, left.dtype),
        compiler_params=pltpu.CompilerParams(
            collective_id=collective_id, has_side_effects=True, vmem_limit_bytes=60 * 2**20
        ),
    )(left, right, *attention)


def exchange_kernel(n, groups, *refs):
    count = len(groups)
    sources, targets = refs[:count], refs[count : 2 * count]
    sent, landed, local = refs[2 * count :]
    me = lax.axis_index("seq")
    barrier = pltpu.get_barrier_semaphore()
    for step in range(1, n):
        pl.semaphore_signal(
            barrier, inc=1, device_id={"seq": lax.rem(me + step, n)}, device_id_type=MESH
        )
    pl.semaphore_wait(barrier, n - 1)
    copies = []
    for j, group in enumerate(groups):
        base = lax.div(me, group) * group
        mine = me - base
        copies.append(
            pltpu.make_async_copy(sources[j].at[mine], targets[j].at[mine], local.at[j])
        )
        copies[-1].start()
        for step in range(1, group):
            other = lax.rem(mine + step, group)
            copies.append(
                pltpu.make_async_remote_copy(
                    src_ref=sources[j].at[other],
                    dst_ref=targets[j].at[mine],
                    send_sem=sent.at[j, step],
                    recv_sem=landed.at[j, step],
                    device_id={"seq": base + other},
                    device_id_type=MESH,
                )
            )
            copies[-1].start()
    for copy in copies:
        copy.wait()


def exchanged(arrays, collective_id):
    n = lax.axis_size("seq")
    count = len(arrays)
    groups = tuple(x.shape[0] for x in arrays)
    return pl.pallas_call(
        functools.partial(exchange_kernel, n, groups),
        out_shape=[jax.ShapeDtypeStruct(x.shape, x.dtype) for x in arrays],
        in_specs=[pl.BlockSpec(memory_space=pl.ANY)] * count,
        out_specs=[pl.BlockSpec(memory_space=pl.ANY)] * count,
        scratch_shapes=[pltpu.SemaphoreType.DMA((count, n))] * 2
        + [pltpu.SemaphoreType.DMA((count,))],
        compiler_params=pltpu.CompilerParams(
            collective_id=collective_id, has_side_effects=True
        ),
    )(*arrays)


def reduce_kernel(n, combine, x_ref, o_ref, shares, total, sent, landed, sent_on, landed_on):
    me = lax.axis_index("seq")
    barrier = pltpu.get_barrier_semaphore()
    others = [lax.rem(me + step, n) for step in range(1, n)]
    for other in others:
        pl.semaphore_signal(barrier, inc=1, device_id={"seq": other}, device_id_type=MESH)
    pl.semaphore_wait(barrier, n - 1)

    def copy(step, source, target, sent, landed):
        return pltpu.make_async_remote_copy(
            src_ref=source,
            dst_ref=target,
            send_sem=sent.at[step],
            recv_sem=landed.at[step],
            device_id={"seq": others[step - 1]},
            device_id_type=MESH,
        )

    there = [copy(i, x_ref.at[others[i - 1]], shares.at[me], sent, landed) for i in range(1, n)]
    for move in there:
        move.start()
    shares[me] = x_ref[me]
    for move in there:
        move.wait()
    total[...] = combine(shares[...])
    back = [copy(i, total, o_ref.at[me], sent_on, landed_on) for i in range(1, n)]
    for move in back:
        move.start()
    o_ref[me] = total[...]
    for move in back:
        move.wait()


def reduced(x, combine, collective_id):
    n = x.shape[0]
    return pl.pallas_call(
        functools.partial(reduce_kernel, n, combine),
        out_shape=jax.ShapeDtypeStruct(x.shape, x.dtype),
        in_specs=[pl.BlockSpec(memory_space=pltpu.VMEM)],
        out_specs=pl.BlockSpec(memory_space=pltpu.VMEM),
        scratch_shapes=[pltpu.VMEM(x.shape, x.dtype), pltpu.VMEM(x.shape[1:], x.dtype)]
        + [pltpu.SemaphoreType.DMA((n,))] * 4,
        compiler_params=pltpu.CompilerParams(
            collective_id=collective_id, has_side_effects=True
        ),
    )(x)


def added(shares):
    return jnp.sum(shares, axis=0)


def softmax_shares(shares):
    column = lax.broadcasted_iota(jnp.int32, shares.shape, 2)
    at_peak = column == RHD
    peak = jnp.max(jnp.where(at_peak, shares, -jnp.inf), axis=2, keepdims=True)
    top = jnp.max(peak, axis=0, keepdims=True)
    sums = jnp.sum(shares * jnp.exp(peak - top), axis=0)
    return jnp.where(at_peak[0], top[0], sums)


def swapped(value):
    return lax.ppermute(value, "tp", [(0, 1), (1, 0)])


def rounded(value):
    return lax.reduce_precision(value, 8, 7)


def paired(value):
    kept = rounded(value)
    return kept + swapped(kept.astype(jnp.bfloat16)).astype(jnp.float32)


def in_order(mine, other, axis):
    first = lax.axis_index("tp") == 0
    return jnp.concatenate(
        [jnp.where(first, mine, other), jnp.where(first, other, mine)], axis=axis
    )


def attend_kernel(scaling, q_ref, k_ref, v_ref, qid_ref, kid_ref, o_ref, lse_ref):
    scores = product_nt(q_ref[...], k_ref[...]) * scaling
    scores = jnp.where(qid_ref[...] == kid_ref[...], scores, -1e30)
    peak = jnp.max(scores, axis=1, keepdims=True)
    weights = jnp.exp(scores - peak)
    total = jnp.sum(weights, axis=1, keepdims=True)
    probability = (weights / total).astype(jnp.bfloat16)
    o_ref[...] = product(probability, v_ref[...]).astype(o_ref.dtype)
    lse_ref[...] = peak + jnp.log(total)


def attend_back_tile(scaling, tile, t, q_ref, k_ref, v_ref, g_ref, qid_ref, kid_ref, lse_ref, *grads):
    dq_ref, dk_ref, dv_ref = grads
    rows = pl.ds(pl.multiple_of(t * tile, tile), tile)
    query, grad = q_ref[rows], g_ref[rows]
    scores = product_nt(query, k_ref[...]) * scaling
    scores = jnp.where(qid_ref[rows] == kid_ref[...], scores, -1e30)
    probability = jnp.exp(scores - lse_ref[rows])
    dprob = product_nt(grad, v_ref[...])
    inner = jnp.sum(probability * dprob, axis=1, keepdims=True)
    low = (probability * (dprob - inner)).astype(jnp.bfloat16)
    dq_ref[rows] = product(low, k_ref[...]) * scaling
    dk_ref[...] += product_tn(low, query) * scaling
    dv_ref[...] += product_tn(probability.astype(jnp.bfloat16), grad)


def attention_call(queries, window, width, tile, scaling):
    tiled = lambda columns: pl.BlockSpec((tile, columns), lambda i: (i, 0))
    whole = lambda rows, columns: pl.BlockSpec((rows, columns), lambda i: (0, 0))
    params = pltpu.CompilerParams(vmem_limit_bytes=56 * 2**20)
    forward = pl.pallas_call(
        functools.partial(attend_kernel, scaling),
        grid=(queries // tile,),
        in_specs=[
            tiled(width),
            whole(window, width),
            whole(window, width),
            tiled(1),
            whole(1, window),
        ],
        out_specs=[tiled(width), tiled(1)],
        out_shape=[
            jax.ShapeDtypeStruct((queries, width), jnp.bfloat16),
            jax.ShapeDtypeStruct((queries, 1), jnp.float32),
        ],
        compiler_params=params,
        cost_estimate=pl.CostEstimate(
            flops=4 * queries * window * width,
            bytes_accessed=2 * (2 * window + 2 * queries) * 128,
            transcendentals=queries * window,
        ),
    )
    return forward


def padded_columns(matrix, width):
    return jnp.pad(matrix, ((0, 0), (0, width - matrix.shape[1])))


def tokens_travel(
    patches,
    lengths,
    ln1_gain,
    ln1_bias,
    q_weight,
    q_bias,
    k_weight,
    v_weight,
    v_bias,
    o_weight,
    o_bias,
    ln2_gain,
    ln2_bias,
    up_weight,
    up_bias,
    down_weight,
    down_bias,
    gate_proj,
    up_proj,
    down_proj,
    ctx_gain,
    rk_weight,
    rv_weight,
    latents,
    lat_gain,
    rq_weight,
    ro_weight,
    feat_grad,
    lat_grad,
):
    low = jnp.bfloat16
    rows, width = patches.shape
    half = rows // 2
    n = lax.axis_size("seq")
    me = lax.axis_index("seq")
    core = lax.axis_index("tp")
    total_rows = rows * n
    longest = min(IMGMAX, (n // 2 - 1) * rows)
    heads = q_bias.shape[0] // HD
    part = me // heads
    queries = total_rows // 2
    window = total_rows - longest
    window_start = part * longest
    query_start = part * (queries - longest)
    scaling = HD ** (-0.5)
    kv_heads = rk_weight.shape[1] // RHD
    q_heads = rq_weight.shape[1] // RHD
    group = q_heads // kv_heads
    lat_rows = latents.shape[0]
    lat_scaling = RHD ** (-0.5)
    first_block = (me == 0).astype(jnp.float32)
    shard = q_weight.shape[0]
    hidden_units = up_bias.shape[0]
    hidden_pad = -(-hidden_units // 128) * 128
    proj_units = gate_proj.shape[1] // n
    own_width = heads * HD
    unit_lanes = -(-proj_units // 128) * 128
    out_width = down_proj.shape[1] * n

    def my_half(value):
        return lax.dynamic_slice_in_dim(value, core * half, half, 0)

    input_f32 = patches.astype(jnp.float32)
    normed_in = layer_norm(input_f32, ln1_gain, ln1_bias).astype(low)
    lanes = -(-HD // 128) * 128

    def wide(heads_of):
        return jnp.pad(heads_of, [(0, 0)] * (heads_of.ndim - 1) + [(0, lanes - HD)])

    def compact(parts):
        joined = jnp.concatenate([p[..., :HD] for p in parts], axis=-1)
        room = -(-joined.shape[-1] // 128) * 128 - joined.shape[-1]
        return jnp.pad(joined, [(0, 0)] * (joined.ndim - 1) + [(0, room)])

    head_shard = compact([split_heads(w, heads) for w in (q_weight, k_weight, v_weight)])
    normed_half, head_weight = gathered_beside(
        my_half(normed_in), jnp.concatenate([head_shard] * 2, axis=0), 2, reach=window // rows
    )

    unit_weights = jnp.stack([gate_proj, up_proj]).reshape(2, shard, n, proj_units)
    unit_weights = jnp.pad(unit_weights, ((0, 0),) * 3 + ((0, unit_lanes - proj_units),))
    ctx_width = rk_weight.shape[1]
    ctx_shard = jnp.concatenate([rk_weight, rv_weight], axis=1)
    unit_weights, normed_half, head_weight, ctx_shard = lax.optimization_barrier(
        (unit_weights.transpose(2, 0, 1, 3), normed_half, head_weight, ctx_shard)
    )
    w_ctx = lax.all_gather(ctx_shard, "seq", axis=0, tiled=True)
    w_ctxkey, w_ctxval = w_ctx[:, :ctx_width], w_ctx[:, ctx_width:]
    unit_weights = lax.all_to_all(unit_weights, "seq", 0, 0)
    normed_half = lax.dynamic_slice_in_dim(normed_half, window_start // rows, window // rows, 0)
    normed_window = in_order(
        normed_half[:, None], swapped(normed_half)[:, None], 1
    ).reshape(window, width)
    head_weight = head_weight.reshape(width, -1)
    head_weight = jnp.concatenate(
        [wide(head_weight[:, i * HD : (i + 1) * HD]) for i in range(3)], axis=1
    )
    head = me - part * heads
    q_bias_one = lax.dynamic_slice_in_dim(q_bias, head * HD, HD, 0)
    v_bias_one = lax.dynamic_slice_in_dim(v_bias, head * HD, HD, 0)
    bias_one = jnp.concatenate(
        [wide(q_bias_one), jnp.zeros((lanes,), jnp.float32), wide(v_bias_one)]
    )
    qkv = (product(normed_window, head_weight) + bias_one).astype(low)
    query_one = lax.dynamic_slice_in_dim(qkv[:, :lanes], query_start, queries, 0)
    key_one = qkv[:, lanes : 2 * lanes]
    value_one = qkv[:, 2 * lanes :]
    key_ids = image_ids(
        lengths, window_start + jnp.arange(window, dtype=jnp.int32), total_rows
    )
    query_ids = lax.dynamic_slice_in_dim(key_ids, query_start, queries, 0)[:, None]
    key_ids = key_ids[None, :]
    attend = attention_call(queries, window, lanes, rows, scaling)
    attended_one, lse_one = attend(query_one, key_one, value_one, query_ids, key_ids)
    attended_low = join_heads(
        exchanged([attended_one.reshape(heads, rows, lanes)], 3)[0][:, :, :HD]
    )

    vision_shard = jnp.concatenate(
        [
            padded_columns(up_weight, hidden_pad),
            padded_columns(down_weight.T, hidden_pad),
            o_weight.T,
        ],
        axis=1,
    )
    unit_weights, vision_shard, attended_low, down_proj = lax.optimization_barrier(
        (unit_weights, vision_shard, attended_low, down_proj)
    )
    vision, down_mine = gathered_beside(vision_shard, down_proj.reshape(n, proj_units, -1), 17)
    vision = vision.reshape(width, -1)
    down_other = swapped(down_mine)
    w_up = vision[:, :hidden_units]
    w_down_t = vision[:, hidden_pad : hidden_pad + hidden_units]
    w_out_t = vision[:, 2 * hidden_pad :]
    unit_weights = unit_weights.transpose(1, 0, 2, 3).reshape(2, width, unit_lanes)
    w_gate, w_up_proj = jnp.concatenate([unit_weights, swapped(unit_weights)], axis=2)

    attn_part = product_nt(attended_low, w_out_t)
    attn_sum = attn_part + swapped(attn_part)
    after_attn = input_f32 + attn_sum + o_bias
    mlp_in = layer_norm(after_attn, ln2_gain, ln2_bias).astype(low)
    hidden = product(mlp_in, w_up) + up_bias
    active_low = gelu_tanh(hidden).astype(low)
    after_mlp = after_attn + paired(product_nt(active_low, w_down_t)) + down_bias
    features = after_mlp.astype(low)

    features_all, proj_gate, proj_up, proj_hidden = gathered_units(
        my_half(features), w_gate, w_up_proj, 4
    )

    def joined_chunks(sums):
        return sums.transpose(1, 0, 2).reshape(half, -1)

    proj_out_low = joined_chunks(scattered_down(proj_hidden, down_mine, down_other, 5))
    proj_out_half = proj_out_low.astype(jnp.float32)
    proj_out = in_order(proj_out_low, swapped(proj_out_low), 0).astype(jnp.float32)
    qkv_shard, _ = lax.optimization_barrier(
        (jnp.concatenate([q_weight, k_weight, v_weight], axis=1), proj_out_low)
    )
    w_qkv = lax.all_gather(qkv_shard, "seq", axis=0, tiled=True)

    context_low = rms_norm(proj_out, ctx_gain).astype(low)
    ctx_keys = product(context_low, w_ctxkey).astype(low)
    ctx_values = product(context_low, w_ctxval).astype(low)
    lat_normed = rms_norm(latents, lat_gain).astype(low)
    lat_queries = product(lat_normed, rq_weight).astype(low)
    lat_keys = product(lat_normed, w_ctxkey).astype(low)
    lat_values = product(lat_normed, w_ctxval).astype(low)
    query_grouped = lat_queries.reshape(lat_rows, kv_heads, group, RHD)
    key_grouped = ctx_keys.reshape(rows, kv_heads, RHD)
    value_grouped = ctx_values.reshape(rows, kv_heads, RHD)
    self_keys = lat_keys.reshape(lat_rows, kv_heads, RHD)
    self_values = lat_values.reshape(lat_rows, kv_heads, RHD)
    lat_scores = (
        jnp.einsum("lkgd,tkd->kglt", query_grouped, key_grouped, preferred_element_type=jnp.float32)
        * lat_scaling
    )
    self_scores = (
        jnp.einsum("lkgd,tkd->kglt", query_grouped, self_keys, preferred_element_type=jnp.float32)
        * lat_scaling
    )
    stats = partial_stats(lat_scores, value_grouped)
    packed = jnp.concatenate([stats[2], stats[0][..., None], stats[1][..., None]], axis=-1)
    packed = jnp.pad(packed.reshape(n, -1, RHD + 2), ((0, 0), (0, 0), (0, 126 - RHD)))
    merged = reduced(packed, softmax_shares, 6).reshape(kv_heads, group, lat_rows, 128)
    lat_peak, lat_total, lat_numer = joint_stats(
        (merged[..., RHD], merged[..., RHD + 1], merged[..., :RHD]),
        partial_stats(self_scores, self_values),
    )
    lat_lse = lat_peak + jnp.log(lat_total)
    pooled_exact = lat_numer / lat_total[..., None]
    pooled_low = pooled_exact.transpose(2, 0, 1, 3).reshape(lat_rows, -1).astype(low)
    pooled_grad = product_nt(lat_grad, ro_weight).astype(low)
    pooled_grouped = pooled_grad.reshape(lat_rows, kv_heads, group, RHD)
    pooled_f32 = pooled_grouped.astype(jnp.float32)
    lat_delta = jnp.sum(pooled_f32.transpose(1, 2, 0, 3) * pooled_exact, axis=-1)

    def score_grads(scores, key_part, value_part):
        probability = jnp.exp(scores - lat_lse[..., None])
        dprob = jnp.einsum(
            "lkgd,tkd->kglt", pooled_grouped, value_part, preferred_element_type=jnp.float32
        )
        dscore = (probability * (dprob - lat_delta[..., None])).astype(low)
        query_term = (
            jnp.einsum("kglt,tkd->lkgd", dscore, key_part, preferred_element_type=jnp.float32)
            * lat_scaling
        )
        key_term = (
            jnp.einsum("kglt,lkgd->tkd", dscore, query_grouped, preferred_element_type=jnp.float32)
            * lat_scaling
        ).astype(low)
        value_term = jnp.einsum(
            "kglt,lkgd->tkd", probability, pooled_f32, precision=lax.Precision.HIGHEST
        ).astype(low)
        return (
            query_term,
            key_term.reshape(key_part.shape[0], -1),
            value_term.reshape(key_part.shape[0], -1),
        )

    ctx_query_term, ctx_keys_grad, ctx_values_grad = score_grads(
        lat_scores, key_grouped, value_grouped
    )
    self_query_term, self_keys_grad, self_values_grad = score_grads(
        self_scores, self_keys, self_values
    )
    ctx_part = product_nt(ctx_keys_grad, w_ctxkey) + product_nt(ctx_values_grad, w_ctxval)
    ctx_kept = rounded(my_half(ctx_part))
    ctx_sent = lax.dynamic_slice_in_dim(ctx_part, (1 - core) * half, half, 0).astype(low)
    ctx_back = ctx_kept + swapped(ctx_sent).astype(jnp.float32)
    ctx_pull = jax.vjp(rms_norm, proj_out_half, ctx_gain)[1]
    proj_out_grad, ctx_gain_part = ctx_pull(ctx_back)
    ctx_grads = jnp.concatenate([ctx_keys_grad, ctx_values_grad], axis=1)
    self_grads = jnp.concatenate([self_keys_grad, self_values_grad], axis=1)
    r_part = product_tn(context_low, ctx_grads) + first_block * product_tn(lat_normed, self_grads)
    r_part, proj_out_grad = lax.optimization_barrier((r_part.astype(low), proj_out_grad))
    r_grad = lax.psum_scatter(r_part, "seq", scatter_dimension=0, tiled=True).astype(jnp.float32)
    _, feat_terms, units_mine, units_other, downs_mine, downs_other = gathered_back(
        proj_out_grad.astype(low),
        w_gate,
        w_up_proj,
        down_mine,
        down_other,
        features_all,
        proj_gate,
        proj_up,
        width // 128,
        8,
    )

    query_part = ctx_query_term + first_block * self_query_term
    feat_half = joined_chunks(scattered_sum(feat_terms, 11))

    proj_in_grad = in_order(feat_half, swapped(feat_half), 0).astype(jnp.float32)
    def core_sum(mine, other):
        return (mine.astype(jnp.float32) + swapped(other).astype(jnp.float32)).astype(low)

    down_blocks = core_sum(downs_mine, downs_other)
    unit_blocks = core_sum(units_mine, units_other)
    unit_blocks = unit_blocks.reshape(n, 2 * shard, unit_lanes)

    mlp_out_grad = feat_grad.astype(jnp.float32) + proj_in_grad
    mlp_out_low = mlp_out_grad.astype(low)
    down_bias_part = jnp.sum(mlp_out_low.astype(jnp.float32), axis=0)
    active_grad = product(mlp_out_low, w_down_t)
    gelu_pull = jax.vjp(gelu_tanh, hidden)[1]
    hidden_grad = gelu_pull(active_grad)[0].astype(low)
    up_bias_part = jnp.sum(hidden_grad.astype(jnp.float32), axis=0)
    mlp_back = paired(product_nt(hidden_grad, w_up))
    ln2_pull = jax.vjp(layer_norm, after_attn, ln2_gain, ln2_bias)[1]
    norm_grad, ln2_gain_part, ln2_bias_part = ln2_pull(mlp_back)
    attn_out_grad = mlp_out_grad + norm_grad
    attn_out_low = attn_out_grad.astype(low)
    o_bias_part = jnp.sum(attn_out_low.astype(jnp.float32), axis=0)
    vision_chunks = 13
    vision_width = 2 * hidden_pad + own_width
    vision_cols = -(-vision_width // (vision_chunks * 128)) * 128
    vision_left = jnp.stack([mlp_in.T, mlp_out_low.T, attn_out_low.T])
    vision_right = jnp.concatenate(
        [
            padded_columns(hidden_grad, hidden_pad),
            padded_columns(active_low, hidden_pad),
            padded_columns(attended_low, vision_chunks * vision_cols - 2 * hidden_pad),
        ],
        axis=1,
    )
    spans = (0, hidden_pad // 128, 2 * hidden_pad // 128)
    attended_grad = product(attn_out_low, w_out_t).astype(low)
    grad_one = exchanged([wide(split_heads(attended_grad, heads))], 12)[0].reshape(queries, lanes)
    vision_grad, dq, dk, dv = scattered_vision(
        vision_left,
        vision_right,
        (query_one, key_one, value_one, grad_one, query_ids, key_ids, lse_one),
        scaling,
        spans,
        vision_chunks,
        18,
    )
    dq_window = lax.dynamic_update_slice_in_dim(
        jnp.zeros((window, lanes), jnp.float32), dq, query_start, 0
    )
    dqkv = compact([dq_window, dk, dv])
    dqkv_low = dqkv.astype(low)
    head_grad = product_tn(normed_window, dqkv_low).astype(low).reshape(n, shard, -1)
    bias_row = jnp.sum(dqkv_low.astype(jnp.float32), axis=0)
    bias_rows = jnp.zeros((heads, dqkv.shape[1]), jnp.float32)
    bias_rows = lax.dynamic_update_slice_in_dim(bias_rows, bias_row[None], head, 0)
    blocks = dqkv.reshape(window // rows, rows, -1)
    other_block = jnp.where(part == 0, blocks[-1], blocks[0]).astype(low)
    across = lax.ppermute(
        other_block, "seq", [(i, (i + heads) % n) for i in range(n)]
    ).astype(jnp.float32)
    own_blocks = lax.dynamic_slice_in_dim(blocks, part, heads, 0)
    edge = jnp.where(part == 0, heads - 1, 0)
    own_blocks = own_blocks + jnp.where(
        (jnp.arange(heads) == edge)[:, None, None], across[None], 0.0
    )
    head_grads, token_grads = exchanged([head_grad, own_blocks.astype(low)], 13)
    head_grads, token_grads, unit_blocks = lax.optimization_barrier(
        (head_grads, token_grads, unit_blocks)
    )
    unit_rows = lax.all_to_all(unit_blocks, "seq", 0, 0)
    queries_grad, keys_grad, values_grad = (
        join_heads(token_grads[:, :, i * HD : (i + 1) * HD]) for i in range(3)
    )
    attn_back = paired(
        product_nt(jnp.concatenate([queries_grad, keys_grad, values_grad], axis=1), w_qkv)
    )
    ln1_pull = jax.vjp(layer_norm, input_f32, ln1_gain, ln1_bias)[1]
    in_grad, ln1_gain_part, ln1_bias_part = ln1_pull(attn_back)
    patches_grad = (attn_out_grad + in_grad).astype(low)

    smalls = (
        ln1_gain_part,
        ln1_bias_part,
        bias_rows[:, :HD].reshape(-1),
        bias_rows[:, 2 * HD : 3 * HD].reshape(-1),
        o_bias_part,
        ln2_gain_part,
        ln2_bias_part,
        up_bias_part,
        down_bias_part,
        ctx_gain_part,
    )
    pieces = [
        jnp.pad(small, (0, -small.shape[0] % 1024)) for small in smalls + (query_part.reshape(-1),)
    ]
    begins = [sum(p.shape[0] for p in pieces[:i]) for i in range(len(pieces))]
    joined_smalls = jnp.concatenate(pieces)
    length = joined_smalls.shape[0]
    per_device = -(-length // (n * 1024)) * 1024
    joined_smalls = jnp.pad(joined_smalls, (0, n * per_device - length))
    small_sum = reduced(joined_smalls.reshape(n, per_device // 128, 128), added, 15).reshape(-1)
    (
        small_sum,
        down_blocks,
        unit_rows,
        vision_grad,
        head_grads,
        pooled_late,
        self_grads,
    ) = lax.optimization_barrier(
        (small_sum, down_blocks, unit_rows, vision_grad, head_grads, pooled_low, self_grads)
    )
    down_rows = lax.all_to_all(down_blocks, "seq", 0, 0)
    vision_grad = vision_grad.transpose(1, 0, 2).reshape(shard, -1).astype(jnp.float32)
    up_weight_grad = vision_grad[:, :hidden_units]
    down_weight_grad = vision_grad[:, hidden_pad : hidden_pad + hidden_units].T
    o_weight_grad = vision_grad[:, 2 * hidden_pad : vision_width].T
    head_grads = head_grads.astype(jnp.float32)
    head_grads = head_grads[:heads] + head_grads[heads:]
    q_weight_grad, k_weight_grad, v_weight_grad = (
        join_heads(head_grads[:, :, i * HD : (i + 1) * HD]) for i in range(3)
    )
    lat_mix = product(pooled_late, ro_weight)
    ro_width = ro_weight.shape[1] // n
    ro_columns = lax.dynamic_slice_in_dim(lat_grad, me * ro_width, ro_width, 1)
    ro_weight_grad = product_tn(pooled_late, ro_columns)
    small_sums = [
        small_sum[begin : begin + small.shape[0]] for begin, small in zip(begins, smalls)
    ]
    ctx_gain_grad = small_sums[9] + swapped(small_sums[9])

    query_sum = small_sum[begins[-1] : begins[-1] + query_part.size].reshape(lat_rows, -1)
    lat_queries_grad = query_sum.astype(low)
    rq_rows = rq_weight.shape[0] // n
    rq_weight_grad = product_tn(
        lax.dynamic_slice_in_dim(lat_normed, me * rq_rows, rq_rows, 1), lat_queries_grad
    )
    lat_part = product_nt(lat_queries_grad, rq_weight) + product_nt(self_grads, w_ctx)
    down_proj_grad = down_rows.reshape(n * proj_units, -1).astype(jnp.float32)
    unit_rows = unit_rows.reshape(n, 2, shard, unit_lanes)[..., :proj_units]
    gate_proj_grad, up_proj_grad = (
        unit_rows.transpose(1, 2, 0, 3).reshape(2, shard, n * proj_units).astype(jnp.float32)
    )
    lat_back, lat_mix_sum = paired(lat_part), paired(lat_mix)
    latents_out = latents + lat_mix_sum
    lat_pull = jax.vjp(rms_norm, latents, lat_gain)[1]
    lat_in_grad, lat_gain_grad = lat_pull(lat_back)
    latents_grad = lat_grad.astype(jnp.float32) + lat_in_grad
    return (
        features,
        latents_out,
        patches_grad,
        latents_grad,
        small_sums[0],
        small_sums[1],
        q_weight_grad,
        small_sums[2],
        k_weight_grad,
        v_weight_grad,
        small_sums[3],
        o_weight_grad,
        small_sums[4],
        small_sums[5],
        small_sums[6],
        up_weight_grad,
        small_sums[7],
        down_weight_grad,
        small_sums[8],
        gate_proj_grad,
        up_proj_grad,
        down_proj_grad,
        ctx_gain_grad,
        r_grad[:, :ctx_width],
        r_grad[:, ctx_width:],
        lat_gain_grad,
        rq_weight_grad,
        ro_weight_grad,
    )


def solution(mesh):
    placed = (
        P("seq", None),
        P(),
        P(),
        P(),
        P("seq", "tp"),
        P("tp"),
        P("seq", "tp"),
        P("seq", "tp"),
        P("tp"),
        P("tp", "seq"),
        P(),
        P(),
        P(),
        P("seq", "tp"),
        P("tp"),
        P("tp", "seq"),
        P(),
        P("seq", "tp"),
        P("seq", "tp"),
        P("tp", "seq"),
        P(),
        P("seq", "tp"),
        P("seq", "tp"),
        P(),
        P(),
        P(None, "tp"),
        P("tp", None),
        P("seq", None),
        P(),
    )
    few = mesh.shape["tp"] == 2 and mesh.shape["seq"] == 16
    return jax.shard_map(
        tokens_travel if few else weights_travel,
        mesh=mesh,
        in_specs=placed,
        out_specs=(
            P("seq", None),
            P(),
            P("seq", None),
            P(),
            P(),
            P(),
            P("seq", "tp"),
            P("tp"),
            P("seq", "tp"),
            P("seq", "tp"),
            P("tp"),
            P("tp", "seq"),
            P(),
            P(),
            P(),
            P("seq", "tp"),
            P("tp"),
            P("tp", "seq"),
            P(),
            P("seq", "tp"),
            P("seq", "tp"),
            P("tp", "seq"),
            P(),
            P("seq", "tp"),
            P("seq", "tp"),
            P(),
            P("seq", "tp"),
            P("tp", "seq"),
        ),
        check_vma=False,
    )
```

```python
import functools

import jax
import jax.experimental.pallas as pl
import jax.experimental.pallas.tpu as pltpu
import jax.numpy as jnp
from jax import lax
from jax.sharding import PartitionSpec as P

HD = 72
RHD = 96
IMGMAX = 4900


EPS = 1e-06


def passed_along(value, axis, steps):
    count = lax.axis_size(axis)
    first, last = (max(0, -steps), min(count, count - steps))
    return lax.ppermute(value, axis, [(source, source + steps) for source in range(first, last)])


def joined(part, axis, combine):
    gathered = jax.tree.map(lambda a: lax.all_gather(a, axis), part)

    def take(source):
        return jax.tree.map(lambda a: lax.dynamic_index_in_dim(a, source, 0, False), gathered)

    return lax.fori_loop(
        1, lax.axis_size(axis), lambda source, state: combine(state, take(source)), take(0)
    )


def layer_norm(value, gain, bias):
    centred = value - jnp.mean(value, axis=-1, keepdims=True)
    return (
        centred * lax.rsqrt(jnp.mean(centred * centred, axis=-1, keepdims=True) + EPS) * gain + bias
    )


def rms_norm(value, gain):
    return value * lax.rsqrt(jnp.mean(value * value, axis=-1, keepdims=True) + EPS) * gain


def gelu_tanh(value):
    return jax.nn.gelu(value, approximate=True)


def product(left, right):
    return jnp.dot(left, right, preferred_element_type=jnp.float32)


def product_nt(left, right):
    return lax.dot_general(
        left, right, (((1,), (1,)), ((), ())), preferred_element_type=jnp.float32
    )


def product_tn(left, right):
    return lax.dot_general(
        left, right, (((0,), (0,)), ((), ())), preferred_element_type=jnp.float32
    )


def image_ids(lengths, positions, total_rows):
    image_ends = jnp.cumsum(lengths)
    counted = jnp.sum((image_ends[None, :] <= positions[:, None]).astype(jnp.int32), axis=1)
    inside = (positions >= 0) & (positions < total_rows)
    return jnp.where(inside, counted, -1)


def split_heads(matrix, count):
    return matrix.reshape(matrix.shape[0], count, -1).transpose(1, 0, 2)


def join_heads(stacked):
    return stacked.transpose(1, 0, 2).reshape(stacked.shape[1], -1)


def neighbour(first, second, offset):
    return passed_along((first, second), "seq", offset)


def returned(first, second, offset):
    return (
        passed_along(first.astype(jnp.bfloat16), "seq", offset).astype(first.dtype),
        passed_along(second.astype(jnp.bfloat16), "seq", offset).astype(second.dtype),
    )


def partial_stats(scores, value_heads):
    peak = jnp.max(scores, axis=-1)
    weights = jnp.exp(scores - peak[..., None])
    total = jnp.sum(weights, axis=-1)
    numer = jnp.einsum(
        "kglt,tkd->kgld", weights, value_heads.astype(jnp.float32), precision=lax.Precision.HIGHEST
    )
    return (peak, total, numer)


def joint_stats(left, right):
    peak = jnp.maximum(left[0], right[0])
    left_scale = jnp.exp(left[0] - peak)
    right_scale = jnp.exp(right[0] - peak)
    total = left[1] * left_scale + right[1] * right_scale
    numer = left[2] * left_scale[..., None] + right[2] * right_scale[..., None]
    return (peak, total, numer)


def weights_travel(
    patches,
    lengths,
    ln1_gain,
    ln1_bias,
    q_weight,
    q_bias,
    k_weight,
    v_weight,
    v_bias,
    o_weight,
    o_bias,
    ln2_gain,
    ln2_bias,
    up_weight,
    up_bias,
    down_weight,
    down_bias,
    gate_proj,
    up_proj,
    down_proj,
    ctx_gain,
    rk_weight,
    rv_weight,
    latents,
    lat_gain,
    rq_weight,
    ro_weight,
    feat_grad,
    lat_grad,
):
    tok_rows = patches.shape[0]
    seq_count = lax.axis_size("seq")
    seq_place = lax.axis_index("seq")
    total_rows = tok_rows * seq_count
    longest = min(IMGMAX, (seq_count // 2 - 1) * tok_rows)
    reach_blocks = (longest + tok_rows - 2) // tok_rows
    local_heads = q_bias.shape[0] // HD
    kv_heads = rk_weight.shape[1] // RHD
    q_heads = rq_weight.shape[1] // RHD
    group = q_heads // kv_heads
    lat_rows = latents.shape[0]
    scaling = HD ** (-0.5)
    lat_scaling = RHD ** (-0.5)
    first_block = (seq_place == 0).astype(jnp.float32)
    gathered = (
        lax.all_gather(q_weight, "seq", axis=0, tiled=True),
        lax.all_gather(k_weight, "seq", axis=0, tiled=True),
        lax.all_gather(v_weight, "seq", axis=0, tiled=True),
        lax.all_gather(o_weight, "seq", axis=1, tiled=True),
        lax.all_gather(up_weight, "seq", axis=0, tiled=True),
        lax.all_gather(down_weight, "seq", axis=1, tiled=True),
        lax.all_gather(gate_proj, "seq", axis=0, tiled=True),
        lax.all_gather(up_proj, "seq", axis=0, tiled=True),
        lax.all_gather(down_proj, "seq", axis=1, tiled=True),
        lax.all_gather(rk_weight, "seq", axis=0, tiled=True),
        lax.all_gather(rv_weight, "seq", axis=0, tiled=True),
    )
    (
        w_query,
        w_key,
        w_value,
        w_out,
        w_up,
        w_down,
        w_gate_proj,
        w_up_proj,
        w_down_proj,
        w_ctxkey,
        w_ctxval,
    ) = gathered
    input_f32 = patches.astype(jnp.float32)
    normed_in = layer_norm(input_f32, ln1_gain, ln1_bias).astype(jnp.bfloat16)
    queries_low = (product(normed_in, w_query) + q_bias).astype(jnp.bfloat16)
    keys_low = product(normed_in, w_key).astype(jnp.bfloat16)
    values_low = (product(normed_in, w_value) + v_bias).astype(jnp.bfloat16)
    upper_pairs = []
    lower_pairs = []
    upper_pair = (keys_low, values_low)
    lower_pair = (keys_low, values_low)
    for distance in range(1, reach_blocks + 1):
        upper_pair = neighbour(upper_pair[0], upper_pair[1], -1)
        lower_pair = neighbour(lower_pair[0], lower_pair[1], 1)
        upper_pairs.append(upper_pair)
        lower_pairs.append(lower_pair)
    ordered = lower_pairs[::-1] + [(keys_low, values_low)] + upper_pairs
    key_buffer = jnp.concatenate([pair[0] for pair in ordered], axis=0)
    value_buffer = jnp.concatenate([pair[1] for pair in ordered], axis=0)
    own_positions = seq_place * tok_rows + jnp.arange(tok_rows, dtype=jnp.int32)
    query_ids = image_ids(lengths, own_positions, total_rows)
    key_positions = (seq_place - reach_blocks) * tok_rows + jnp.arange(
        (2 * reach_blocks + 1) * tok_rows, dtype=jnp.int32
    )
    key_ids = image_ids(lengths, key_positions, total_rows)
    allowed = query_ids[:, None] == key_ids[None, :]
    query_heads = split_heads(queries_low, local_heads)
    key_heads = split_heads(key_buffer, local_heads)
    value_heads = split_heads(value_buffer, local_heads)

    def head_forward(operands):
        query_one, key_one, value_one = operands
        scores = jnp.where(allowed, product_nt(query_one, key_one) * scaling, -1e30)
        peak = jnp.max(scores, axis=1, keepdims=True)
        exponent = jnp.exp(scores - peak)
        total_exp = jnp.sum(exponent, axis=1, keepdims=True)
        probability = exponent / total_exp
        result = product(probability.astype(jnp.bfloat16), value_one)
        return (result, peak[:, 0] + jnp.log(total_exp[:, 0]))

    head_result, head_lse = lax.map(head_forward, (query_heads, key_heads, value_heads))
    attended_low = join_heads(head_result).astype(jnp.bfloat16)
    attn_sum = lax.psum(product(attended_low, w_out), "tp")
    after_attn = input_f32 + attn_sum + o_bias
    mlp_in = layer_norm(after_attn, ln2_gain, ln2_bias).astype(jnp.bfloat16)
    hidden = product(mlp_in, w_up) + up_bias
    active_low = gelu_tanh(hidden).astype(jnp.bfloat16)
    mlp_sum = lax.psum(product(active_low, w_down).astype(jnp.bfloat16), "tp").astype(jnp.float32)
    after_mlp = after_attn + mlp_sum + down_bias
    features = after_mlp.astype(jnp.bfloat16)
    proj_gate = product(features, w_gate_proj)
    proj_up = product(features, w_up_proj)
    silu_gate = jax.nn.silu(proj_gate)
    proj_hidden = (silu_gate * proj_up).astype(jnp.bfloat16)
    proj_out = lax.psum(product(proj_hidden, w_down_proj).astype(jnp.bfloat16), "tp").astype(
        jnp.float32
    )
    context_low = rms_norm(proj_out, ctx_gain).astype(jnp.bfloat16)
    ctx_keys = product(context_low, w_ctxkey).astype(jnp.bfloat16)
    ctx_values = product(context_low, w_ctxval).astype(jnp.bfloat16)
    lat_normed = rms_norm(latents, lat_gain).astype(jnp.bfloat16)
    lat_queries = product(lat_normed, rq_weight).astype(jnp.bfloat16)
    lat_keys = product(lat_normed, w_ctxkey).astype(jnp.bfloat16)
    lat_values = product(lat_normed, w_ctxval).astype(jnp.bfloat16)
    query_grouped = lat_queries.reshape(lat_rows, kv_heads, group, RHD)
    key_grouped = ctx_keys.reshape(tok_rows, kv_heads, RHD)
    value_grouped = ctx_values.reshape(tok_rows, kv_heads, RHD)
    self_keys = lat_keys.reshape(lat_rows, kv_heads, RHD)
    self_values = lat_values.reshape(lat_rows, kv_heads, RHD)
    lat_scores = (
        jnp.einsum("lkgd,tkd->kglt", query_grouped, key_grouped, preferred_element_type=jnp.float32)
        * lat_scaling
    )
    self_scores = (
        jnp.einsum("lkgd,tkd->kglt", query_grouped, self_keys, preferred_element_type=jnp.float32)
        * lat_scaling
    )
    merged = joined(partial_stats(lat_scores, value_grouped), "seq", joint_stats)
    lat_peak, lat_total, lat_numer = joint_stats(merged, partial_stats(self_scores, self_values))
    lat_lse = lat_peak + jnp.log(lat_total)
    pooled_exact = lat_numer / lat_total[..., None]
    pooled_low = pooled_exact.transpose(2, 0, 1, 3).reshape(lat_rows, -1).astype(jnp.bfloat16)
    lat_mix = product(pooled_low, ro_weight)
    ro_width = ro_weight.shape[1] // seq_count
    ro_columns = lax.dynamic_slice_in_dim(lat_grad, seq_place * ro_width, ro_width, 1)
    ro_weight_grad = product_tn(pooled_low, ro_columns)
    pooled_grad = product_nt(lat_grad, ro_weight).astype(jnp.bfloat16)
    pooled_grouped = pooled_grad.reshape(lat_rows, kv_heads, group, RHD)
    pooled_f32 = pooled_grouped.astype(jnp.float32)
    lat_delta = jnp.sum(pooled_f32.transpose(1, 2, 0, 3) * pooled_exact, axis=-1)

    def score_grads(scores, key_part, value_part):
        probability = jnp.exp(scores - lat_lse[..., None])
        dprob = jnp.einsum(
            "lkgd,tkd->kglt", pooled_grouped, value_part, preferred_element_type=jnp.float32
        )
        dscore = (probability * (dprob - lat_delta[..., None])).astype(jnp.bfloat16)
        query_term = (
            jnp.einsum("kglt,tkd->lkgd", dscore, key_part, preferred_element_type=jnp.float32)
            * lat_scaling
        )
        key_term = (
            jnp.einsum("kglt,lkgd->tkd", dscore, query_grouped, preferred_element_type=jnp.float32)
            * lat_scaling
        ).astype(jnp.bfloat16)
        value_term = jnp.einsum(
            "kglt,lkgd->tkd", probability, pooled_f32, precision=lax.Precision.HIGHEST
        ).astype(jnp.bfloat16)
        return (
            query_term,
            key_term.reshape(key_part.shape[0], -1),
            value_term.reshape(key_part.shape[0], -1),
        )

    ctx_query_term, ctx_keys_grad, ctx_values_grad = score_grads(
        lat_scores, key_grouped, value_grouped
    )
    self_query_term, self_keys_grad, self_values_grad = score_grads(
        self_scores, self_keys, self_values
    )
    query_part = ctx_query_term + first_block * self_query_term
    query_sum = lax.psum(query_part, "seq")
    lat_queries_grad = query_sum.reshape(lat_rows, -1).astype(jnp.bfloat16)
    rq_rows = rq_weight.shape[0] // seq_count
    rq_weight_grad = product_tn(
        lax.dynamic_slice_in_dim(lat_normed, seq_place * rq_rows, rq_rows, 1), lat_queries_grad
    )
    rk_part = product_tn(context_low, ctx_keys_grad) + first_block * product_tn(
        lat_normed, self_keys_grad
    )
    rv_part = product_tn(context_low, ctx_values_grad) + first_block * product_tn(
        lat_normed, self_values_grad
    )
    ctx_part = product_nt(ctx_keys_grad, w_ctxkey) + product_nt(ctx_values_grad, w_ctxval)
    lat_part = (
        product_nt(lat_queries_grad, rq_weight)
        + product_nt(self_keys_grad, w_ctxkey)
        + product_nt(self_values_grad, w_ctxval)
    )
    ctx_back, lat_back, lat_mix_sum = (
        lax.psum(ctx_part.astype(jnp.bfloat16), "tp").astype(jnp.float32),
        lax.psum(lat_part.astype(jnp.bfloat16), "tp").astype(jnp.float32),
        lax.psum(lat_mix.astype(jnp.bfloat16), "tp").astype(jnp.float32),
    )
    latents_out = latents + lat_mix_sum
    lat_pull = jax.vjp(rms_norm, latents, lat_gain)[1]
    lat_in_grad, lat_gain_grad = lat_pull(lat_back)
    latents_grad = lat_grad.astype(jnp.float32) + lat_in_grad
    ctx_pull = jax.vjp(rms_norm, proj_out, ctx_gain)[1]
    proj_out_grad, ctx_gain_part = ctx_pull(ctx_back)
    proj_out_low = proj_out_grad.astype(jnp.bfloat16)
    down_proj_part = product_tn(proj_hidden, proj_out_low)
    hidden_pgrad = product_nt(proj_out_low, w_down_proj)
    silu_pull = jax.vjp(jax.nn.silu, proj_gate)[1]
    gate_grad_low = silu_pull(hidden_pgrad * proj_up)[0].astype(jnp.bfloat16)
    up_grad_low = (hidden_pgrad * silu_gate).astype(jnp.bfloat16)
    gate_proj_part = product_tn(features, gate_grad_low)
    up_proj_part = product_tn(features, up_grad_low)
    proj_in_grad = lax.psum(
        (product_nt(gate_grad_low, w_gate_proj) + product_nt(up_grad_low, w_up_proj)).astype(
            jnp.bfloat16
        ),
        "tp",
    ).astype(jnp.float32)
    mlp_out_grad = feat_grad.astype(jnp.float32) + proj_in_grad
    mlp_out_low = mlp_out_grad.astype(jnp.bfloat16)
    down_part = product_tn(active_low, mlp_out_low)
    down_bias_part = jnp.sum(mlp_out_low.astype(jnp.float32), axis=0)
    active_grad = product_nt(mlp_out_low, w_down)
    gelu_pull = jax.vjp(gelu_tanh, hidden)[1]
    hidden_grad = gelu_pull(active_grad)[0].astype(jnp.bfloat16)
    up_part = product_tn(mlp_in, hidden_grad)
    up_bias_part = jnp.sum(hidden_grad.astype(jnp.float32), axis=0)
    mlp_back = lax.psum(product_nt(hidden_grad, w_up).astype(jnp.bfloat16), "tp").astype(
        jnp.float32
    )
    ln2_pull = jax.vjp(layer_norm, after_attn, ln2_gain, ln2_bias)[1]
    norm_grad, ln2_gain_part, ln2_bias_part = ln2_pull(mlp_back)
    attn_out_grad = mlp_out_grad + norm_grad
    attn_out_low = attn_out_grad.astype(jnp.bfloat16)
    o_part = product_tn(attended_low, attn_out_low)
    o_bias_part = jnp.sum(attn_out_low.astype(jnp.float32), axis=0)
    attended_grad = product_nt(attn_out_low, w_out).astype(jnp.bfloat16)
    grad_heads = split_heads(attended_grad, local_heads)

    def head_backward(operands):
        query_one, key_one, value_one, grad_one, lse_one = operands
        scores = jnp.where(allowed, product_nt(query_one, key_one) * scaling, -1e30)
        probability = jnp.exp(scores - lse_one[:, None])
        dprob = product_nt(grad_one, value_one)
        row_inner = jnp.sum(probability * dprob, axis=1, keepdims=True)
        score_low = (probability * (dprob - row_inner)).astype(jnp.bfloat16)
        query_one_grad = product(score_low, key_one) * scaling
        key_one_grad = product_tn(score_low, query_one) * scaling
        value_one_grad = product_tn(probability.astype(jnp.bfloat16), grad_one)
        return (query_one_grad, key_one_grad, value_one_grad)

    query_hgrad, key_hgrad, value_hgrad = lax.map(
        head_backward, (query_heads, key_heads, value_heads, grad_heads, head_lse)
    )
    key_blocks = join_heads(key_hgrad).reshape(2 * reach_blocks + 1, tok_rows, -1)
    value_blocks = join_heads(value_hgrad).reshape(2 * reach_blocks + 1, tok_rows, -1)
    key_total = key_blocks[reach_blocks]
    value_total = value_blocks[reach_blocks]
    carry_upper = (key_blocks[2 * reach_blocks], value_blocks[2 * reach_blocks])
    carry_lower = (key_blocks[0], value_blocks[0])
    for distance in range(reach_blocks - 1, 0, -1):
        moved_upper = returned(carry_upper[0], carry_upper[1], 1)
        carry_upper = (
            moved_upper[0] + key_blocks[reach_blocks + distance],
            moved_upper[1] + value_blocks[reach_blocks + distance],
        )
        moved_lower = returned(carry_lower[0], carry_lower[1], -1)
        carry_lower = (
            moved_lower[0] + key_blocks[reach_blocks - distance],
            moved_lower[1] + value_blocks[reach_blocks - distance],
        )
    moved_upper = returned(carry_upper[0], carry_upper[1], 1)
    moved_lower = returned(carry_lower[0], carry_lower[1], -1)
    key_total = key_total + moved_upper[0] + moved_lower[0]
    value_total = value_total + moved_upper[1] + moved_lower[1]
    queries_grad = join_heads(query_hgrad).astype(jnp.bfloat16)
    keys_grad = key_total.astype(jnp.bfloat16)
    values_grad = value_total.astype(jnp.bfloat16)
    q_part = product_tn(normed_in, queries_grad)
    k_part = product_tn(normed_in, keys_grad)
    v_part = product_tn(normed_in, values_grad)
    q_bias_part = jnp.sum(queries_grad.astype(jnp.float32), axis=0)
    v_bias_part = jnp.sum(values_grad.astype(jnp.float32), axis=0)
    attn_back = lax.psum(
        (
            product_nt(queries_grad, w_query)
            + product_nt(keys_grad, w_key)
            + product_nt(values_grad, w_value)
        ).astype(jnp.bfloat16),
        "tp",
    ).astype(jnp.float32)
    ln1_pull = jax.vjp(layer_norm, input_f32, ln1_gain, ln1_bias)[1]
    in_grad, ln1_gain_part, ln1_bias_part = ln1_pull(attn_back)
    patches_grad = (attn_out_grad + in_grad).astype(jnp.bfloat16)
    weight_sums = (
        lax.psum_scatter(q_part, "seq", scatter_dimension=0, tiled=True),
        lax.psum_scatter(k_part, "seq", scatter_dimension=0, tiled=True),
        lax.psum_scatter(v_part, "seq", scatter_dimension=0, tiled=True),
        lax.psum_scatter(o_part, "seq", scatter_dimension=1, tiled=True),
        lax.psum_scatter(up_part, "seq", scatter_dimension=0, tiled=True),
        lax.psum_scatter(down_part, "seq", scatter_dimension=1, tiled=True),
        lax.psum_scatter(gate_proj_part, "seq", scatter_dimension=0, tiled=True),
        lax.psum_scatter(up_proj_part, "seq", scatter_dimension=0, tiled=True),
        lax.psum_scatter(down_proj_part, "seq", scatter_dimension=1, tiled=True),
        lax.psum_scatter(rk_part, "seq", scatter_dimension=0, tiled=True),
        lax.psum_scatter(rv_part, "seq", scatter_dimension=0, tiled=True),
    )
    small_sums = lax.psum(
        (
            ln1_gain_part,
            ln1_bias_part,
            q_bias_part,
            v_bias_part,
            o_bias_part,
            ln2_gain_part,
            ln2_bias_part,
            up_bias_part,
            down_bias_part,
            ctx_gain_part,
        ),
        "seq",
    )
    return (
        features,
        latents_out,
        patches_grad,
        latents_grad,
        small_sums[0],
        small_sums[1],
        weight_sums[0],
        small_sums[2],
        weight_sums[1],
        weight_sums[2],
        small_sums[3],
        weight_sums[3],
        small_sums[4],
        small_sums[5],
        small_sums[6],
        weight_sums[4],
        small_sums[7],
        weight_sums[5],
        small_sums[8],
        weight_sums[6],
        weight_sums[7],
        weight_sums[8],
        small_sums[9],
        weight_sums[9],
        weight_sums[10],
        lat_gain_grad,
        rq_weight_grad,
        ro_weight_grad,
    )


MESH = pl.DeviceIdType.MESH


def greet(partners):
    barrier = pltpu.get_barrier_semaphore()
    for present, device in partners:

        @pl.when(present)
        def _():
            pl.semaphore_signal(
                barrier, inc=1, device_id={"seq": device}, device_id_type=MESH
            )

    pl.semaphore_wait(barrier, sum(jnp.where(present, 1, 0) for present, _ in partners))


def place():
    me = lax.axis_index("seq")
    x, y, z = lax.rem(me, 2), lax.rem(lax.div(me, 2), 2), lax.div(me, 4)
    first = lax.axis_index("tp") == 0
    a, b = jnp.where(first, x, y), jnp.where(first, y, x)
    step_a, step_b = jnp.where(first, 1, 2), jnp.where(first, 2, 1)
    return me, z, a, b, step_a, step_b


def neighbours(layers):
    me, z, a, b, step_a, step_b = place()
    up, down = z < layers - 1, z > 0
    return (
        (up, jnp.where(up, me + 4, me)),
        (down, jnp.where(down, me - 4, me)),
        (me >= 0, me + step_a * (1 - 2 * a)),
        (me >= 0, me + step_b * (1 - 2 * b)),
    )


class Arrivals:
    def __init__(self, n, x_ref, slots, sent, landed, local, reach=None):
        self.n, self.layers, self.reach = n, n // 4, reach
        self.x_ref, self.slots, self.sent, self.landed = x_ref, slots, sent, landed
        self.me, self.z, self.a, self.b, self.step_a, self.step_b = place()
        self.partners = neighbours(self.layers)
        (self.up, self.to_up), (self.down, self.to_down) = self.partners[:2]
        self.to_a, self.to_b = self.partners[2][1], self.partners[3][1]
        self.own = pltpu.make_async_copy(x_ref, slots.at[self.me], local)

    def at(self, layer, of_a, of_b):
        return layer * 4 + of_a * self.step_a + of_b * self.step_b

    def wanted(self, slot, layer):
        if self.reach is None:
            return slot >= 0
        return jnp.where(
            layer < self.layers // 2, slot < self.reach, slot >= self.n - self.reach
        )

    def send(self, slot, device, way, source=None):
        return pltpu.make_async_remote_copy(
            src_ref=self.slots.at[slot] if source is None else source,
            dst_ref=self.slots.at[slot],
            send_sem=self.sent.at[way, slot],
            recv_sem=self.landed.at[slot],
            device_id={"seq": device},
            device_id_type=MESH,
        )

    def layer(self, k):
        z, last = self.z, self.layers - 1
        both = 2 * jnp.minimum(z, last - z)
        step = (k + 1) // 2
        near = jnp.where(k % 2 == 1, z - step, z + step)
        far = jnp.where(z < last - z, k, last - k)
        return jnp.where(k <= both, near, far)

    def block(self, i):
        last = 2 * self.layers - 1
        over_b = i // (2 * self.layers)
        j = i - over_b * 2 * self.layers
        over_a = jnp.where((j > 0) & ((j % 2 == 0) | (j == last)), 1, 0)
        nearness = jnp.where(over_a == 1, jnp.maximum(j - 1, 0) // 2, (j + 1) // 2)
        layer = self.layer(nearness)
        of_a = jnp.where(over_a == 1, 1 - self.a, self.a)
        of_b = jnp.where(over_b == 1, 1 - self.b, self.b)
        return layer, over_a, over_b, self.at(layer, of_a, of_b)

    def start(self, beside=None):
        if beside is None:
            greet(self.partners)
        else:
            beside.greet()
        self.own.start()
        me, x_ref = self.me, self.x_ref

        @pl.when(self.up & self.wanted(me, self.z + 1))
        def _():
            self.send(me, self.to_up, 0, x_ref).start()

        @pl.when(self.down & self.wanted(me, self.z - 1))
        def _():
            self.send(me, self.to_down, 1, x_ref).start()

        self.send(me, self.to_b, 3, x_ref).start()
        self.send(me, self.to_a, 2, x_ref).start()
        self.own.wait()

    def take(self, i):
        layer, over_a, over_b, slot = self.block(i)
        here = (i > 0) & self.wanted(slot, self.z)

        @pl.when(here)
        def _():
            self.send(slot, self.to_b, 3).wait_recv()

        @pl.when(here & (over_b == 0))
        def _():
            @pl.when(over_a == 0)
            def _():
                @pl.when((layer < self.z) & self.up & self.wanted(slot, self.z + 1))
                def _():
                    self.send(slot, self.to_up, 0).start()

                @pl.when((layer > self.z) & self.down & self.wanted(slot, self.z - 1))
                def _():
                    self.send(slot, self.to_down, 1).start()

                self.send(slot, self.to_a, 2).start()

            self.send(slot, self.to_b, 3).start()

        return slot

    def drain(self):
        def body(layer, _):
            slot = self.at(layer, self.a, self.b)
            beyond = self.at(layer, 1 - self.a, self.b)

            @pl.when(self.wanted(slot, self.z))
            def _():
                self.send(slot, self.to_a, 2).wait_send()
                self.send(slot, self.to_b, 3).wait_send()

            @pl.when(self.wanted(beyond, self.z))
            def _():
                self.send(beyond, self.to_b, 3).wait_send()

            @pl.when((layer <= self.z) & self.up & self.wanted(slot, self.z + 1))
            def _():
                self.send(slot, self.to_up, 0).wait_send()

            @pl.when((layer >= self.z) & self.down & self.wanted(slot, self.z - 1))
            def _():
                self.send(slot, self.to_down, 1).wait_send()

            return 0

        lax.fori_loop(0, self.layers, body, 0)


def gather_semaphores(n):
    return [
        pltpu.SemaphoreType.DMA((4, n)),
        pltpu.SemaphoreType.DMA((n,)),
        pltpu.SemaphoreType.DMA(()),
    ]


def gather_kernel(n, x_ref, o_ref, *semaphores):
    arrivals = Arrivals(n, x_ref, o_ref, *semaphores)
    arrivals.start()

    def body(i, _):
        arrivals.take(i)
        return 0

    lax.fori_loop(0, n, body, 0)
    arrivals.drain()


def gathered_blocks(x, collective_id):
    n = lax.axis_size("seq")
    return pl.pallas_call(
        functools.partial(gather_kernel, n),
        out_shape=jax.ShapeDtypeStruct((n,) + x.shape, x.dtype),
        in_specs=[pl.BlockSpec(memory_space=pl.ANY)],
        out_specs=pl.BlockSpec(memory_space=pl.ANY),
        scratch_shapes=gather_semaphores(n),
        compiler_params=pltpu.CompilerParams(
            collective_id=collective_id, has_side_effects=True
        ),
    )(x)


def gather_beside_kernel(n, reach, x_ref, y_ref, o_ref, y_out, sent, landed, local, *semaphores):
    beside = Beside(n, 1, ((y_ref, y_out),), sent, landed, local)
    arrivals = Arrivals(n, x_ref, o_ref, *semaphores, reach=reach)
    arrivals.start(beside)

    def body(i, _):
        arrivals.take(i)
        beside.start(i)
        return 0

    lax.fori_loop(0, n, body, 0)
    beside.finish()
    arrivals.drain()


def gathered_beside(x, y, collective_id, reach=None):
    n = lax.axis_size("seq")
    anywhere = pl.BlockSpec(memory_space=pl.ANY)
    return pl.pallas_call(
        functools.partial(gather_beside_kernel, n, reach),
        out_shape=[
            jax.ShapeDtypeStruct((n,) + x.shape, x.dtype),
            jax.ShapeDtypeStruct(y.shape, y.dtype),
        ],
        in_specs=[anywhere] * 2,
        out_specs=[anywhere] * 2,
        scratch_shapes=[pltpu.SemaphoreType.DMA((1, n))] * 2
        + [pltpu.SemaphoreType.DMA((1,))]
        + gather_semaphores(n),
        compiler_params=pltpu.CompilerParams(
            collective_id=collective_id, has_side_effects=True
        ),
    )(x, y)


def pair_rows(pair):
    return pair.reshape(pair.shape[0] * pair.shape[1], pair.shape[2])


def units_kernel(
    n,
    x_ref,
    w_gate_ref,
    w_up_ref,
    slots,
    gate_ref,
    up_ref,
    hidden_ref,
    x_buf,
    gate_buf,
    up_buf,
    hidden_buf,
    load_sem,
    store_sem,
    *semaphores,
):
    arrivals = Arrivals(n, x_ref, slots, *semaphores)
    arrivals.start()
    kept = ((gate_ref, gate_buf), (up_ref, up_buf), (hidden_ref, hidden_buf))

    def stores(pair):
        buf = pair % 2
        return [
            pltpu.make_async_copy(
                held.at[buf, i], out.at[arrivals.block(2 * pair + i)[3]], store_sem.at[buf, i, j]
            )
            for i in range(2)
            for j, (out, held) in enumerate(kept)
        ]

    def body(pair, _):
        buf = pair % 2
        loads = [
            pltpu.make_async_copy(
                slots.at[arrivals.take(2 * pair + i)], x_buf.at[i], load_sem.at[i]
            )
            for i in range(2)
        ]
        for load in loads:
            load.start()
        for load in loads:
            load.wait()

        @pl.when(pair >= 2)
        def _():
            for store in stores(pair - 2):
                store.wait()

        x = pair_rows(x_buf[...])
        shape = gate_buf.shape[1:]
        gate = product(x, w_gate_ref[...])
        up = product(x, w_up_ref[...])
        gate_buf[buf] = gate.reshape(shape)
        up_buf[buf] = up.reshape(shape)
        hidden_buf[buf] = (gate * jax.nn.sigmoid(gate) * up).astype(jnp.bfloat16).reshape(shape)
        for store in stores(pair):
            store.start()
        return 0

    lax.fori_loop(0, n // 2, body, 0)
    for pair in (n // 2 - 2, n // 2 - 1):
        for store in stores(pair):
            store.wait()
    arrivals.drain()


def gathered_units(x, w_gate, w_up, collective_id):
    n = lax.axis_size("seq")
    rows, units = x.shape[0], w_gate.shape[1]
    exact = jax.ShapeDtypeStruct((n, rows, units), jnp.float32)
    low = jax.ShapeDtypeStruct((n, rows, units), jnp.bfloat16)
    anywhere = pl.BlockSpec(memory_space=pl.ANY)
    return pl.pallas_call(
        functools.partial(units_kernel, n),
        out_shape=[jax.ShapeDtypeStruct((n,) + x.shape, x.dtype), exact, exact, low],
        in_specs=[anywhere] + [pl.BlockSpec(memory_space=pltpu.VMEM)] * 2,
        out_specs=[anywhere] * 4,
        scratch_shapes=[
            pltpu.VMEM((2,) + x.shape, x.dtype),
            pltpu.VMEM((2, 2, rows, units), jnp.float32),
            pltpu.VMEM((2, 2, rows, units), jnp.float32),
            pltpu.VMEM((2, 2, rows, units), jnp.bfloat16),
            pltpu.SemaphoreType.DMA((2,)),
            pltpu.SemaphoreType.DMA((2, 2, 3)),
        ]
        + gather_semaphores(n),
        compiler_params=pltpu.CompilerParams(
            collective_id=collective_id, has_side_effects=True, vmem_limit_bytes=60 * 2**20
        ),
    )(x, w_gate, w_up)


def units_back_kernel(
    n,
    x_ref,
    w_gate_ref,
    w_up_ref,
    down_mine_ref,
    down_other_ref,
    features_ref,
    gate_ref,
    up_ref,
    slots,
    terms_ref,
    dunits_mine,
    dunits_other,
    ddown_mine,
    ddown_other,
    x_buf,
    features_buf,
    gate_buf,
    up_buf,
    terms_buf,
    hidden_grad,
    gate_sum,
    up_sum,
    down_sum,
    down_buf,
    units_buf,
    load_sem,
    store_sem,
    out_sem,
    *semaphores,
):
    arrivals = Arrivals(n, x_ref, slots, *semaphores)
    arrivals.start()
    gate_sum[...] = jnp.zeros_like(gate_sum)
    up_sum[...] = jnp.zeros_like(up_sum)
    down_sum[...] = jnp.zeros_like(down_sum)
    units, cols = down_mine_ref.shape[1:]
    room = hidden_grad.shape[1] // 2
    out_width = n * cols
    several = 4
    tile = several * cols
    chunks, chunk = terms_ref.shape[0], terms_ref.shape[3]

    def stores(pair):
        return [
            pltpu.make_async_copy(
                terms_buf.at[i, :, pl.ds(c * chunk, chunk)],
                terms_ref.at[c, arrivals.block(2 * pair + i)[3]],
                store_sem.at[i, c],
            )
            for i in range(2)
            for c in range(chunks)
        ]

    def loads(pair):
        return [
            pltpu.make_async_copy(
                source.at[arrivals.block(2 * pair + i)[3]],
                held.at[pair % 2, i] if j < 2 else held.at[i],
                load_sem.at[pair % 2, i, j],
            )
            for i in range(2)
            for j, (source, held) in enumerate(
                ((slots, x_buf), (features_ref, features_buf), (gate_ref, gate_buf), (up_ref, up_buf))
            )
        ]

    def take_pair(pair):
        arrivals.take(2 * pair)
        arrivals.take(2 * pair + 1)
        for load in loads(pair):
            load.start()

    take_pair(0)

    def body(pair, _):
        buf = pair % 2
        for load in loads(pair):
            load.wait()
        hidden_grad[...] = jnp.zeros_like(hidden_grad)

        def back_tile(t, _):
            for i, held in enumerate((down_mine_ref, down_other_ref)):
                hidden_grad[:, i * room : i * room + units] += sum(
                    product_nt(
                        pair_rows(
                            x_buf[buf, :, :, pl.ds(pl.multiple_of(t * tile + j * cols, cols), cols)]
                        ),
                        held[t * several + j],
                    )
                    for j in range(several)
                )
            return 0

        lax.fori_loop(0, out_width // tile, back_tile, 0)
        gate, up, grad = pair_rows(gate_buf[...]), pair_rows(up_buf[...]), hidden_grad[...]
        share = jax.nn.sigmoid(gate)
        silu = gate * share
        gate_low = (grad * up * (share * (1.0 + gate * (1.0 - share)))).astype(jnp.bfloat16)
        up_low = (grad * silu).astype(jnp.bfloat16)
        hidden_t = (silu * up).astype(jnp.bfloat16).T
        terms = product_nt(gate_low, w_gate_ref[...]) + product_nt(up_low, w_up_ref[...])

        @pl.when(pair >= 1)
        def _():
            for store in stores(pair - 1):
                store.wait()

        terms_buf[...] = terms.astype(jnp.bfloat16).reshape(terms_buf.shape)
        for store in stores(pair):
            store.start()

        @pl.when(pair + 1 < n // 2)
        def _():
            take_pair(pair + 1)

        features_t = pair_rows(features_buf[buf]).T
        for begin in range(0, gate_low.shape[1], 256):
            columns = slice(begin, begin + 256)
            gate_sum[:, columns] += product(features_t, gate_low[:, columns])
            up_sum[:, columns] += product(features_t, up_low[:, columns])

        def down_tile(t, _):
            columns = pl.ds(pl.multiple_of(t * tile, tile), tile)
            x = pair_rows(x_buf[buf, :, :, columns])
            for i in range(2):
                down_sum[i, :, columns] += product(hidden_t[i * room : i * room + units], x)
            return 0

        lax.fori_loop(0, out_width // tile, down_tile, 0)
        return 0

    lax.fori_loop(0, n // 2, body, 0)
    def grad_stores(j):
        return [
            pltpu.make_async_copy(source, target.at[j], out_sem.at[j % 2, i])
            for i, (source, target) in enumerate(
                (
                    (down_buf.at[j % 2, 0], ddown_mine),
                    (down_buf.at[j % 2, 1], ddown_other),
                    (units_buf.at[j % 2, 0], dunits_mine),
                    (units_buf.at[j % 2, 1], dunits_other),
                )
            )
        ]

    def grads_out(j, _):
        @pl.when(j >= 2)
        def _():
            for store in grad_stores(j - 2):
                store.wait()

        columns = pl.ds(pl.multiple_of(j * cols, cols), cols)
        down_buf[j % 2] = down_sum[:, :, columns].astype(jnp.bfloat16)
        owned = units_buf.shape[3]
        owner = pl.ds(pl.multiple_of(j * owned, 8), owned)
        for i in range(2):
            for k, total in enumerate((gate_sum, up_sum)):
                units_buf[j % 2, i, k] = total[owner, i * room : (i + 1) * room].astype(
                    jnp.bfloat16
                )
        for store in grad_stores(j):
            store.start()
        return 0

    lax.fori_loop(0, n, grads_out, 0)
    for j in (n - 2, n - 1):
        for store in grad_stores(j):
            store.wait()
    for store in stores(n // 2 - 1):
        store.wait()
    arrivals.drain()


def gathered_back(x, w_gate, w_up, mine, other, features, gate, up, chunks, collective_id):
    n = lax.axis_size("seq")
    rows, out_width = x.shape
    width, units = w_gate.shape
    low, exact = jnp.bfloat16, jnp.float32
    anywhere = pl.BlockSpec(memory_space=pl.ANY)
    in_vmem = pl.BlockSpec(memory_space=pltpu.VMEM)
    return pl.pallas_call(
        functools.partial(units_back_kernel, n),
        out_shape=[
            jax.ShapeDtypeStruct((n,) + x.shape, low),
            jax.ShapeDtypeStruct((chunks, n, rows, width // chunks), low),
            jax.ShapeDtypeStruct((n, 2, width // n, units // 2), low),
            jax.ShapeDtypeStruct((n, 2, width // n, units // 2), low),
            jax.ShapeDtypeStruct(mine.shape, low),
            jax.ShapeDtypeStruct(mine.shape, low),
        ],
        in_specs=[anywhere] + [in_vmem] * 4 + [anywhere] * 3,
        out_specs=[anywhere] * 6,
        scratch_shapes=[
            pltpu.VMEM((2, 2, rows, out_width), low),
            pltpu.VMEM((2, 2, rows, width), low),
            pltpu.VMEM((2, rows, units), exact),
            pltpu.VMEM((2, rows, units), exact),
            pltpu.VMEM((2, rows, width), low),
            pltpu.VMEM((2 * rows, units), exact),
            pltpu.VMEM((width, units), exact),
            pltpu.VMEM((width, units), exact),
            pltpu.VMEM((2, mine.shape[1], out_width), exact),
            pltpu.VMEM((2, 2) + mine.shape[1:], low),
            pltpu.VMEM((2, 2, 2, width // n, units // 2), low),
            pltpu.SemaphoreType.DMA((2, 2, 4)),
            pltpu.SemaphoreType.DMA((2, chunks)),
            pltpu.SemaphoreType.DMA((2, 4)),
        ]
        + gather_semaphores(n),
        compiler_params=pltpu.CompilerParams(
            collective_id=collective_id, has_side_effects=True, vmem_limit_bytes=60 * 2**20
        ),
    )(x, w_gate, w_up, mine, other, features, gate, up)


def scatter_kernel(n, chunks, p_ref, o_ref, from_b, from_a, from_down, from_up, *semaphores, fill=None, work=None):
    layers = n // 4
    me, z, a, b, step_a, step_b = place()
    partners = neighbours(layers)
    (up, to_up), (down, to_down), (_, to_a), (_, to_b) = partners
    b_sent, b_landed, a_sent, a_landed, u_sent, u_landed, d_sent, d_landed = semaphores
    greet(partners)

    def at(layer, of_a, of_b):
        return layer * 4 + of_a * step_a + of_b * step_b

    def copy(source, target, sent, landed, device):
        return pltpu.make_async_remote_copy(
            src_ref=source,
            dst_ref=target,
            send_sem=sent,
            recv_sem=landed,
            device_id={"seq": device},
            device_id_type=MESH,
        )

    def over_b(c, of_a, layer):
        return copy(
            p_ref.at[c, at(layer, of_a, 1 - b)],
            from_b.at[c, of_a, layer],
            b_sent.at[c, of_a, layer],
            b_landed.at[c, of_a, layer],
            to_b,
        )

    def over_a(c, layer):
        return copy(
            p_ref.at[c, at(layer, 1 - a, b)],
            from_a.at[c, layer],
            a_sent.at[c, layer],
            a_landed.at[c, layer],
            to_a,
        )

    def upward(c, layer):
        return copy(
            p_ref.at[c, at(layer, a, b)],
            from_down.at[c, layer],
            u_sent.at[c, layer],
            u_landed.at[c, layer],
            to_up,
        )

    def downward(c, layer):
        return copy(
            p_ref.at[c, at(layer, a, b)],
            from_up.at[c, layer],
            d_sent.at[c, layer],
            d_landed.at[c, layer],
            to_down,
        )

    def each_layer(body):
        lax.fori_loop(0, layers, lambda layer, _: (body(layer), 0)[1], 0)

    def send_b(c):
        each_layer(lambda layer: over_b(c, 1 - a, layer).start())
        each_layer(lambda layer: over_b(c, a, layer).start())

    def send_a(c):
        def body(layer):
            over_b(c, 1 - a, layer).wait_recv()
            slot = at(layer, 1 - a, b)
            p_ref[c, slot] = p_ref[c, slot] + from_b[c, 1 - a, layer]
            over_a(c, layer).start()

        each_layer(body)

    def join_line(c):
        def body(layer):
            over_b(c, a, layer).wait_recv()
            over_a(c, layer).wait_recv()
            slot = at(layer, a, b)
            p_ref[c, slot] = p_ref[c, slot] + from_b[c, a, layer] + from_a[c, layer]

            @pl.when((layer > z) & (z == 0))
            def _():
                upward(c, layer).start()

            @pl.when((layer < z) & (z == layers - 1))
            def _():
                downward(c, layer).start()

        each_layer(body)

    def pass_up(c):
        def body(layer):
            @pl.when(layer > z)
            def _():
                upward(c, layer).wait_recv()
                slot = at(layer, a, b)
                p_ref[c, slot] = p_ref[c, slot] + from_down[c, layer]
                upward(c, layer).start()

        each_layer(body)

    def pass_down(c):
        def body(layer):
            @pl.when(layer < z)
            def _():
                downward(c, layer).wait_recv()
                slot = at(layer, a, b)
                p_ref[c, slot] = p_ref[c, slot] + from_up[c, layer]
                downward(c, layer).start()

        each_layer(body)

    def finish(c):
        @pl.when(down)
        def _():
            upward(c, z).wait_recv()
            p_ref[c, me] = p_ref[c, me] + from_down[c, z]

        @pl.when(up)
        def _():
            downward(c, z).wait_recv()
            p_ref[c, me] = p_ref[c, me] + from_up[c, z]

        o_ref[c] = p_ref[c, me]

    def when_chunk(step, stage):
        @pl.when((step >= 0) & (step < chunks))
        def _():
            stage(jnp.clip(step, 0, chunks - 1))

    def fill_and_send(c):
        if fill is not None:
            fill(c)
        send_b(c)

    fill_and_send(0)

    def step(t, _):
        when_chunk(t + 1, fill_and_send)
        if work is not None:
            work(t)
        when_chunk(t, send_a)
        when_chunk(t - 1, join_line)
        inner = (z > 0) & (z < layers - 1)

        @pl.when(inner)
        def _():
            when_chunk(t - 1 - z, pass_up)
            when_chunk(t - layers + z, pass_down)

        when_chunk(t - layers, finish)
        return 0

    lax.fori_loop(0, chunks + layers, step, 0)

    def drain(c, _):
        def body(layer):
            over_b(c, 0, layer).wait_send()
            over_b(c, 1, layer).wait_send()
            over_a(c, layer).wait_send()

            @pl.when(layer > z)
            def _():
                upward(c, layer).wait_send()

            @pl.when(layer < z)
            def _():
                downward(c, layer).wait_send()

        each_layer(body)
        return 0

    lax.fori_loop(0, chunks, drain, 0)


def scatter_scratch(chunks, n, block, dtype):
    layers = n // 4

    def slots(*count):
        return pltpu.VMEM((chunks,) + count + block, dtype)

    def semaphores(*count):
        return pltpu.SemaphoreType.DMA((chunks,) + count)

    return (
        [slots(2, layers)]
        + [slots(layers)] * 3
        + [semaphores(2, layers)] * 2
        + [semaphores(layers)] * 6
    )


def scattered_sum(terms, collective_id):
    chunks, n = terms.shape[:2]
    block = terms.shape[2:]
    return pl.pallas_call(
        functools.partial(scatter_kernel, n, chunks),
        out_shape=jax.ShapeDtypeStruct((chunks,) + block, terms.dtype),
        in_specs=[pl.BlockSpec(memory_space=pltpu.VMEM)],
        out_specs=pl.BlockSpec(memory_space=pltpu.VMEM),
        scratch_shapes=scatter_scratch(chunks, n, block, terms.dtype),
        compiler_params=pltpu.CompilerParams(
            collective_id=collective_id, has_side_effects=True, vmem_limit_bytes=60 * 2**20
        ),
    )(terms)


def down_kernel(n, hidden_ref, mine_ref, other_ref, o_ref, p_ref, *scratch):
    units = mine_ref.shape[1]
    room = hidden_ref.shape[2] // 2

    def fill(c):
        def body(pair, _):
            owners = pl.ds(2 * pair, 2)
            terms = sum(
                product(pair_rows(hidden_ref[owners, :, pl.ds(i * room, units)]), held[c])
                for i, held in enumerate((mine_ref, other_ref))
            )
            p_ref[c, owners] = terms.astype(p_ref.dtype).reshape((2,) + p_ref.shape[2:])
            return 0

        lax.fori_loop(0, n // 2, body, 0)

    scatter_kernel(n, n, p_ref, o_ref, *scratch, fill=fill)


def scattered_down(hidden, mine, other, collective_id):
    n, rows = hidden.shape[:2]
    block = (rows, mine.shape[2])
    return pl.pallas_call(
        functools.partial(down_kernel, n),
        out_shape=jax.ShapeDtypeStruct((n,) + block, hidden.dtype),
        in_specs=[pl.BlockSpec(memory_space=pltpu.VMEM)] * 3,
        out_specs=pl.BlockSpec(memory_space=pltpu.VMEM),
        scratch_shapes=[pltpu.VMEM((n, n) + block, hidden.dtype)]
        + scatter_scratch(n, n, block, hidden.dtype),
        compiler_params=pltpu.CompilerParams(
            collective_id=collective_id, has_side_effects=True, vmem_limit_bytes=60 * 2**20
        ),
    )(hidden, mine, other)


class Beside:
    def __init__(self, n, per_step, pairs, sent, landed, local):
        self.n, self.per_step, self.pairs = n, per_step, pairs
        self.sent, self.landed = sent, landed
        self.me = lax.axis_index("seq")
        self.own = [
            pltpu.make_async_copy(source.at[self.me], target.at[self.me], local.at[j])
            for j, (source, target) in enumerate(pairs)
        ]

    def greet(self):
        barrier = pltpu.get_barrier_semaphore()
        for step in range(1, self.n):
            pl.semaphore_signal(
                barrier,
                inc=1,
                device_id={"seq": lax.rem(self.me + step, self.n)},
                device_id_type=MESH,
            )
        pl.semaphore_wait(barrier, self.n - 1)
        for own in self.own:
            own.start()

    def copies(self, step):
        other = lax.rem(self.me + step, self.n)
        return [
            pltpu.make_async_remote_copy(
                src_ref=source.at[other],
                dst_ref=target.at[self.me],
                send_sem=self.sent.at[j, step],
                recv_sem=self.landed.at[j, step],
                device_id={"seq": other},
                device_id_type=MESH,
            )
            for j, (source, target) in enumerate(self.pairs)
        ]

    def start(self, t):
        for i in range(self.per_step):
            step = t * self.per_step + i + 1

            @pl.when(step < self.n)
            def _():
                for copy in self.copies(jnp.minimum(step, self.n - 1)):
                    copy.start()

    def finish(self):
        def body(step, _):
            for copy in self.copies(step):
                copy.wait()
            return 0

        lax.fori_loop(1, self.n, body, 0)
        for own in self.own:
            own.wait()


def vision_kernel(n, chunks, spans, scaling, *refs):
    left_ref, right_ref, *attention = refs[:9]
    o_ref, *grads = refs[9:13]
    p_ref, *scratch = refs[13:]
    cols = right_ref.shape[1] // chunks
    shard = left_ref.shape[1] // n
    tile = 128
    for total in grads[1:]:
        total[...] = jnp.zeros_like(total)

    def fill(c):
        def body(t, _):
            tile = c * (cols // 128) + t
            source = sum(jnp.where(tile >= span, 1, 0) for span in spans[1:])
            columns = pl.ds(pl.multiple_of(tile * 128, 128), 128)
            terms = product(left_ref[source], right_ref[:, columns])
            p_ref[c, :, :, pl.ds(pl.multiple_of(t * 128, 128), 128)] = terms.reshape(
                n, shard, 128
            ).astype(p_ref.dtype)
            return 0

        lax.fori_loop(0, cols // 128, body, 0)

    tiles = attention[0].shape[0] // tile
    assert tiles <= chunks + n // 4

    def work(t):
        @pl.when(t < tiles)
        def _():
            attend_back_tile(scaling, tile, jnp.minimum(t, tiles - 1), *attention, *grads)

    scatter_kernel(n, chunks, p_ref, o_ref, *scratch, fill=fill, work=work)


def scattered_vision(left, right, attention, scaling, spans, chunks, collective_id):
    n = lax.axis_size("seq")
    block = (left.shape[1] // n, right.shape[1] // chunks)
    in_vmem = pl.BlockSpec(memory_space=pltpu.VMEM)
    return pl.pallas_call(
        functools.partial(vision_kernel, n, chunks, spans, scaling),
        out_shape=[jax.ShapeDtypeStruct((chunks,) + block, left.dtype)]
        + [jax.ShapeDtypeStruct(x.shape, jnp.float32) for x in attention[:3]],
        in_specs=[in_vmem] * 9,
        out_specs=[in_vmem] * 4,
        scratch_shapes=[pltpu.VMEM((chunks, n) + block, left.dtype)]
        + scatter_scratch(chunks, n, block, left.dtype),
        compiler_params=pltpu.CompilerParams(
            collective_id=collective_id, has_side_effects=True, vmem_limit_bytes=60 * 2**20
        ),
    )(left, right, *attention)


def exchange_kernel(n, groups, *refs):
    count = len(groups)
    sources, targets = refs[:count], refs[count : 2 * count]
    sent, landed, local = refs[2 * count :]
    me = lax.axis_index("seq")
    barrier = pltpu.get_barrier_semaphore()
    for step in range(1, n):
        pl.semaphore_signal(
            barrier, inc=1, device_id={"seq": lax.rem(me + step, n)}, device_id_type=MESH
        )
    pl.semaphore_wait(barrier, n - 1)
    copies = []
    for j, group in enumerate(groups):
        base = lax.div(me, group) * group
        mine = me - base
        copies.append(
            pltpu.make_async_copy(sources[j].at[mine], targets[j].at[mine], local.at[j])
        )
        copies[-1].start()
        for step in range(1, group):
            other = lax.rem(mine + step, group)
            copies.append(
                pltpu.make_async_remote_copy(
                    src_ref=sources[j].at[other],
                    dst_ref=targets[j].at[mine],
                    send_sem=sent.at[j, step],
                    recv_sem=landed.at[j, step],
                    device_id={"seq": base + other},
                    device_id_type=MESH,
                )
            )
            copies[-1].start()
    for copy in copies:
        copy.wait()


def exchanged(arrays, collective_id):
    n = lax.axis_size("seq")
    count = len(arrays)
    groups = tuple(x.shape[0] for x in arrays)
    return pl.pallas_call(
        functools.partial(exchange_kernel, n, groups),
        out_shape=[jax.ShapeDtypeStruct(x.shape, x.dtype) for x in arrays],
        in_specs=[pl.BlockSpec(memory_space=pl.ANY)] * count,
        out_specs=[pl.BlockSpec(memory_space=pl.ANY)] * count,
        scratch_shapes=[pltpu.SemaphoreType.DMA((count, n))] * 2
        + [pltpu.SemaphoreType.DMA((count,))],
        compiler_params=pltpu.CompilerParams(
            collective_id=collective_id, has_side_effects=True
        ),
    )(*arrays)


def reduce_kernel(n, combine, x_ref, o_ref, shares, total, sent, landed, sent_on, landed_on):
    me = lax.axis_index("seq")
    barrier = pltpu.get_barrier_semaphore()
    others = [lax.rem(me + step, n) for step in range(1, n)]
    for other in others:
        pl.semaphore_signal(barrier, inc=1, device_id={"seq": other}, device_id_type=MESH)
    pl.semaphore_wait(barrier, n - 1)

    def copy(step, source, target, sent, landed):
        return pltpu.make_async_remote_copy(
            src_ref=source,
            dst_ref=target,
            send_sem=sent.at[step],
            recv_sem=landed.at[step],
            device_id={"seq": others[step - 1]},
            device_id_type=MESH,
        )

    there = [copy(i, x_ref.at[others[i - 1]], shares.at[me], sent, landed) for i in range(1, n)]
    for move in there:
        move.start()
    shares[me] = x_ref[me]
    for move in there:
        move.wait()
    total[...] = combine(shares[...])
    back = [copy(i, total, o_ref.at[me], sent_on, landed_on) for i in range(1, n)]
    for move in back:
        move.start()
    o_ref[me] = total[...]
    for move in back:
        move.wait()


def reduced(x, combine, collective_id):
    n = x.shape[0]
    return pl.pallas_call(
        functools.partial(reduce_kernel, n, combine),
        out_shape=jax.ShapeDtypeStruct(x.shape, x.dtype),
        in_specs=[pl.BlockSpec(memory_space=pltpu.VMEM)],
        out_specs=pl.BlockSpec(memory_space=pltpu.VMEM),
        scratch_shapes=[pltpu.VMEM(x.shape, x.dtype), pltpu.VMEM(x.shape[1:], x.dtype)]
        + [pltpu.SemaphoreType.DMA((n,))] * 4,
        compiler_params=pltpu.CompilerParams(
            collective_id=collective_id, has_side_effects=True
        ),
    )(x)


def added(shares):
    return jnp.sum(shares, axis=0)


def softmax_shares(shares):
    column = lax.broadcasted_iota(jnp.int32, shares.shape, 2)
    at_peak = column == RHD
    peak = jnp.max(jnp.where(at_peak, shares, -jnp.inf), axis=2, keepdims=True)
    top = jnp.max(peak, axis=0, keepdims=True)
    sums = jnp.sum(shares * jnp.exp(peak - top), axis=0)
    return jnp.where(at_peak[0], top[0], sums)


def swapped(value):
    return lax.ppermute(value, "tp", [(0, 1), (1, 0)])


def rounded(value):
    return lax.reduce_precision(value, 8, 7)


def paired(value):
    kept = rounded(value)
    return kept + swapped(kept.astype(jnp.bfloat16)).astype(jnp.float32)


def in_order(mine, other, axis):
    first = lax.axis_index("tp") == 0
    return jnp.concatenate(
        [jnp.where(first, mine, other), jnp.where(first, other, mine)], axis=axis
    )


def attend_kernel(scaling, q_ref, k_ref, v_ref, qid_ref, kid_ref, o_ref, lse_ref):
    scores = product_nt(q_ref[...], k_ref[...]) * scaling
    scores = jnp.where(qid_ref[...] == kid_ref[...], scores, -1e30)
    peak = jnp.max(scores, axis=1, keepdims=True)
    weights = jnp.exp(scores - peak)
    total = jnp.sum(weights, axis=1, keepdims=True)
    probability = (weights / total).astype(jnp.bfloat16)
    o_ref[...] = product(probability, v_ref[...]).astype(o_ref.dtype)
    lse_ref[...] = peak + jnp.log(total)


def attend_back_tile(scaling, tile, t, q_ref, k_ref, v_ref, g_ref, qid_ref, kid_ref, lse_ref, *grads):
    dq_ref, dk_ref, dv_ref = grads
    rows = pl.ds(pl.multiple_of(t * tile, tile), tile)
    query, grad = q_ref[rows], g_ref[rows]
    scores = product_nt(query, k_ref[...]) * scaling
    scores = jnp.where(qid_ref[rows] == kid_ref[...], scores, -1e30)
    probability = jnp.exp(scores - lse_ref[rows])
    dprob = product_nt(grad, v_ref[...])
    inner = jnp.sum(probability * dprob, axis=1, keepdims=True)
    low = (probability * (dprob - inner)).astype(jnp.bfloat16)
    dq_ref[rows] = product(low, k_ref[...]) * scaling
    dk_ref[...] += product_tn(low, query) * scaling
    dv_ref[...] += product_tn(probability.astype(jnp.bfloat16), grad)


def attention_call(queries, window, width, tile, scaling):
    tiled = lambda columns: pl.BlockSpec((tile, columns), lambda i: (i, 0))
    whole = lambda rows, columns: pl.BlockSpec((rows, columns), lambda i: (0, 0))
    params = pltpu.CompilerParams(vmem_limit_bytes=56 * 2**20)
    forward = pl.pallas_call(
        functools.partial(attend_kernel, scaling),
        grid=(queries // tile,),
        in_specs=[
            tiled(width),
            whole(window, width),
            whole(window, width),
            tiled(1),
            whole(1, window),
        ],
        out_specs=[tiled(width), tiled(1)],
        out_shape=[
            jax.ShapeDtypeStruct((queries, width), jnp.bfloat16),
            jax.ShapeDtypeStruct((queries, 1), jnp.float32),
        ],
        compiler_params=params,
        cost_estimate=pl.CostEstimate(
            flops=4 * queries * window * width,
            bytes_accessed=2 * (2 * window + 2 * queries) * 128,
            transcendentals=queries * window,
        ),
    )
    return forward


def padded_columns(matrix, width):
    return jnp.pad(matrix, ((0, 0), (0, width - matrix.shape[1])))


def tokens_travel(
    patches,
    lengths,
    ln1_gain,
    ln1_bias,
    q_weight,
    q_bias,
    k_weight,
    v_weight,
    v_bias,
    o_weight,
    o_bias,
    ln2_gain,
    ln2_bias,
    up_weight,
    up_bias,
    down_weight,
    down_bias,
    gate_proj,
    up_proj,
    down_proj,
    ctx_gain,
    rk_weight,
    rv_weight,
    latents,
    lat_gain,
    rq_weight,
    ro_weight,
    feat_grad,
    lat_grad,
):
    low = jnp.bfloat16
    rows, width = patches.shape
    half = rows // 2
    n = lax.axis_size("seq")
    me = lax.axis_index("seq")
    core = lax.axis_index("tp")
    total_rows = rows * n
    longest = min(IMGMAX, (n // 2 - 1) * rows)
    heads = q_bias.shape[0] // HD
    part = me // heads
    queries = total_rows // 2
    window = total_rows - longest
    window_start = part * longest
    query_start = part * (queries - longest)
    scaling = HD ** (-0.5)
    kv_heads = rk_weight.shape[1] // RHD
    q_heads = rq_weight.shape[1] // RHD
    group = q_heads // kv_heads
    lat_rows = latents.shape[0]
    lat_scaling = RHD ** (-0.5)
    first_block = (me == 0).astype(jnp.float32)
    shard = q_weight.shape[0]
    hidden_units = up_bias.shape[0]
    hidden_pad = -(-hidden_units // 128) * 128
    proj_units = gate_proj.shape[1] // n
    own_width = heads * HD
    unit_lanes = -(-proj_units // 128) * 128
    out_width = down_proj.shape[1] * n

    def my_half(value):
        return lax.dynamic_slice_in_dim(value, core * half, half, 0)

    input_f32 = patches.astype(jnp.float32)
    normed_in = layer_norm(input_f32, ln1_gain, ln1_bias).astype(low)
    lanes = -(-HD // 128) * 128

    def wide(heads_of):
        return jnp.pad(heads_of, [(0, 0)] * (heads_of.ndim - 1) + [(0, lanes - HD)])

    def compact(parts):
        joined = jnp.concatenate([p[..., :HD] for p in parts], axis=-1)
        room = -(-joined.shape[-1] // 128) * 128 - joined.shape[-1]
        return jnp.pad(joined, [(0, 0)] * (joined.ndim - 1) + [(0, room)])

    head_shard = compact([split_heads(w, heads) for w in (q_weight, k_weight, v_weight)])
    normed_half, head_weight = gathered_beside(
        my_half(normed_in), jnp.concatenate([head_shard] * 2, axis=0), 2, reach=window // rows
    )

    unit_weights = jnp.stack([gate_proj, up_proj]).reshape(2, shard, n, proj_units)
    unit_weights = jnp.pad(unit_weights, ((0, 0),) * 3 + ((0, unit_lanes - proj_units),))
    ctx_width = rk_weight.shape[1]
    ctx_shard = jnp.concatenate([rk_weight, rv_weight], axis=1)
    unit_weights, normed_half, head_weight = lax.optimization_barrier(
        (unit_weights.transpose(2, 0, 1, 3), normed_half, head_weight)
    )
    unit_weights = lax.all_to_all(unit_weights, "seq", 0, 0)
    normed_half = lax.dynamic_slice_in_dim(normed_half, window_start // rows, window // rows, 0)
    normed_window = in_order(
        normed_half[:, None], swapped(normed_half)[:, None], 1
    ).reshape(window, width)
    head_weight = head_weight.reshape(width, -1)
    head_weight = jnp.concatenate(
        [wide(head_weight[:, i * HD : (i + 1) * HD]) for i in range(3)], axis=1
    )
    head = me - part * heads
    q_bias_one = lax.dynamic_slice_in_dim(q_bias, head * HD, HD, 0)
    v_bias_one = lax.dynamic_slice_in_dim(v_bias, head * HD, HD, 0)
    bias_one = jnp.concatenate(
        [wide(q_bias_one), jnp.zeros((lanes,), jnp.float32), wide(v_bias_one)]
    )
    qkv = (product(normed_window, head_weight) + bias_one).astype(low)
    query_one = lax.dynamic_slice_in_dim(qkv[:, :lanes], query_start, queries, 0)
    key_one = qkv[:, lanes : 2 * lanes]
    value_one = qkv[:, 2 * lanes :]
    key_ids = image_ids(
        lengths, window_start + jnp.arange(window, dtype=jnp.int32), total_rows
    )
    query_ids = lax.dynamic_slice_in_dim(key_ids, query_start, queries, 0)[:, None]
    key_ids = key_ids[None, :]
    attend = attention_call(queries, window, lanes, rows, scaling)
    attended_one, lse_one = attend(query_one, key_one, value_one, query_ids, key_ids)
    attended_low = join_heads(
        exchanged([attended_one.reshape(heads, rows, lanes)], 3)[0][:, :, :HD]
    )

    vision_shard = jnp.concatenate(
        [
            padded_columns(up_weight, hidden_pad),
            padded_columns(down_weight.T, hidden_pad),
            o_weight.T,
        ],
        axis=1,
    )
    unit_weights, vision_shard, attended_low, down_proj = lax.optimization_barrier(
        (unit_weights, vision_shard, attended_low, down_proj)
    )
    vision, down_mine = gathered_beside(vision_shard, down_proj.reshape(n, proj_units, -1), 17)
    vision, ctx_shard = lax.optimization_barrier((vision.reshape(width, -1), ctx_shard))
    w_ctx = lax.all_gather(ctx_shard, "seq", axis=0, tiled=True)
    w_ctxkey, w_ctxval = w_ctx[:, :ctx_width], w_ctx[:, ctx_width:]
    down_other = swapped(down_mine)
    w_up = vision[:, :hidden_units]
    w_down_t = vision[:, hidden_pad : hidden_pad + hidden_units]
    w_out_t = vision[:, 2 * hidden_pad :]
    unit_weights = unit_weights.transpose(1, 0, 2, 3).reshape(2, width, unit_lanes)
    w_gate, w_up_proj = jnp.concatenate([unit_weights, swapped(unit_weights)], axis=2)

    attn_part = product_nt(attended_low, w_out_t)
    attn_sum = attn_part + swapped(attn_part)
    after_attn = input_f32 + attn_sum + o_bias
    mlp_in = layer_norm(after_attn, ln2_gain, ln2_bias).astype(low)
    hidden = product(mlp_in, w_up) + up_bias
    active_low = gelu_tanh(hidden).astype(low)
    after_mlp = after_attn + paired(product_nt(active_low, w_down_t)) + down_bias
    features = after_mlp.astype(low)

    features_all, proj_gate, proj_up, proj_hidden = gathered_units(
        my_half(features), w_gate, w_up_proj, 4
    )

    def joined_chunks(sums):
        return sums.transpose(1, 0, 2).reshape(half, -1)

    proj_out_low = joined_chunks(scattered_down(proj_hidden, down_mine, down_other, 5))
    proj_out_half = proj_out_low.astype(jnp.float32)
    proj_out = in_order(proj_out_low, swapped(proj_out_low), 0).astype(jnp.float32)
    qkv_shard, _ = lax.optimization_barrier(
        (jnp.concatenate([q_weight, k_weight, v_weight], axis=1), proj_out_low)
    )
    w_qkv = lax.all_gather(qkv_shard, "seq", axis=0, tiled=True)

    context_low = rms_norm(proj_out, ctx_gain).astype(low)
    ctx_keys = product(context_low, w_ctxkey).astype(low)
    ctx_values = product(context_low, w_ctxval).astype(low)
    lat_normed = rms_norm(latents, lat_gain).astype(low)
    lat_queries = product(lat_normed, rq_weight).astype(low)
    lat_keys = product(lat_normed, w_ctxkey).astype(low)
    lat_values = product(lat_normed, w_ctxval).astype(low)
    query_grouped = lat_queries.reshape(lat_rows, kv_heads, group, RHD)
    key_grouped = ctx_keys.reshape(rows, kv_heads, RHD)
    value_grouped = ctx_values.reshape(rows, kv_heads, RHD)
    self_keys = lat_keys.reshape(lat_rows, kv_heads, RHD)
    self_values = lat_values.reshape(lat_rows, kv_heads, RHD)
    lat_scores = (
        jnp.einsum("lkgd,tkd->kglt", query_grouped, key_grouped, preferred_element_type=jnp.float32)
        * lat_scaling
    )
    self_scores = (
        jnp.einsum("lkgd,tkd->kglt", query_grouped, self_keys, preferred_element_type=jnp.float32)
        * lat_scaling
    )
    stats = partial_stats(lat_scores, value_grouped)
    packed = jnp.concatenate([stats[2], stats[0][..., None], stats[1][..., None]], axis=-1)
    packed = jnp.pad(packed.reshape(n, -1, RHD + 2), ((0, 0), (0, 0), (0, 126 - RHD)))
    merged = reduced(packed, softmax_shares, 6).reshape(kv_heads, group, lat_rows, 128)
    lat_peak, lat_total, lat_numer = joint_stats(
        (merged[..., RHD], merged[..., RHD + 1], merged[..., :RHD]),
        partial_stats(self_scores, self_values),
    )
    lat_lse = lat_peak + jnp.log(lat_total)
    pooled_exact = lat_numer / lat_total[..., None]
    pooled_low = pooled_exact.transpose(2, 0, 1, 3).reshape(lat_rows, -1).astype(low)
    pooled_grad = product_nt(lat_grad, ro_weight).astype(low)
    pooled_grouped = pooled_grad.reshape(lat_rows, kv_heads, group, RHD)
    pooled_f32 = pooled_grouped.astype(jnp.float32)
    lat_delta = jnp.sum(pooled_f32.transpose(1, 2, 0, 3) * pooled_exact, axis=-1)

    def score_grads(scores, key_part, value_part):
        probability = jnp.exp(scores - lat_lse[..., None])
        dprob = jnp.einsum(
            "lkgd,tkd->kglt", pooled_grouped, value_part, preferred_element_type=jnp.float32
        )
        dscore = (probability * (dprob - lat_delta[..., None])).astype(low)
        query_term = (
            jnp.einsum("kglt,tkd->lkgd", dscore, key_part, preferred_element_type=jnp.float32)
            * lat_scaling
        )
        key_term = (
            jnp.einsum("kglt,lkgd->tkd", dscore, query_grouped, preferred_element_type=jnp.float32)
            * lat_scaling
        ).astype(low)
        value_term = jnp.einsum(
            "kglt,lkgd->tkd", probability, pooled_f32, precision=lax.Precision.HIGHEST
        ).astype(low)
        return (
            query_term,
            key_term.reshape(key_part.shape[0], -1),
            value_term.reshape(key_part.shape[0], -1),
        )

    ctx_query_term, ctx_keys_grad, ctx_values_grad = score_grads(
        lat_scores, key_grouped, value_grouped
    )
    self_query_term, self_keys_grad, self_values_grad = score_grads(
        self_scores, self_keys, self_values
    )
    ctx_part = product_nt(ctx_keys_grad, w_ctxkey) + product_nt(ctx_values_grad, w_ctxval)
    ctx_kept = rounded(my_half(ctx_part))
    ctx_sent = lax.dynamic_slice_in_dim(ctx_part, (1 - core) * half, half, 0).astype(low)
    ctx_back = ctx_kept + swapped(ctx_sent).astype(jnp.float32)
    ctx_pull = jax.vjp(rms_norm, proj_out_half, ctx_gain)[1]
    proj_out_grad, ctx_gain_part = ctx_pull(ctx_back)
    ctx_grads = jnp.concatenate([ctx_keys_grad, ctx_values_grad], axis=1)
    self_grads = jnp.concatenate([self_keys_grad, self_values_grad], axis=1)
    r_part = product_tn(context_low, ctx_grads) + first_block * product_tn(lat_normed, self_grads)
    r_part, proj_out_grad = lax.optimization_barrier((r_part.astype(low), proj_out_grad))
    r_grad = lax.psum_scatter(r_part, "seq", scatter_dimension=0, tiled=True).astype(jnp.float32)
    _, feat_terms, units_mine, units_other, downs_mine, downs_other = gathered_back(
        proj_out_grad.astype(low),
        w_gate,
        w_up_proj,
        down_mine,
        down_other,
        features_all,
        proj_gate,
        proj_up,
        width // 128,
        8,
    )

    query_part = ctx_query_term + first_block * self_query_term
    r_grad, feat_terms = lax.optimization_barrier((r_grad, feat_terms))
    feat_half = joined_chunks(scattered_sum(feat_terms, 11))

    proj_in_grad = in_order(feat_half, swapped(feat_half), 0).astype(jnp.float32)
    def core_sum(mine, other):
        return (mine.astype(jnp.float32) + swapped(other).astype(jnp.float32)).astype(low)

    down_blocks = core_sum(downs_mine, downs_other)
    unit_blocks = core_sum(units_mine, units_other)
    unit_blocks = unit_blocks.reshape(n, 2 * shard, unit_lanes)

    mlp_out_grad = feat_grad.astype(jnp.float32) + proj_in_grad
    mlp_out_low = mlp_out_grad.astype(low)
    down_bias_part = jnp.sum(mlp_out_low.astype(jnp.float32), axis=0)
    active_grad = product(mlp_out_low, w_down_t)
    gelu_pull = jax.vjp(gelu_tanh, hidden)[1]
    hidden_grad = gelu_pull(active_grad)[0].astype(low)
    up_bias_part = jnp.sum(hidden_grad.astype(jnp.float32), axis=0)
    mlp_back = paired(product_nt(hidden_grad, w_up))
    ln2_pull = jax.vjp(layer_norm, after_attn, ln2_gain, ln2_bias)[1]
    norm_grad, ln2_gain_part, ln2_bias_part = ln2_pull(mlp_back)
    attn_out_grad = mlp_out_grad + norm_grad
    attn_out_low = attn_out_grad.astype(low)
    o_bias_part = jnp.sum(attn_out_low.astype(jnp.float32), axis=0)
    vision_chunks = 13
    vision_width = 2 * hidden_pad + own_width
    vision_cols = -(-vision_width // (vision_chunks * 128)) * 128
    vision_left = jnp.stack([mlp_in.T, mlp_out_low.T, attn_out_low.T])
    vision_right = jnp.concatenate(
        [
            padded_columns(hidden_grad, hidden_pad),
            padded_columns(active_low, hidden_pad),
            padded_columns(attended_low, vision_chunks * vision_cols - 2 * hidden_pad),
        ],
        axis=1,
    )
    spans = (0, hidden_pad // 128, 2 * hidden_pad // 128)
    attended_grad = product(attn_out_low, w_out_t).astype(low)
    grad_one = exchanged([wide(split_heads(attended_grad, heads))], 12)[0].reshape(queries, lanes)
    vision_grad, dq, dk, dv = scattered_vision(
        vision_left,
        vision_right,
        (query_one, key_one, value_one, grad_one, query_ids, key_ids, lse_one),
        scaling,
        spans,
        vision_chunks,
        18,
    )
    dq_window = lax.dynamic_update_slice_in_dim(
        jnp.zeros((window, lanes), jnp.float32), dq, query_start, 0
    )
    dqkv = compact([dq_window, dk, dv])
    dqkv_low = dqkv.astype(low)
    head_grad = product_tn(normed_window, dqkv_low).astype(low).reshape(n, shard, -1)
    bias_row = jnp.sum(dqkv_low.astype(jnp.float32), axis=0)
    bias_rows = jnp.zeros((heads, dqkv.shape[1]), jnp.float32)
    bias_rows = lax.dynamic_update_slice_in_dim(bias_rows, bias_row[None], head, 0)
    blocks = dqkv.reshape(window // rows, rows, -1)
    other_block = jnp.where(part == 0, blocks[-1], blocks[0]).astype(low)
    across = lax.ppermute(
        other_block, "seq", [(i, (i + heads) % n) for i in range(n)]
    ).astype(jnp.float32)
    own_blocks = lax.dynamic_slice_in_dim(blocks, part, heads, 0)
    edge = jnp.where(part == 0, heads - 1, 0)
    own_blocks = own_blocks + jnp.where(
        (jnp.arange(heads) == edge)[:, None, None], across[None], 0.0
    )
    head_grads, token_grads = exchanged([head_grad, own_blocks.astype(low)], 13)
    head_grads, token_grads, unit_blocks = lax.optimization_barrier(
        (head_grads, token_grads, unit_blocks)
    )
    unit_rows = lax.all_to_all(unit_blocks, "seq", 0, 0)
    queries_grad, keys_grad, values_grad = (
        join_heads(token_grads[:, :, i * HD : (i + 1) * HD]) for i in range(3)
    )
    attn_back = paired(
        product_nt(jnp.concatenate([queries_grad, keys_grad, values_grad], axis=1), w_qkv)
    )
    ln1_pull = jax.vjp(layer_norm, input_f32, ln1_gain, ln1_bias)[1]
    in_grad, ln1_gain_part, ln1_bias_part = ln1_pull(attn_back)
    patches_grad = (attn_out_grad + in_grad).astype(low)

    smalls = (
        ln1_gain_part,
        ln1_bias_part,
        bias_rows[:, :HD].reshape(-1),
        bias_rows[:, 2 * HD : 3 * HD].reshape(-1),
        o_bias_part,
        ln2_gain_part,
        ln2_bias_part,
        up_bias_part,
        down_bias_part,
        ctx_gain_part,
    )
    pieces = [
        jnp.pad(small, (0, -small.shape[0] % 1024)) for small in smalls + (query_part.reshape(-1),)
    ]
    begins = [sum(p.shape[0] for p in pieces[:i]) for i in range(len(pieces))]
    joined_smalls = jnp.concatenate(pieces)
    length = joined_smalls.shape[0]
    per_device = -(-length // (n * 1024)) * 1024
    joined_smalls = jnp.pad(joined_smalls, (0, n * per_device - length))
    small_sum = reduced(joined_smalls.reshape(n, per_device // 128, 128), added, 15).reshape(-1)
    (
        small_sum,
        down_blocks,
        unit_rows,
        vision_grad,
        head_grads,
        pooled_late,
        self_grads,
    ) = lax.optimization_barrier(
        (small_sum, down_blocks, unit_rows, vision_grad, head_grads, pooled_low, self_grads)
    )
    down_rows = lax.all_to_all(down_blocks, "seq", 0, 0)
    vision_grad = vision_grad.transpose(1, 0, 2).reshape(shard, -1).astype(jnp.float32)
    up_weight_grad = vision_grad[:, :hidden_units]
    down_weight_grad = vision_grad[:, hidden_pad : hidden_pad + hidden_units].T
    o_weight_grad = vision_grad[:, 2 * hidden_pad : vision_width].T
    head_grads = head_grads.astype(jnp.float32)
    head_grads = head_grads[:heads] + head_grads[heads:]
    q_weight_grad, k_weight_grad, v_weight_grad = (
        join_heads(head_grads[:, :, i * HD : (i + 1) * HD]) for i in range(3)
    )
    lat_mix = product(pooled_late, ro_weight)
    ro_width = ro_weight.shape[1] // n
    ro_columns = lax.dynamic_slice_in_dim(lat_grad, me * ro_width, ro_width, 1)
    ro_weight_grad = product_tn(pooled_late, ro_columns)
    small_sums = [
        small_sum[begin : begin + small.shape[0]] for begin, small in zip(begins, smalls)
    ]
    ctx_gain_grad = small_sums[9] + swapped(small_sums[9])

    query_sum = small_sum[begins[-1] : begins[-1] + query_part.size].reshape(lat_rows, -1)
    lat_queries_grad = query_sum.astype(low)
    rq_rows = rq_weight.shape[0] // n
    rq_weight_grad = product_tn(
        lax.dynamic_slice_in_dim(lat_normed, me * rq_rows, rq_rows, 1), lat_queries_grad
    )
    lat_part = product_nt(lat_queries_grad, rq_weight) + product_nt(self_grads, w_ctx)
    down_proj_grad = down_rows.reshape(n * proj_units, -1).astype(jnp.float32)
    unit_rows = unit_rows.reshape(n, 2, shard, unit_lanes)[..., :proj_units]
    gate_proj_grad, up_proj_grad = (
        unit_rows.transpose(1, 2, 0, 3).reshape(2, shard, n * proj_units).astype(jnp.float32)
    )
    lat_back, lat_mix_sum = paired(lat_part), paired(lat_mix)
    latents_out = latents + lat_mix_sum
    lat_pull = jax.vjp(rms_norm, latents, lat_gain)[1]
    lat_in_grad, lat_gain_grad = lat_pull(lat_back)
    latents_grad = lat_grad.astype(jnp.float32) + lat_in_grad
    return (
        features,
        latents_out,
        patches_grad,
        latents_grad,
        small_sums[0],
        small_sums[1],
        q_weight_grad,
        small_sums[2],
        k_weight_grad,
        v_weight_grad,
        small_sums[3],
        o_weight_grad,
        small_sums[4],
        small_sums[5],
        small_sums[6],
        up_weight_grad,
        small_sums[7],
        down_weight_grad,
        small_sums[8],
        gate_proj_grad,
        up_proj_grad,
        down_proj_grad,
        ctx_gain_grad,
        r_grad[:, :ctx_width],
        r_grad[:, ctx_width:],
        lat_gain_grad,
        rq_weight_grad,
        ro_weight_grad,
    )


def solution(mesh):
    placed = (
        P("seq", None),
        P(),
        P(),
        P(),
        P("seq", "tp"),
        P("tp"),
        P("seq", "tp"),
        P("seq", "tp"),
        P("tp"),
        P("tp", "seq"),
        P(),
        P(),
        P(),
        P("seq", "tp"),
        P("tp"),
        P("tp", "seq"),
        P(),
        P("seq", "tp"),
        P("seq", "tp"),
        P("tp", "seq"),
        P(),
        P("seq", "tp"),
        P("seq", "tp"),
        P(),
        P(),
        P(None, "tp"),
        P("tp", None),
        P("seq", None),
        P(),
    )
    few = mesh.shape["tp"] == 2 and mesh.shape["seq"] == 16
    return jax.shard_map(
        tokens_travel if few else weights_travel,
        mesh=mesh,
        in_specs=placed,
        out_specs=(
            P("seq", None),
            P(),
            P("seq", None),
            P(),
            P(),
            P(),
            P("seq", "tp"),
            P("tp"),
            P("seq", "tp"),
            P("seq", "tp"),
            P("tp"),
            P("tp", "seq"),
            P(),
            P(),
            P(),
            P("seq", "tp"),
            P("tp"),
            P("tp", "seq"),
            P(),
            P("seq", "tp"),
            P("seq", "tp"),
            P("tp", "seq"),
            P(),
            P("seq", "tp"),
            P("seq", "tp"),
            P(),
            P("seq", "tp"),
            P("tp", "seq"),
        ),
        check_vma=False,
    )
```
